32 devices in a mesh: comp: 4 (over z), tile: 8 (over y, x, core).
Axes of the slice: x: 2, y: 2, z: 4, core: 2. Of those that a mesh axis runs over, the one named last changes fastest.
Arguments:
- atm_flux: float32 [8, 32768], P(None, ('comp', 'tile')), may hold values from -6 to 6
- intersection_weight: float32 [256, 4, 128, 128], P(('comp', 'tile')), may hold values from -0.5 to 0.5
- dest_tile: int32 [256, 4], P(('comp', 'tile')), may hold values from 0 to 7, all different within a row; in each aligned block of 8 rows (0 to 7, 8 to 15, ...) at most 4 rows name the same one
- dest_block: int32 [256, 4], P(('comp', 'tile')), may hold values from 0 to 31
- block_count: int32 [256], P(('comp', 'tile')), may hold values from 2 to 4
- sea_height: float32 [128, 1024], P('comp', 'tile'), may hold values from -6 to 6
- velocity_x: float32 [128, 1024], P('comp', 'tile'), may hold values from -3 to 3
- velocity_y: float32 [128, 1024], P('comp', 'tile'), may hold values from -3 to 3
- depth: float32 [128, 1024], P('comp', 'tile'), may hold values from 0.3 to 1
- sea_mask: int32 [128, 1024], P('comp', 'tile'), may hold values 0 or 1
Outputs:
- forcing: float32 [8, 128, 1024], P(None, 'comp', 'tile')
- height_out: float32 [128, 1024], P('comp', 'tile')
- flow_x: float32 [128, 1024], P('comp', 'tile')
- flow_y: float32 [128, 1024], P('comp', 'tile')
The draws below stay inside these ranges and needn't reach their ends.
Inputs may be any that keep to these rules, and one draw needn't show every extreme that they name: `dest_tile`: within the 8 rows of one device no tile number is named more than 4 times, and some device names some tile exactly 4 times; each row names 4 different tiles of its own section. Slots k with k < block_count carry weights; the others are padding.
All inputs are finite; a program needn't handle non-finite values. No bound on the sum of `sea_mask` on one device may be relied on, other than what follows from the above.
Results may differ from the reference program's by a relative error of at most 0.000094.
Values sent between devices are 32-bit elements; how exact they have to be, the bound alone decides.
No kernel may reach another device: no remote copies, remote signals or barrier semaphores. Data moves between devices by JAX's collectives and lax.ppermute only.
A program may use at most 64 MiB of HBM per device.

```python
import math
import jax
import jax.numpy as jnp
import numpy as np
from jax import lax

FIELDS = 8
AB = 128
OB = 128
NB = 8
K = 4
CAP = 4
OY = 32
OX = 128
NSUB = 8
OBLK = 32
NBLK = 256
ATM = 32768
NY = 128
NX = 1024
N_COMP = 4
N_TILE = 8


def set_ends(array, stream_key, low, high):
    longest = array.shape.index(max(array.shape))
    spots = []
    for shift in (0, 1):
        where = [jax.random.randint(jax.random.fold_in(stream_key, axis), (), 0, length) for axis, length in enumerate(array.shape)]
        where[longest] = (where[longest] + shift) % array.shape[longest]
        spots.append(tuple(where))
    return array.at[spots[0]].set(low).at[spots[1]].set(high)


def block_levels(rng, dims, cuts, least, high):
    def one(axis_at, parts):
        steps = jax.random.uniform(jax.random.fold_in(jax.random.fold_in(rng, 6), axis_at), (parts,), jnp.float32, least / len(cuts), high / len(cuts))
        return jnp.repeat(jnp.exp(steps), dims[axis_at] // parts).reshape((-1,) + (1,) * (len(dims) - axis_at - 1))

    gain = one(*cuts[0])
    for cut in cuts[1:]:
        gain = gain * one(*cut)
    return gain


def shared_out(key, own, number, rows, number_of, top, most, skew):
    ranking = jax.random.permutation(key, number_of)
    packed, common = portions_of(number_of, rows * top, most, skew, True), portions_of(number_of, rows * top, most, skew, False)
    places = jnp.arange(number_of)

    def named(sizes, rotation):
        used = int((sizes > 0).sum())
        fixed = max(1, used // 4)
        shifted = fixed + (places - fixed + rotation * (used - fixed)) % max(1, number_of - fixed)
        return jnp.zeros((number_of,), jnp.int32).at[ranking[jnp.where(places < fixed, places, shifted)]].set(jnp.asarray(sizes, jnp.int32))

    sizes = jnp.where(number % 4 == 0, named(packed, number // 4), named(common, number - number // 4 - 1))
    mixed = jax.random.permutation(jax.random.fold_in(own, 3), number_of)
    source_of, receiver = mixed[0:number_of // 2 * 2:2], mixed[1:number_of // 2 * 2:2]
    room = jnp.minimum(sizes[source_of] - 1, most - sizes[receiver]) // 2
    room = jnp.where((source_of == ranking[0]) | (receiver == ranking[0]) | (sizes[receiver] == 0), 0, jnp.maximum(room, 0))
    shifted = jax.random.randint(jax.random.fold_in(own, 4), (number_of // 2,), 0, 1 << 20) % (room + 1)
    sizes = sizes.at[source_of].add(-shifted).at[receiver].add(shifted)
    items = jnp.searchsorted(jnp.cumsum(sizes), jnp.arange(rows * top), side="right").astype(jnp.int32)
    table = items.reshape(top, rows).T
    table = table[jax.random.permutation(jax.random.fold_in(own, 1), rows)]
    rotation = jax.random.randint(jax.random.fold_in(own, 2), (rows, 1), 0, top)
    return jnp.take_along_axis(table, (jnp.arange(top)[None, :] + rotation) % top, axis=1)


def portions_of(number_of, total, reach, lean, full):
    portions = [(1 << 20) // math.isqrt(grade ** lean) + 1 for grade in range(1, number_of + 1)]
    largest = reach if full else min(reach, max(-(-total // number_of), total * portions[0] // sum(portions)))
    least = 1 if total - largest >= number_of - 1 else 0
    holding, rest = [largest] + [least] * (number_of - 1), total - largest - least * (number_of - 1)
    while rest > 0:
        movable = [i for i in range(1, number_of) if holding[i] < largest] or [i for i in range(1, number_of) if holding[i] < reach]
        mass, left = sum([portions[i] for i in movable]), rest
        for i in movable:
            extra = min(reach - holding[i], max(1, left * portions[i] // mass), rest)
            holding[i] = holding[i] + extra
            rest = rest - extra
    return np.array(holding)


def gaussian(key, dims, deviation, reach, split=(), kind=jnp.bfloat16):
    entries = deviation * jax.random.normal(key, dims, jnp.float32)
    if split:
        entries = entries * block_levels(key, dims, split, -0.22, 0.18)
    return jnp.clip(entries, -reach, reach).astype(kind)


def setup_inputs(seed: int = 0) -> dict:
    arg_keys = jax.random.split(jax.random.key(seed), 11)
    atm_flux = gaussian(arg_keys[0], (FIELDS, ATM), 1.0, 6.0, ((1, 32),), jnp.float32)
    intersection_weight = gaussian(arg_keys[1], (NBLK, K, AB, OB), AB ** -0.5, 0.5, ((0, 32),), jnp.float32)
    dest_tile_keys = jax.random.split(jax.random.fold_in(arg_keys[2], 1), NBLK // NB)
    dest_tile_turns = jax.random.permutation(jax.random.fold_in(arg_keys[2], 3), NBLK // NB)
    dest_tile = jax.vmap(lambda own, number: shared_out(jax.random.fold_in(arg_keys[2], 2), own, number, NB, N_TILE, K, CAP, 2))(dest_tile_keys, dest_tile_turns).reshape((NBLK, K))
    dest_block = set_ends(jax.random.randint(arg_keys[3], (NBLK, K), 0, OBLK), jax.random.fold_in(arg_keys[3], 1), 0, OBLK - 1).astype(jnp.int32)
    block_count = set_ends(jax.random.randint(arg_keys[4], (NBLK,), K // 2, K + 1), jax.random.fold_in(arg_keys[4], 1), K // 2, K).astype(jnp.int32)
    sea_height = gaussian(arg_keys[5], (NY, NX), 1.0, 6.0, ((0, 4), (1, 8)), jnp.float32)
    velocity_x = gaussian(arg_keys[6], (NY, NX), 0.5, 3.0, ((0, 4), (1, 8)), jnp.float32)
    velocity_y = gaussian(arg_keys[7], (NY, NX), 0.5, 3.0, ((0, 4), (1, 8)), jnp.float32)
    depth = jnp.clip(jnp.exp(math.log(1.0) - 1.2039728 * jax.random.uniform(arg_keys[8], (NY, NX), jnp.float32) ** block_levels(arg_keys[8], (NY, NX), ((0, 4), (1, 8)), -0.2, 0.2)), 0.3, 1.0)
    sea_mask = set_ends((jax.random.randint(arg_keys[9], (NY, NX), 0, 10) < 9).astype(jnp.int32), jax.random.fold_in(arg_keys[9], 1), 0, 1)
    return {"atm_flux": atm_flux, "intersection_weight": intersection_weight, "dest_tile": dest_tile, "dest_block": dest_block, "block_count": block_count, "sea_height": sea_height, "velocity_x": velocity_x, "velocity_y": velocity_y, "depth": depth, "sea_mask": sea_mask}


def diff_cols(field):
    padded = jnp.pad(field, ((0, 0), (1, 1)))
    return 0.5 * (padded[:, 2:] - padded[:, :-2])


def diff_rows(field):
    padded = jnp.pad(field, ((1, 1), (0, 0)))
    return 0.5 * (padded[2:, :] - padded[:-2, :])


def reference(atm_flux, intersection_weight, dest_tile, dest_block, block_count, sea_height, velocity_x, velocity_y, depth, sea_mask):
    nblk = dest_tile.shape[0]
    pieces = atm_flux.reshape(FIELDS, nblk, AB).transpose(1, 0, 2)
    slot_part = jnp.einsum("bfa,bkao->bkfo", pieces, intersection_weight, precision=lax.Precision.HIGHEST)
    slot_live = (jnp.arange(K, dtype=jnp.int32)[None, :] < block_count[:, None]).astype(jnp.float32)
    slot_part = slot_part * slot_live[:, :, None, None]
    section = (jnp.arange(nblk, dtype=jnp.int32) // (NB * N_TILE)).astype(jnp.int32)
    target = ((section[:, None] * N_TILE + dest_tile) * OBLK + dest_block).astype(jnp.int32)
    summed = jax.ops.segment_sum(slot_part.reshape(nblk * K, FIELDS, OB), target.reshape(-1), num_segments=N_COMP * N_TILE * OBLK)
    grid = summed.reshape(N_COMP, N_TILE, OBLK, FIELDS, OB).transpose(3, 0, 1, 2, 4)
    grid = grid.reshape(FIELDS, N_COMP, N_TILE, OY, OX).transpose(0, 1, 3, 2, 4).reshape(FIELDS, NY, NX)
    sea_float = sea_mask.astype(jnp.float32)
    forcing = grid * sea_float
    row_frac = jnp.arange(NY, dtype=jnp.int32).astype(jnp.float32) / NY
    coriolis = (0.02 + 0.06 * row_frac)[:, None] * jnp.ones((NY, NX), jnp.float32)
    wind_x = 0.05 * forcing[0] * (1.0 / depth)
    wind_y = 0.05 * forcing[1] * (1.0 / depth)
    fresh = 0.1 * forcing[2]
    height, flow_u, flow_v = sea_height, velocity_x, velocity_y
    for cycle in range(NSUB):
        spread = diff_cols(depth * flow_u) + diff_rows(depth * flow_v)
        height = sea_float * (height - 0.4 * spread + fresh)
        next_u = sea_float * (0.98 * flow_u - 0.4 * diff_cols(height) + coriolis * flow_v + wind_x)
        next_v = sea_float * (0.98 * flow_v - 0.4 * diff_rows(height) - coriolis * flow_u + wind_y)
        flow_u, flow_v = next_u, next_v
    return (forcing, height, flow_u, flow_v)
```

```python
import functools

import jax
import jax.numpy as jnp
from jax import lax
from jax.experimental import pallas as pl
from jax.experimental.pallas import tpu as pltpu
from jax.sharding import PartitionSpec as P

NSUB = 8
HALO = 2 * NSUB
CAP = 4
LANES = 128
WET = 3
F32 = jnp.float32
BF16 = jnp.bfloat16
VMEM = pl.BlockSpec(memory_space=pltpu.VMEM)
SMEM = pl.BlockSpec(memory_space=pltpu.SMEM)
HBM = pl.BlockSpec(memory_space=pltpu.HBM)


def halves(x):
    high = x.astype(BF16)
    return high, (x - high.astype(F32)).astype(BF16)


def lanes_of(rows):
    return lax.broadcasted_iota(jnp.int32, (rows, LANES), 1)


def remap_kernel(
    flux_far, weight, tile_far, block_far, count_far, height, vel_x, vel_y, depth, mask,
    send, own, flux, stage, dest_tile, dest_block, count, sea_int, table, seen, sems,
):
    slots, blocks = dest_tile.shape
    fields, rows = flux.shape[0], height.shape[0]
    tiles = send.shape[0]
    base = CAP * fields
    moves = [(tile_far, dest_tile), (block_far, dest_block), (count_far, count)]
    moves += [(flux_far, flux), (mask, sea_int)]
    moves += [(x, own.at[q * rows : (q + 1) * rows]) for q, x in enumerate((height, vel_x, vel_y, depth))]
    moves += [(weight.at[b], stage.at[b]) for b in range(blocks)]
    copies = [pltpu.make_async_copy(x, y, sems.at[i]) for i, (x, y) in enumerate(moves)]
    for copy in copies:
        copy.start()
    for t in range(tiles):
        seen[t] = 0
        for r in range(CAP):
            table[t * CAP + r] = -1
        send[t, 0:base, :] = jnp.zeros((base, LANES), F32)
    for copy in copies[:3]:
        copy.wait()
    places = []
    for b in range(blocks):
        live = count[b]
        for k in range(slots):
            t = dest_tile[k, b]
            r = jnp.minimum(seen[t], CAP - 1)
            seen[t] = r + 1
            table[t * CAP + r] = jnp.where(k < live, dest_block[k, b], -1)
            places.append((t, r))
    for copy in copies[3:9]:
        copy.wait()
    state = [own[q * rows : (q + 1) * rows] for q in range(4)]
    sea = sea_int[...].astype(F32)
    own[4 * rows : 5 * rows] = sea
    lane16 = lanes_of(16)
    lane8 = lanes_of(8)
    row8 = lax.broadcasted_iota(jnp.int32, (8, LANES), 0)

    def edges(first):
        packed = jnp.zeros((16, LANES), F32)
        for half in range(2):
            for q in range(4):
                to = 64 * half + 16 * q
                moved = pltpu.roll(state[q][16 * half : 16 * half + 16], (to - first) % LANES, 1)
                packed = jnp.where((lane16 >= to) & (lane16 < to + 16), moved, packed)
        small = jnp.zeros((8, LANES), F32)
        for g in range(4):
            moved = pltpu.roll(sea[8 * g : 8 * g + 8], (16 * g - first) % LANES, 1)
            small = jnp.where((lane8 >= 16 * g) & (lane8 < 16 * g + 16), moved, small)
        return packed, small

    to_right = edges(LANES - HALO)
    to_left = edges(0)
    me = lax.axis_index("tile")

    for b in range(blocks):
        copies[9 + b].wait()
        high, low = halves(flux[:, b * LANES : (b + 1) * LANES])
        left = jnp.concatenate(
            [
                jnp.concatenate([high, low], axis=0),
                jnp.concatenate([high, jnp.zeros_like(low)], axis=0),
            ],
            axis=1,
        )
        for k in range(slots):
            w_high, w_low = halves(stage[b, k])
            both = jnp.dot(
                left, jnp.concatenate([w_high, w_low], axis=0), preferred_element_type=F32
            )
            t, r = places[b * slots + k]
            send[t, pl.ds(pl.multiple_of(r * fields, fields), fields), :] = both[:fields] + both[fields:]

    for t in range(tiles):
        toward_right = me < t
        packed = jnp.where(toward_right, to_right[0], to_left[0])
        small = jnp.where(toward_right, to_right[1], to_left[1])
        send[t, base : base + 16, :] = packed
        lefts, rights = max(t - 1, 0), min(t + 1, tiles - 1)
        out = small
        for f in range(WET):
            to = 64 + 16 * f
            part_l = send[lefts, pl.ds(f, CAP, stride=fields), :]
            part_r = send[rights, pl.ds(f, CAP, stride=fields), :]
            part_l = pltpu.roll(part_l, (to - (LANES - HALO)) % LANES, 1)
            part_r = pltpu.roll(part_r, to, 1)
            part = jnp.concatenate([part_l, part_r], axis=0)
            out = jnp.where((lane8 >= to) & (lane8 < to + 16), part, out)
        side = jnp.full((8, LANES), -1, jnp.int32)
        main = jnp.full((8, LANES), -1, jnp.int32)
        for r in range(CAP):
            if t > 0:
                side = jnp.where(row8 == r, table[lefts * CAP + r], side)
            if t < tiles - 1:
                named = table[rights * CAP + r]
                side = jnp.where(row8 == CAP + r, jnp.where(named < 0, -1, named + 32), side)
            main = jnp.where(row8 == r, table[t * CAP + r], main)
        out = jnp.where(lane8 == 112, side.astype(F32), out)
        out = jnp.where(lane8 == 113, main.astype(F32), out)
        send[t, base + 16 : base + 24, :] = out


def place_kernel(recv, state, forcing, wet_out, up, down, left, right, *, tiles):
    fields, rows = forcing.shape[:2]
    chunk = recv.shape[0] // tiles
    base = CAP * fields
    tail = base + 16
    names = jnp.concatenate([recv[pl.ds(tail + j, tiles, stride=chunk), :] for j in range(8)], axis=0)

    def one_hot(ids):
        lane = lanes_of(ids.shape[0]).astype(F32)
        return jnp.where(lane == ids, 1.0, 0.0).T

    hot_side = one_hot(names[:, 112:113])[: 2 * rows].astype(BF16)
    hot_main = one_hot(names[: CAP * tiles, 113:114])[:rows].astype(BF16)

    def spread(hot, values):
        high, low = halves(values)
        return jnp.dot(hot, high, preferred_element_type=F32) + jnp.dot(
            hot, low, preferred_element_type=F32
        )

    own = [state[q * rows : (q + 1) * rows] for q in range(5)]
    sea = own[4]
    for f in range(fields):
        values = jnp.concatenate(
            [recv[pl.ds(r * fields + f, tiles, stride=chunk), :] for r in range(CAP)], axis=0
        )
        grid = spread(hot_main, values) * sea
        forcing[f] = grid
        if f < WET:
            wet_out[f * rows : (f + 1) * rows] = grid
            own.append(grid)
    sides = spread(hot_side, names)
    lane = lanes_of(rows)
    me = lax.axis_index("tile")
    for which, out in ((0, left), (1, right)):
        source = jnp.maximum(me - 1, 0) if which == 0 else jnp.minimum(me + 1, tiles - 1)
        exists = (me > 0) if which == 0 else (me < tiles - 1)
        start = pl.multiple_of(source * chunk + base, 8)
        packed = recv[pl.ds(start, 16), :]
        small = recv[pl.ds(start + 16, 8), :]
        whole = jnp.concatenate([packed, pltpu.roll(packed, 64, 1)], axis=0)
        sea_part = jnp.concatenate(
            [pltpu.roll(small, (64 - 16 * g) % LANES, 1) for g in range(4)], axis=0
        )
        driven = pltpu.roll(sides[which * rows : (which + 1) * rows], 16, 1)
        full = jnp.where(lane < 64, whole, jnp.where(lane < 80, sea_part, driven))
        full = jnp.where(exists, full, 0.0)
        out[...] = full
        at = (5 + WET) * 16 + which * 16
        up[at : at + 16, :] = full[:16]
        down[at : at + 16, :] = full[rows - 16 :]
    for q, field in enumerate(own):
        up[16 * q : 16 * q + 16, :] = field[:16]
        down[16 * q : 16 * q + 16, :] = field[rows - 16 :]


def cycle_kernel(
    state, wet, left, right, above, below, height_out, flow_x, flow_y, *, comps
):
    rows = height_out.shape[0]
    total = rows + 2 * HALO
    count = 5 + WET
    own = [state[q * rows : (q + 1) * rows] for q in range(5)]
    own += [wet[f * rows : (f + 1) * rows] for f in range(WET)]
    at = count * 16
    side_l = jnp.concatenate([above[at : at + 16], left[...], below[at : at + 16]], axis=0)
    side_r = jnp.concatenate([above[at + 16 : at + 32], right[...], below[at + 16 : at + 32]], axis=0)
    lane = lanes_of(total)
    wide = []
    for q in range(count):
        center = jnp.concatenate(
            [above[16 * q : 16 * q + 16], own[q], below[16 * q : 16 * q + 16]], axis=0
        )
        from_l = pltpu.roll(side_l, (LANES - HALO - 16 * q) % LANES, 1)
        from_r = pltpu.roll(side_r, (LANES - 16 * q) % LANES, 1)
        side = jnp.where(lane < HALO, from_r, jnp.where(lane >= LANES - HALO, from_l, 0.0))
        wide.append(jnp.concatenate([center, side], axis=1))
    eta, u, v, deep, sea, push_x, push_y, rain = wide
    shape = (total, 2 * LANES)
    row = lax.axis_index("comp") * rows - HALO + lax.broadcasted_iota(jnp.int32, shape, 0)
    frac = row.astype(F32) / float(rows * comps)
    turn = (0.02 + 0.06 * frac) * sea
    inverse = jnp.where(deep > 0.0, 1.0 / jnp.where(deep > 0.0, deep, 1.0), 0.0)
    wind_x = sea * (0.05 * push_x * inverse)
    wind_y = sea * (0.05 * push_y * inverse)
    fresh = sea * (0.1 * rain)
    slope = 0.2 * sea
    deep = 0.2 * deep

    def cols(x):
        return pltpu.roll(x, 2 * LANES - 1, 1) - pltpu.roll(x, 1, 1)

    def lines(x):
        return pltpu.roll(x, total - 1, 0) - pltpu.roll(x, 1, 0)

    through_x, through_y = deep * u, deep * v
    eta, u, v = sea * eta, sea * u, sea * v
    for _ in range(NSUB):
        eta = eta + fresh - sea * (cols(through_x) + lines(through_y))
        next_u = 0.98 * u - slope * cols(eta) + turn * v + wind_x
        next_v = 0.98 * v - slope * lines(eta) - turn * u + wind_y
        u, v = next_u, next_v
        through_x, through_y = deep * u, deep * v
    height_out[...] = eta[HALO : HALO + rows, :LANES]
    flow_x[...] = u[HALO : HALO + rows, :LANES]
    flow_y[...] = v[HALO : HALO + rows, :LANES]


def local(tiles, comps, flux, weight, dest_tile, dest_block, count, height, vel_x, vel_y, depth, mask):
    fields = flux.shape[0]
    blocks, slots = dest_tile.shape
    rows, cols = height.shape
    chunk = CAP * fields + 24
    state = (height, vel_x, vel_y, depth, mask)
    plane = jax.ShapeDtypeStruct((rows, cols), F32)
    params = pltpu.CompilerParams(vmem_limit_bytes=16 * 1024 * 1024)

    def near(*shape):
        return pltpu.VMEM(shape, F32)

    def far(x):
        return pltpu.with_memory_space_constraint(x, pltpu.HBM)

    send, own = pl.pallas_call(
        remap_kernel,
        out_shape=[near(tiles, chunk, LANES), near(5 * rows, cols)],
        in_specs=[HBM] * 10,
        out_specs=[VMEM] * 2,
        scratch_shapes=[
            pltpu.VMEM(flux.shape, F32),
            pltpu.VMEM(weight.shape, F32),
            pltpu.SMEM((slots, blocks), jnp.int32),
            pltpu.SMEM((slots, blocks), jnp.int32),
            pltpu.SMEM((blocks,), jnp.int32),
            pltpu.VMEM((rows, cols), jnp.int32),
            pltpu.SMEM((tiles * CAP,), jnp.int32),
            pltpu.SMEM((tiles,), jnp.int32),
            pltpu.SemaphoreType.DMA((9 + blocks,)),
        ],
        compiler_params=params,
        name="remap",
    )(*map(far, (flux, weight, dest_tile.T, dest_block.T, count, *state)))
    recv = lax.all_to_all(send, "tile", 0, 0, tiled=True).reshape(tiles * chunk, LANES)
    message = near((5 + WET + 2) * 16, LANES)
    forcing, wet, up, down, left, right = pl.pallas_call(
        functools.partial(place_kernel, tiles=tiles),
        out_shape=[
            jax.ShapeDtypeStruct((fields, rows, cols), F32), near(WET * rows, cols),
            message, message, near(rows, cols), near(rows, cols),
        ],
        in_specs=[VMEM] * 2,
        out_specs=[VMEM] * 6,
        compiler_params=params,
        name="place",
    )(recv, own)
    above = lax.ppermute(down, "comp", [(i, i + 1) for i in range(comps - 1)])
    below = lax.ppermute(up, "comp", [(i + 1, i) for i in range(comps - 1)])
    outs = pl.pallas_call(
        functools.partial(cycle_kernel, comps=comps),
        out_shape=[plane] * 3,
        in_specs=[VMEM] * 6,
        out_specs=[VMEM] * 3,
        compiler_params=params,
        name="cycles",
    )(own, wet, left, right, above, below)
    return (forcing, *outs)


def solution(mesh):
    both = ("comp", "tile")
    grid = P("comp", "tile")
    in_specs = (P(None, both), P(both, None, None, None), P(both, None), P(both, None), P(both)) + (grid,) * 5
    out_specs = (P(None, "comp", "tile"), grid, grid, grid)
    body = functools.partial(local, mesh.shape["tile"], mesh.shape["comp"])
    return jax.shard_map(body, mesh=mesh, in_specs=in_specs, out_specs=out_specs, check_vma=False)
```

```python
import functools

import jax
import jax.numpy as jnp
from jax import lax
from jax.experimental import pallas as pl
from jax.experimental.pallas import tpu as pltpu
from jax.sharding import PartitionSpec as P

NSUB = 8
HALO = 2 * NSUB
CAP = 4
LANES = 128
WET = 3
F32 = jnp.float32
BF16 = jnp.bfloat16
VMEM = pl.BlockSpec(memory_space=pltpu.VMEM)
SMEM = pl.BlockSpec(memory_space=pltpu.SMEM)
HBM = pl.BlockSpec(memory_space=pltpu.HBM)


def halves(x):
    high = x.astype(BF16)
    return high, (x - high.astype(F32)).astype(BF16)


def lanes_of(rows):
    return lax.broadcasted_iota(jnp.int32, (rows, LANES), 1)


def remap_kernel(
    flux_far, weight, tile_far, block_far, count_far, height, vel_x, vel_y, depth, mask,
    send, own, flux, stage, dest_tile, dest_block, count, sea_int, table, seen, sems,
):
    slots, blocks = dest_tile.shape
    fields, rows = flux.shape[0], height.shape[0]
    tiles = send.shape[0]
    base = CAP * fields
    moves = [(tile_far, dest_tile), (block_far, dest_block), (count_far, count)]
    moves += [(flux_far, flux), (mask, sea_int)]
    moves += [(x, own.at[q * rows : (q + 1) * rows]) for q, x in enumerate((height, vel_x, vel_y, depth))]
    moves += [(weight.at[b], stage.at[b]) for b in range(blocks)]
    copies = [pltpu.make_async_copy(x, y, sems.at[i]) for i, (x, y) in enumerate(moves)]
    for copy in copies:
        copy.start()
    for t in range(tiles):
        seen[t] = 0
        for r in range(CAP):
            table[t * CAP + r] = -1
        send[t, 0:base, :] = jnp.zeros((base, LANES), F32)
    for copy in copies[:3]:
        copy.wait()
    places = []
    for b in range(blocks):
        live = count[b]
        for k in range(slots):
            t = dest_tile[k, b]
            r = jnp.minimum(seen[t], CAP - 1)
            seen[t] = r + 1
            table[t * CAP + r] = jnp.where(k < live, dest_block[k, b], -1)
            places.append((t, r))
    for copy in copies[3:9]:
        copy.wait()
    state = [own[q * rows : (q + 1) * rows] for q in range(4)]
    sea = sea_int[...].astype(F32)
    own[4 * rows : 5 * rows] = sea
    lane16 = lanes_of(16)
    lane8 = lanes_of(8)
    row8 = lax.broadcasted_iota(jnp.int32, (8, LANES), 0)

    def edges(first):
        packed = jnp.zeros((16, LANES), F32)
        for half in range(2):
            for q in range(4):
                to = 64 * half + 16 * q
                moved = pltpu.roll(state[q][16 * half : 16 * half + 16], (to - first) % LANES, 1)
                packed = jnp.where((lane16 >= to) & (lane16 < to + 16), moved, packed)
        small = jnp.zeros((8, LANES), F32)
        for g in range(4):
            moved = pltpu.roll(sea[8 * g : 8 * g + 8], (16 * g - first) % LANES, 1)
            small = jnp.where((lane8 >= 16 * g) & (lane8 < 16 * g + 16), moved, small)
        return packed, small

    to_right = edges(LANES - HALO)
    to_left = edges(0)
    me = lax.axis_index("tile")

    for b in range(blocks):
        copies[9 + b].wait()
        high, low = halves(flux[:, b * LANES : (b + 1) * LANES])
        left = jnp.concatenate(
            [
                jnp.concatenate([high, low], axis=0),
                jnp.concatenate([high, jnp.zeros_like(low)], axis=0),
            ],
            axis=1,
        )
        for k in range(slots):
            w_high, w_low = halves(stage[b, k])
            both = jnp.dot(
                left, jnp.concatenate([w_high, w_low], axis=0), preferred_element_type=F32
            )
            t, r = places[b * slots + k]
            send[t, pl.ds(pl.multiple_of(r * fields, fields), fields), :] = both[:fields] + both[fields:]

    for t in range(tiles):
        toward_right = me < t
        packed = jnp.where(toward_right, to_right[0], to_left[0])
        small = jnp.where(toward_right, to_right[1], to_left[1])
        send[t, base : base + 16, :] = packed
        lefts, rights = max(t - 1, 0), min(t + 1, tiles - 1)
        out = small
        for f in range(WET):
            to = 64 + 16 * f
            part_l = send[lefts, pl.ds(f, CAP, stride=fields), :]
            part_r = send[rights, pl.ds(f, CAP, stride=fields), :]
            part_l = pltpu.roll(part_l, (to - (LANES - HALO)) % LANES, 1)
            part_r = pltpu.roll(part_r, to, 1)
            part = jnp.concatenate([part_l, part_r], axis=0)
            out = jnp.where((lane8 >= to) & (lane8 < to + 16), part, out)
        side = jnp.full((8, LANES), -1, jnp.int32)
        main = jnp.full((8, LANES), -1, jnp.int32)
        for r in range(CAP):
            if t > 0:
                side = jnp.where(row8 == r, table[lefts * CAP + r], side)
            if t < tiles - 1:
                named = table[rights * CAP + r]
                side = jnp.where(row8 == CAP + r, jnp.where(named < 0, -1, named + 32), side)
            main = jnp.where(row8 == r, table[t * CAP + r], main)
        out = jnp.where(lane8 == 112, side.astype(F32), out)
        out = jnp.where(lane8 == 113, main.astype(F32), out)
        send[t, base + 16 : base + 24, :] = out


def place_kernel(recv, state, forcing, wet, first, second, left, right, *, tiles):
    fields, rows = forcing.shape[:2]
    chunk = recv.shape[0] // tiles
    base = CAP * fields
    tail = base + 16
    names = jnp.concatenate([recv[pl.ds(tail + j, tiles, stride=chunk), :] for j in range(8)], axis=0)

    def one_hot(ids):
        lane = lanes_of(ids.shape[0]).astype(F32)
        return jnp.where(lane == ids, 1.0, 0.0).T

    hot_side = one_hot(names[:, 112:113])[: 2 * rows].astype(BF16)
    hot_main = one_hot(names[: CAP * tiles, 113:114])[:rows].astype(BF16)

    def spread(hot, values):
        high, low = halves(values)
        return jnp.dot(hot, high, preferred_element_type=F32) + jnp.dot(
            hot, low, preferred_element_type=F32
        )

    sea = state[4 * rows : 5 * rows]
    for f in range(fields):
        values = jnp.concatenate(
            [recv[pl.ds(r * fields + f, tiles, stride=chunk), :] for r in range(CAP)], axis=0
        )
        grid = spread(hot_main, values) * sea
        forcing[f] = grid
        if f < WET:
            wet[f * rows : (f + 1) * rows] = grid
    sides = spread(hot_side, names)
    lane = lanes_of(rows)
    me = lax.axis_index("tile")
    for which, out in ((0, left), (1, right)):
        source = jnp.maximum(me - 1, 0) if which == 0 else jnp.minimum(me + 1, tiles - 1)
        exists = (me > 0) if which == 0 else (me < tiles - 1)
        start = pl.multiple_of(source * chunk + base, 8)
        packed = recv[pl.ds(start, 16), :]
        small = recv[pl.ds(start + 16, 8), :]
        whole = jnp.concatenate([packed, pltpu.roll(packed, 64, 1)], axis=0)
        sea_part = jnp.concatenate(
            [pltpu.roll(small, (64 - 16 * g) % LANES, 1) for g in range(4)], axis=0
        )
        driven = pltpu.roll(sides[which * rows : (which + 1) * rows], 16, 1)
        full = jnp.where(lane < 64, whole, jnp.where(lane < 80, sea_part, driven))
        full = jnp.where(exists, full, 0.0)
        out[...] = full
    even = lax.axis_index("comp") % 2 == 0
    for message, low in ((first, even), (second, jnp.logical_not(even))):
        start = pl.multiple_of(jnp.where(low, rows - HALO, 0), 8)
        parts = [(state, q) for q in range(5)] + [(wet, f) for f in range(WET)] + [(left, 0), (right, 0)]
        for i, (ref, q) in enumerate(parts):
            message[i * HALO : (i + 1) * HALO, :] = ref[pl.ds(q * rows + start, HALO), :]


def cycle_kernel(
    state, wet, left, right, first, second, height_out, flow_x, flow_y, *, comps
):
    rows = height_out.shape[0]
    even = lax.axis_index("comp") % 2 == 0
    first, second = first[...], second[...]
    above, below = jnp.where(even, second, first), jnp.where(even, first, second)
    total = rows + 2 * HALO
    count = 5 + WET
    own = [state[q * rows : (q + 1) * rows] for q in range(5)]
    own += [wet[f * rows : (f + 1) * rows] for f in range(WET)]
    at = count * 16
    side_l = jnp.concatenate([above[at : at + 16], left[...], below[at : at + 16]], axis=0)
    side_r = jnp.concatenate([above[at + 16 : at + 32], right[...], below[at + 16 : at + 32]], axis=0)
    lane = lanes_of(total)
    wide = []
    for q in range(count):
        center = jnp.concatenate(
            [above[16 * q : 16 * q + 16], own[q], below[16 * q : 16 * q + 16]], axis=0
        )
        from_l = pltpu.roll(side_l, (LANES - HALO - 16 * q) % LANES, 1)
        from_r = pltpu.roll(side_r, (LANES - 16 * q) % LANES, 1)
        side = jnp.where(lane < HALO, from_r, jnp.where(lane >= LANES - HALO, from_l, 0.0))
        wide.append(jnp.concatenate([center, side], axis=1))
    eta, u, v, deep, sea, push_x, push_y, rain = wide
    shape = (total, 2 * LANES)
    row = lax.axis_index("comp") * rows - HALO + lax.broadcasted_iota(jnp.int32, shape, 0)
    inside = (row >= 0) & (row < rows * comps)
    deep, sea = jnp.where(inside, deep, 0.0), jnp.where(inside, sea, 0.0)
    frac = row.astype(F32) / float(rows * comps)
    turn = (0.02 + 0.06 * frac) * sea
    inverse = jnp.where(deep > 0.0, 1.0 / jnp.where(deep > 0.0, deep, 1.0), 0.0)
    wind_x = sea * (0.05 * push_x * inverse)
    wind_y = sea * (0.05 * push_y * inverse)
    fresh = sea * (0.1 * rain)
    slope = 0.2 * sea
    deep = 0.2 * deep

    def cols(x):
        return pltpu.roll(x, 2 * LANES - 1, 1) - pltpu.roll(x, 1, 1)

    def lines(x):
        return pltpu.roll(x, total - 1, 0) - pltpu.roll(x, 1, 0)

    through_x, through_y = deep * u, deep * v
    eta, u, v = sea * eta, sea * u, sea * v
    for _ in range(NSUB):
        eta = eta + fresh - sea * (cols(through_x) + lines(through_y))
        next_u = 0.98 * u - slope * cols(eta) + turn * v + wind_x
        next_v = 0.98 * v - slope * lines(eta) - turn * u + wind_y
        u, v = next_u, next_v
        through_x, through_y = deep * u, deep * v
    height_out[...] = eta[HALO : HALO + rows, :LANES]
    flow_x[...] = u[HALO : HALO + rows, :LANES]
    flow_y[...] = v[HALO : HALO + rows, :LANES]


def swaps(parity, comps, tiles):
    pairs = []
    for s in range(comps):
        other = s + 1 if s % 2 == parity else s - 1
        for t in range(tiles):
            there = other * tiles + t if 0 <= other < comps else s * tiles + (t ^ 1)
            pairs.append((s * tiles + t, there))
    return pairs


def local(tiles, comps, flux, weight, dest_tile, dest_block, count, height, vel_x, vel_y, depth, mask):
    fields = flux.shape[0]
    blocks, slots = dest_tile.shape
    rows, cols = height.shape
    chunk = CAP * fields + 24
    state = (height, vel_x, vel_y, depth, mask)
    plane = jax.ShapeDtypeStruct((rows, cols), F32)
    params = pltpu.CompilerParams(vmem_limit_bytes=16 * 1024 * 1024)

    def near(*shape):
        return pltpu.VMEM(shape, F32)

    def far(x):
        return pltpu.with_memory_space_constraint(x, pltpu.HBM)

    send, own = pl.pallas_call(
        remap_kernel,
        out_shape=[near(tiles, chunk, LANES), near(5 * rows, cols)],
        in_specs=[HBM] * 10,
        out_specs=[VMEM] * 2,
        scratch_shapes=[
            pltpu.VMEM(flux.shape, F32),
            pltpu.VMEM(weight.shape, F32),
            pltpu.SMEM((slots, blocks), jnp.int32),
            pltpu.SMEM((slots, blocks), jnp.int32),
            pltpu.SMEM((blocks,), jnp.int32),
            pltpu.VMEM((rows, cols), jnp.int32),
            pltpu.SMEM((tiles * CAP,), jnp.int32),
            pltpu.SMEM((tiles,), jnp.int32),
            pltpu.SemaphoreType.DMA((9 + blocks,)),
        ],
        compiler_params=params,
        name="remap",
    )(*map(far, (flux, weight, dest_tile.T, dest_block.T, count, *state)))
    recv = lax.all_to_all(send, "tile", 0, 0, tiled=True).reshape(tiles * chunk, LANES)
    message = near((5 + WET + 2) * 16, LANES)
    forcing, wet, first, second, left, right = pl.pallas_call(
        functools.partial(place_kernel, tiles=tiles),
        out_shape=[
            jax.ShapeDtypeStruct((fields, rows, cols), F32), near(WET * rows, cols),
            message, message, near(rows, cols), near(rows, cols),
        ],
        in_specs=[VMEM] * 2,
        out_specs=[VMEM] * 6,
        compiler_params=params,
        name="place",
    )(recv, own)
    received = [
        lax.ppermute(x, ("comp", "tile"), swaps(parity, comps, tiles))
        for parity, x in enumerate((first, second))
    ]
    outs = pl.pallas_call(
        functools.partial(cycle_kernel, comps=comps),
        out_shape=[plane] * 3,
        in_specs=[VMEM] * 6,
        out_specs=[VMEM] * 3,
        compiler_params=params,
        name="cycles",
    )(own, wet, left, right, *received)
    return (forcing, *outs)


def solution(mesh):
    both = ("comp", "tile")
    grid = P("comp", "tile")
    in_specs = (P(None, both), P(both, None, None, None), P(both, None), P(both, None), P(both)) + (grid,) * 5
    out_specs = (P(None, "comp", "tile"), grid, grid, grid)
    body = functools.partial(local, mesh.shape["tile"], mesh.shape["comp"])
    return jax.shard_map(body, mesh=mesh, in_specs=in_specs, out_specs=out_specs, check_vma=False)
```

```python
import functools

import jax
import jax.numpy as jnp
from jax import lax
from jax.experimental import pallas as pl
from jax.experimental.pallas import tpu as pltpu
from jax.sharding import PartitionSpec as P

NSUB = 8
HALO = 2 * NSUB
CAP = 4
LANES = 128
WET = 3
F32 = jnp.float32
BF16 = jnp.bfloat16
VMEM = pl.BlockSpec(memory_space=pltpu.VMEM)
SMEM = pl.BlockSpec(memory_space=pltpu.SMEM)
HBM = pl.BlockSpec(memory_space=pltpu.HBM)


def halves(x):
    high = x.astype(BF16)
    return high, (x - high.astype(F32)).astype(BF16)


def lanes_of(rows):
    return lax.broadcasted_iota(jnp.int32, (rows, LANES), 1)


def remap_kernel(
    flux_far, weight, tile_far, block_far, count_far, height, vel_x, vel_y, depth, mask,
    send, own, flux, stage, dest_tile, dest_block, count, sea_int, table, seen, sems,
):
    slots, blocks = dest_tile.shape
    fields, rows = flux.shape[0], height.shape[0]
    tiles = send.shape[0]
    base = CAP * fields
    moves = [(tile_far, dest_tile), (block_far, dest_block), (count_far, count)]
    moves += [(flux_far, flux), (mask, sea_int)]
    moves += [(x, own.at[q * rows : (q + 1) * rows]) for q, x in enumerate((height, vel_x, vel_y, depth))]
    moves += [(weight.at[b], stage.at[b]) for b in range(blocks)]
    copies = [pltpu.make_async_copy(x, y, sems.at[i]) for i, (x, y) in enumerate(moves)]
    for copy in copies:
        copy.start()
    for t in range(tiles):
        seen[t] = 0
        for r in range(CAP):
            table[t * CAP + r] = -1
        send[t, 0:base, :] = jnp.zeros((base, LANES), F32)
    for copy in copies[:3]:
        copy.wait()
    places = []
    for b in range(blocks):
        live = count[b]
        for k in range(slots):
            t = dest_tile[k, b]
            r = jnp.minimum(seen[t], CAP - 1)
            seen[t] = r + 1
            table[t * CAP + r] = jnp.where(k < live, dest_block[k, b], -1)
            places.append((t, r))
    for copy in copies[3:9]:
        copy.wait()
    state = [own[q * rows : (q + 1) * rows] for q in range(4)]
    sea = sea_int[...].astype(F32)
    own[4 * rows : 5 * rows] = sea
    lane16 = lanes_of(16)
    lane8 = lanes_of(8)
    row8 = lax.broadcasted_iota(jnp.int32, (8, LANES), 0)

    def edges(first):
        packed = jnp.zeros((16, LANES), F32)
        for half in range(2):
            for q in range(4):
                to = 64 * half + 16 * q
                moved = pltpu.roll(state[q][16 * half : 16 * half + 16], (to - first) % LANES, 1)
                packed = jnp.where((lane16 >= to) & (lane16 < to + 16), moved, packed)
        small = jnp.zeros((8, LANES), F32)
        for g in range(4):
            moved = pltpu.roll(sea[8 * g : 8 * g + 8], (16 * g - first) % LANES, 1)
            small = jnp.where((lane8 >= 16 * g) & (lane8 < 16 * g + 16), moved, small)
        return packed, small

    to_right = edges(LANES - HALO)
    to_left = edges(0)
    me = lax.axis_index("tile")

    for b in range(blocks):
        if b % (blocks // 2) == 0:
            for copy in copies[9 + b : 9 + b + blocks // 2]:
                copy.wait()
        high, low = halves(flux[:, b * LANES : (b + 1) * LANES])
        left = jnp.concatenate(
            [
                jnp.concatenate([high, low], axis=0),
                jnp.concatenate([high, jnp.zeros_like(low)], axis=0),
            ],
            axis=1,
        )
        for k in range(slots):
            w_high, w_low = halves(stage[b, k])
            both = jnp.dot(
                left, jnp.concatenate([w_high, w_low], axis=0), preferred_element_type=F32
            )
            t, r = places[b * slots + k]
            send[t, pl.ds(pl.multiple_of(r * fields, fields), fields), :] = both[:fields] + both[fields:]

    for t in range(tiles):
        toward_right = me < t
        packed = jnp.where(toward_right, to_right[0], to_left[0])
        small = jnp.where(toward_right, to_right[1], to_left[1])
        send[t, base : base + 16, :] = packed
        lefts, rights = max(t - 1, 0), min(t + 1, tiles - 1)
        out = small
        for f in range(WET):
            to = 64 + 16 * f
            part_l = send[lefts, pl.ds(f, CAP, stride=fields), :]
            part_r = send[rights, pl.ds(f, CAP, stride=fields), :]
            part_l = pltpu.roll(part_l, (to - (LANES - HALO)) % LANES, 1)
            part_r = pltpu.roll(part_r, to, 1)
            part = jnp.concatenate([part_l, part_r], axis=0)
            out = jnp.where((lane8 >= to) & (lane8 < to + 16), part, out)
        side = jnp.full((8, LANES), -1, jnp.int32)
        main = jnp.full((8, LANES), -1, jnp.int32)
        for r in range(CAP):
            if t > 0:
                side = jnp.where(row8 == r, table[lefts * CAP + r], side)
            if t < tiles - 1:
                named = table[rights * CAP + r]
                side = jnp.where(row8 == CAP + r, jnp.where(named < 0, -1, named + 32), side)
            main = jnp.where(row8 == r, table[t * CAP + r], main)
        out = jnp.where(lane8 == 112, side.astype(F32), out)
        out = jnp.where(lane8 == 113, main.astype(F32), out)
        send[t, base + 16 : base + 24, :] = out


def spread(hot, values):
    high, low = halves(values)
    return jnp.dot(hot, high, preferred_element_type=F32) + jnp.dot(hot, low, preferred_element_type=F32)


def one_hot(ids):
    lane = lanes_of(ids.shape[0]).astype(F32)
    return jnp.where(lane == ids, 1.0, 0.0).T.astype(BF16)


def slots_of(recv, row, tiles, count):
    chunk = recv.shape[0] // tiles
    return [recv[pl.ds(row + j, tiles, stride=chunk), :] for j in range(count)]


def field_values(recv, f, fields, tiles):
    chunk = recv.shape[0] // tiles
    return jnp.concatenate([recv[pl.ds(r * fields + f, tiles, stride=chunk), :] for r in range(CAP)], axis=0)


def forcing_kernel(recv, state, forcing, *, tiles):
    fields, rows = forcing.shape[:2]
    names = jnp.concatenate(slots_of(recv, CAP * fields + 16, tiles, CAP), axis=0)
    hot = one_hot(names[:, 113:114])[:rows]
    sea = state[4 * rows : 5 * rows]
    for f in range(fields):
        forcing[f] = spread(hot, field_values(recv, f, fields, tiles)) * sea


def place_kernel(recv, state, wet, first, second, left, right, *, tiles, fields):
    rows = left.shape[0]
    chunk = recv.shape[0] // tiles
    base = CAP * fields
    names = jnp.concatenate(slots_of(recv, base + 16, tiles, 8), axis=0)
    hot_side = one_hot(names[:, 112:113])[: 2 * rows]
    hot_main = one_hot(names[: CAP * tiles, 113:114])[:rows]
    sea = state[4 * rows : 5 * rows]
    for f in range(WET):
        wet[f * rows : (f + 1) * rows] = spread(hot_main, field_values(recv, f, fields, tiles)) * sea
    sides = spread(hot_side, names)
    lane = lanes_of(rows)
    me = lax.axis_index("tile")
    for which, out in ((0, left), (1, right)):
        source = jnp.maximum(me - 1, 0) if which == 0 else jnp.minimum(me + 1, tiles - 1)
        exists = (me > 0) if which == 0 else (me < tiles - 1)
        start = pl.multiple_of(source * chunk + base, 8)
        packed = recv[pl.ds(start, 16), :]
        small = recv[pl.ds(start + 16, 8), :]
        whole = jnp.concatenate([packed, pltpu.roll(packed, 64, 1)], axis=0)
        sea_part = jnp.concatenate(
            [pltpu.roll(small, (64 - 16 * g) % LANES, 1) for g in range(4)], axis=0
        )
        driven = pltpu.roll(sides[which * rows : (which + 1) * rows], 16, 1)
        full = jnp.where(lane < 64, whole, jnp.where(lane < 80, sea_part, driven))
        full = jnp.where(exists, full, 0.0)
        out[...] = full
    even = lax.axis_index("comp") % 2 == 0
    for message, low in ((first, even), (second, jnp.logical_not(even))):
        start = pl.multiple_of(jnp.where(low, rows - HALO, 0), 8)
        parts = [(state, q) for q in range(5)] + [(wet, f) for f in range(WET)] + [(left, 0), (right, 0)]
        for i, (ref, q) in enumerate(parts):
            message[i * HALO : (i + 1) * HALO, :] = ref[pl.ds(q * rows + start, HALO), :]


def cycle_kernel(
    state, wet, left, right, first, second, height_out, flow_x, flow_y, *, comps
):
    rows = height_out.shape[0]
    even = lax.axis_index("comp") % 2 == 0
    first, second = first[...], second[...]
    above, below = jnp.where(even, second, first), jnp.where(even, first, second)
    total = rows + 2 * HALO
    count = 5 + WET
    own = [state[q * rows : (q + 1) * rows] for q in range(5)]
    own += [wet[f * rows : (f + 1) * rows] for f in range(WET)]
    at = count * 16
    side_l = jnp.concatenate([above[at : at + 16], left[...], below[at : at + 16]], axis=0)
    side_r = jnp.concatenate([above[at + 16 : at + 32], right[...], below[at + 16 : at + 32]], axis=0)
    lane = lanes_of(total)
    wide = []
    for q in range(count):
        center = jnp.concatenate(
            [above[16 * q : 16 * q + 16], own[q], below[16 * q : 16 * q + 16]], axis=0
        )
        from_l = pltpu.roll(side_l, (LANES - HALO - 16 * q) % LANES, 1)
        from_r = pltpu.roll(side_r, (LANES - 16 * q) % LANES, 1)
        side = jnp.where(lane < HALO, from_r, jnp.where(lane >= LANES - HALO, from_l, 0.0))
        wide.append(jnp.concatenate([center, side], axis=1))
    eta, u, v, deep, sea, push_x, push_y, rain = wide
    shape = (total, 2 * LANES)
    row = lax.axis_index("comp") * rows - HALO + lax.broadcasted_iota(jnp.int32, shape, 0)
    inside = (row >= 0) & (row < rows * comps)
    deep, sea = jnp.where(inside, deep, 0.0), jnp.where(inside, sea, 0.0)
    frac = row.astype(F32) / float(rows * comps)
    turn = (0.02 + 0.06 * frac) * sea
    inverse = jnp.where(deep > 0.0, 1.0 / jnp.where(deep > 0.0, deep, 1.0), 0.0)
    wind_x = sea * (0.05 * push_x * inverse)
    wind_y = sea * (0.05 * push_y * inverse)
    fresh = sea * (0.1 * rain)
    slope = 0.2 * sea
    deep = 0.2 * deep

    def cols(x):
        return pltpu.roll(x, 2 * LANES - 1, 1) - pltpu.roll(x, 1, 1)

    def lines(x):
        return pltpu.roll(x, total - 1, 0) - pltpu.roll(x, 1, 0)

    through_x, through_y = deep * u, deep * v
    eta, u, v = sea * eta, sea * u, sea * v
    for _ in range(NSUB):
        eta = eta + fresh - sea * (cols(through_x) + lines(through_y))
        next_u = 0.98 * u - slope * cols(eta) + turn * v + wind_x
        next_v = 0.98 * v - slope * lines(eta) - turn * u + wind_y
        u, v = next_u, next_v
        through_x, through_y = deep * u, deep * v
    height_out[...] = eta[HALO : HALO + rows, :LANES]
    flow_x[...] = u[HALO : HALO + rows, :LANES]
    flow_y[...] = v[HALO : HALO + rows, :LANES]


def swaps(parity, comps, tiles):
    pairs = []
    for s in range(comps):
        other = s + 1 if s % 2 == parity else s - 1
        for t in range(tiles):
            there = other * tiles + t if 0 <= other < comps else s * tiles + (t ^ 1)
            pairs.append((s * tiles + t, there))
    return pairs


def local(tiles, comps, flux, weight, dest_tile, dest_block, count, height, vel_x, vel_y, depth, mask):
    fields = flux.shape[0]
    blocks, slots = dest_tile.shape
    rows, cols = height.shape
    chunk = CAP * fields + 24
    state = (height, vel_x, vel_y, depth, mask)
    plane = jax.ShapeDtypeStruct((rows, cols), F32)
    params = pltpu.CompilerParams(vmem_limit_bytes=16 * 1024 * 1024)

    def near(*shape):
        return pltpu.VMEM(shape, F32)

    def far(x):
        return pltpu.with_memory_space_constraint(x, pltpu.HBM)

    send, own = pl.pallas_call(
        remap_kernel,
        out_shape=[near(tiles, chunk, LANES), near(5 * rows, cols)],
        in_specs=[HBM] * 10,
        out_specs=[VMEM] * 2,
        scratch_shapes=[
            pltpu.VMEM(flux.shape, F32),
            pltpu.VMEM(weight.shape, F32),
            pltpu.SMEM((slots, blocks), jnp.int32),
            pltpu.SMEM((slots, blocks), jnp.int32),
            pltpu.SMEM((blocks,), jnp.int32),
            pltpu.VMEM((rows, cols), jnp.int32),
            pltpu.SMEM((tiles * CAP,), jnp.int32),
            pltpu.SMEM((tiles,), jnp.int32),
            pltpu.SemaphoreType.DMA((9 + blocks,)),
        ],
        compiler_params=params,
        name="remap",
    )(*map(far, (flux, weight, dest_tile.T, dest_block.T, count, *state)))
    recv = lax.all_to_all(send, "tile", 0, 0, tiled=True).reshape(tiles * chunk, LANES)
    message = near((5 + WET + 2) * 16, LANES)
    wet, first, second, left, right = pl.pallas_call(
        functools.partial(place_kernel, tiles=tiles, fields=fields),
        out_shape=[near(WET * rows, cols), message, message, near(rows, cols), near(rows, cols)],
        in_specs=[VMEM] * 2,
        out_specs=[VMEM] * 5,
        compiler_params=params,
        name="place",
    )(recv, own)
    received = [
        lax.ppermute(x, ("comp", "tile"), swaps(parity, comps, tiles))
        for parity, x in enumerate((first, second))
    ]
    forcing = pl.pallas_call(
        functools.partial(forcing_kernel, tiles=tiles),
        out_shape=jax.ShapeDtypeStruct((fields, rows, cols), F32),
        in_specs=[VMEM] * 2,
        out_specs=VMEM,
        compiler_params=params,
        cost_estimate=pl.CostEstimate(flops=10**8, bytes_accessed=4 * 2**20, transcendentals=0),
        name="forcing",
    )(recv, own)
    outs = pl.pallas_call(
        functools.partial(cycle_kernel, comps=comps),
        out_shape=[plane] * 3,
        in_specs=[VMEM] * 6,
        out_specs=[VMEM] * 3,
        compiler_params=params,
        name="cycles",
    )(own, wet, left, right, *received)
    return (forcing, *outs)


def solution(mesh):
    both = ("comp", "tile")
    grid = P("comp", "tile")
    in_specs = (P(None, both), P(both, None, None, None), P(both, None), P(both, None), P(both)) + (grid,) * 5
    out_specs = (P(None, "comp", "tile"), grid, grid, grid)
    body = functools.partial(local, mesh.shape["tile"], mesh.shape["comp"])
    return jax.shard_map(body, mesh=mesh, in_specs=in_specs, out_specs=out_specs, check_vma=False)
```

```python
import functools

import jax
import jax.numpy as jnp
from jax import lax
from jax.experimental import pallas as pl
from jax.experimental.pallas import tpu as pltpu
from jax.sharding import PartitionSpec as P

NSUB = 8
HALO = 2 * NSUB
CAP = 4
LANES = 128
WET = 3
F32 = jnp.float32
BF16 = jnp.bfloat16
VMEM = pl.BlockSpec(memory_space=pltpu.VMEM)
SMEM = pl.BlockSpec(memory_space=pltpu.SMEM)
HBM = pl.BlockSpec(memory_space=pltpu.HBM)


def halves(x):
    high = x.astype(BF16)
    return high, (x - high.astype(F32)).astype(BF16)


def lanes_of(rows):
    return lax.broadcasted_iota(jnp.int32, (rows, LANES), 1)


def position(k, chips):
    return lax.rem(chips - k, chips) if isinstance(k, jax.Array) else (chips - k) % chips


def remap_kernel(
    flux_far, weight, tile_far, block_far, count_far, height, vel_x, vel_y, depth, mask,
    send, own, flux, stage, held, dest_tile, dest_block, count, sea_int, table, seen, sems, *, tiles,
):
    slots, blocks = dest_tile.shape
    fields, rows = flux.shape[0], height.shape[0]
    values = CAP * fields
    share = values + 8
    chips = tiles // 2
    moves = [(tile_far, dest_tile), (block_far, dest_block), (count_far, count)]
    moves += [(flux_far, flux), (mask, sea_int)]
    moves += [(x, own.at[q * rows : (q + 1) * rows]) for q, x in enumerate((height, vel_x, vel_y, depth))]
    moves += [(weight.at[b], stage.at[b]) for b in range(blocks)]
    copies = [pltpu.make_async_copy(x, y, sems.at[i]) for i, (x, y) in enumerate(moves)]
    for copy in copies:
        copy.start()
    for t in range(tiles):
        seen[t] = 0
        for r in range(CAP):
            table[t * CAP + r] = -1
    held[...] = jnp.zeros(held.shape, F32)
    for copy in copies[:3]:
        copy.wait()
    places = []
    for b in range(blocks):
        live = count[b]
        for k in range(slots):
            t = dest_tile[k, b]
            r = jnp.minimum(seen[t], CAP - 1)
            seen[t] = r + 1
            table[t * CAP + r] = jnp.where(k < live, dest_block[k, b], -1)
            places.append(pl.multiple_of(t * values + r * fields, 8))
    for copy in copies[3:9]:
        copy.wait()
    state = [own[q * rows : (q + 1) * rows] for q in range(4)]
    sea = sea_int[...].astype(F32)
    own[4 * rows : 5 * rows] = sea
    lane16 = lanes_of(16)
    lane8 = lanes_of(8)
    row8 = lax.broadcasted_iota(jnp.int32, (8, LANES), 0)

    def edges(first):
        packed = jnp.zeros((16, LANES), F32)
        for half in range(2):
            for q in range(4):
                to = 64 * half + 16 * q
                moved = pltpu.roll(state[q][16 * half : 16 * half + 16], (to - first) % LANES, 1)
                packed = jnp.where((lane16 >= to) & (lane16 < to + 16), moved, packed)
        small = jnp.zeros((8, LANES), F32)
        for g in range(4):
            moved = pltpu.roll(sea[8 * g : 8 * g + 8], (16 * g - first) % LANES, 1)
            small = jnp.where((lane8 >= 16 * g) & (lane8 < 16 * g + 16), moved, small)
        return jnp.concatenate([packed, small], axis=0)

    me = lax.axis_index("tile")
    core, chip = me % 2, me // 2
    to_right, to_left = edges(LANES - HALO), edges(0)
    tail = 2 * chips * share
    send[tail : tail + 24, :] = jnp.where(core == 0, to_left, to_right)
    send[tail + 24 : tail + 48, :] = jnp.where(core == 0, to_right, to_left)

    for b in range(blocks):
        if b % (blocks // 2) == 0:
            for copy in copies[9 + b : 9 + b + blocks // 2]:
                copy.wait()
        high, low = halves(flux[:, b * LANES : (b + 1) * LANES])
        left = jnp.concatenate(
            [
                jnp.concatenate([high, low], axis=0),
                jnp.concatenate([high, jnp.zeros_like(low)], axis=0),
            ],
            axis=1,
        )
        for k in range(slots):
            w_high, w_low = halves(stage[b, k])
            both = jnp.dot(
                left, jnp.concatenate([w_high, w_low], axis=0), preferred_element_type=F32
            )
            held[pl.ds(places[b * slots + k], fields), :] = both[:fields] + both[fields:]

    for t in range(tiles):
        lefts, rights = max(t - 1, 0), min(t + 1, tiles - 1)
        out = jnp.zeros((8, LANES), F32)
        for f in range(WET):
            to = 64 + 16 * f
            part_l = held[pl.ds(lefts * values + f, CAP, stride=fields), :]
            part_r = held[pl.ds(rights * values + f, CAP, stride=fields), :]
            part_l = pltpu.roll(part_l, (to - (LANES - HALO)) % LANES, 1)
            part_r = pltpu.roll(part_r, to, 1)
            part = jnp.concatenate([part_l, part_r], axis=0)
            out = jnp.where((lane8 >= to) & (lane8 < to + 16), part, out)
        mine = core == t % 2
        offset = position(lax.bitwise_xor(chip, t // 2), chips) * share
        shift = jnp.where(mine, 0, CAP)
        side = jnp.full((8, LANES), -1, jnp.int32)
        main = jnp.zeros((8, LANES), jnp.int32)
        for r in range(CAP):
            if t > 0:
                side = jnp.where(row8 == r, table[lefts * CAP + r], side)
            if t < tiles - 1:
                named = table[rights * CAP + r]
                side = jnp.where(row8 == CAP + r, jnp.where(named < 0, -1, named + 32), side)
            main = jnp.where(row8 == r + shift, table[t * CAP + r], main)
        out = jnp.where(lane8 == 112, side.astype(F32), out)
        out = jnp.where(lane8 == 113, main.astype(F32), out)
        at_names = jnp.where(mine, offset, chips * share + offset + values)
        at_values = jnp.where(mine, offset + 8, chips * share + offset)
        send[pl.ds(pl.multiple_of(at_names, 8), 8), :] = out
        send[pl.ds(pl.multiple_of(at_values, 8), values), :] = held[t * values : (t + 1) * values, :]


def beside(k):
    return k & (k + 1) == 0


def spread(hot, values):
    high, low = halves(values)
    return jnp.dot(hot, high, preferred_element_type=F32) + jnp.dot(hot, low, preferred_element_type=F32)


def one_hot(ids):
    lane = lanes_of(ids.shape[0]).astype(F32)
    return jnp.where(lane == ids, 1.0, 0.0).T.astype(BF16)


def field_values(boxes, f, fields):
    return jnp.concatenate([box[pl.ds(8 + f, 2 * CAP, stride=fields), :] for box in boxes], axis=0)


def names_of(box, values):
    return box[0:8, :], box[8 + 2 * values : 16 + 2 * values, :]


def hot_slots(boxes, values, rows):
    ids = [sum(names_of(box, values)) for box in boxes]
    return one_hot(jnp.concatenate(ids, axis=0)[:, 113:114])[:rows]


def forcing_kernel(*refs):
    boxes, state, forcing = refs[:-2], refs[-2], refs[-1]
    fields, rows = forcing.shape[:2]
    hot = hot_slots(boxes, CAP * fields, rows)
    sea = state[4 * rows : 5 * rows]
    for f in range(fields):
        forcing[f] = spread(hot, field_values(boxes, f, fields)) * sea


def place_kernel(*refs, fields):
    boxes = refs[:-6]
    state, wet, first, second, left, right = refs[-6:]
    rows = left.shape[0]
    chips = len(boxes)
    values = CAP * fields
    names = jnp.concatenate([x for box in boxes for x in names_of(box, values)], axis=0)
    hot_side = one_hot(names[:, 112:113])[: 2 * rows]
    hot_main = hot_slots(boxes, values, rows)
    sea = state[4 * rows : 5 * rows]
    for f in range(WET):
        wet[f * rows : (f + 1) * rows] = spread(hot_main, field_values(boxes, f, fields)) * sea
    sides = spread(hot_side, names)
    lane = lanes_of(rows)
    me = lax.axis_index("tile")
    core, chip = me % 2, me // 2
    beyond = jnp.where(core == 0, chip - 1, chip + 1)
    at = 16 + 2 * values
    facing = boxes[0][at : at + 24, :]
    away = jnp.zeros((24, LANES), F32)
    for k in filter(beside, range(1, chips)):
        away = jnp.where(beyond == lax.bitwise_xor(chip, k), boxes[k][at : at + 24, :], away)
    for which, out in ((0, left), (1, right)):
        edge = jnp.where(core == which, away, facing)
        packed, small = edge[:16], edge[16:]
        whole = jnp.concatenate([packed, pltpu.roll(packed, 64, 1)], axis=0)
        sea_part = jnp.concatenate(
            [pltpu.roll(small, (64 - 16 * g) % LANES, 1) for g in range(4)], axis=0
        )
        driven = pltpu.roll(sides[which * rows : (which + 1) * rows], 16, 1)
        full = jnp.where(lane < 64, whole, jnp.where(lane < 80, sea_part, driven))
        exists = (me > 0) if which == 0 else (me < 2 * chips - 1)
        full = jnp.where(exists, full, 0.0)
        out[...] = full
    even = lax.axis_index("comp") % 2 == 0
    for message, low in ((first, even), (second, jnp.logical_not(even))):
        start = pl.multiple_of(jnp.where(low, rows - HALO, 0), 8)
        parts = [(state, q) for q in range(5)] + [(wet, f) for f in range(WET)] + [(left, 0), (right, 0)]
        for i, (ref, q) in enumerate(parts):
            message[i * HALO : (i + 1) * HALO, :] = ref[pl.ds(q * rows + start, HALO), :]


def cycle_kernel(
    state, wet, left, right, first, second, height_out, flow_x, flow_y, *, comps
):
    rows = height_out.shape[0]
    even = lax.axis_index("comp") % 2 == 0
    first, second = first[...], second[...]
    above, below = jnp.where(even, second, first), jnp.where(even, first, second)
    total = rows + 2 * HALO
    count = 5 + WET
    own = [state[q * rows : (q + 1) * rows] for q in range(5)]
    own += [wet[f * rows : (f + 1) * rows] for f in range(WET)]
    at = count * 16
    side_l = jnp.concatenate([above[at : at + 16], left[...], below[at : at + 16]], axis=0)
    side_r = jnp.concatenate([above[at + 16 : at + 32], right[...], below[at + 16 : at + 32]], axis=0)
    lane = lanes_of(total)
    wide = []
    for q in range(count):
        center = jnp.concatenate(
            [above[16 * q : 16 * q + 16], own[q], below[16 * q : 16 * q + 16]], axis=0
        )
        from_l = pltpu.roll(side_l, (LANES - HALO - 16 * q) % LANES, 1)
        from_r = pltpu.roll(side_r, (LANES - 16 * q) % LANES, 1)
        side = jnp.where(lane < HALO, from_r, jnp.where(lane >= LANES - HALO, from_l, 0.0))
        wide.append(jnp.concatenate([center, side], axis=1))
    eta, u, v, deep, sea, push_x, push_y, rain = wide
    shape = (total, 2 * LANES)
    row = lax.axis_index("comp") * rows - HALO + lax.broadcasted_iota(jnp.int32, shape, 0)
    inside = (row >= 0) & (row < rows * comps)
    deep, sea = jnp.where(inside, deep, 0.0), jnp.where(inside, sea, 0.0)
    frac = row.astype(F32) / float(rows * comps)
    turn = (0.02 + 0.06 * frac) * sea
    inverse = jnp.where(deep > 0.0, 1.0 / jnp.where(deep > 0.0, deep, 1.0), 0.0)
    wind_x = sea * (0.05 * push_x * inverse)
    wind_y = sea * (0.05 * push_y * inverse)
    fresh = sea * (0.1 * rain)
    slope = 0.2 * sea
    deep = 0.2 * deep

    def cols(x):
        return pltpu.roll(x, 2 * LANES - 1, 1) - pltpu.roll(x, 1, 1)

    def lines(x):
        return pltpu.roll(x, total - 1, 0) - pltpu.roll(x, 1, 0)

    through_x, through_y = deep * u, deep * v
    eta, u, v = sea * eta, sea * u, sea * v
    for _ in range(NSUB):
        eta = eta + fresh - sea * (cols(through_x) + lines(through_y))
        next_u = 0.98 * u - slope * cols(eta) + turn * v + wind_x
        next_v = 0.98 * v - slope * lines(eta) - turn * u + wind_y
        u, v = next_u, next_v
        through_x, through_y = deep * u, deep * v
    height_out[...] = eta[HALO : HALO + rows, :LANES]
    flow_x[...] = u[HALO : HALO + rows, :LANES]
    flow_y[...] = v[HALO : HALO + rows, :LANES]


def swaps(parity, comps, tiles):
    pairs = []
    for s in range(comps):
        other = s + 1 if s % 2 == parity else s - 1
        for t in range(tiles):
            there = other * tiles + t if 0 <= other < comps else s * tiles + (t ^ 1)
            pairs.append((s * tiles + t, there))
    return pairs


def local(tiles, comps, flux, weight, dest_tile, dest_block, count, height, vel_x, vel_y, depth, mask):
    fields = flux.shape[0]
    blocks, slots = dest_tile.shape
    rows, cols = height.shape
    state = (height, vel_x, vel_y, depth, mask)
    plane = jax.ShapeDtypeStruct((rows, cols), F32)
    params = pltpu.CompilerParams(vmem_limit_bytes=16 * 1024 * 1024)

    def near(*shape):
        return pltpu.VMEM(shape, F32)

    def far(x):
        return pltpu.with_memory_space_constraint(x, pltpu.HBM)

    values = CAP * fields
    share = values + 8
    chips = tiles // 2
    send, own = pl.pallas_call(
        functools.partial(remap_kernel, tiles=tiles),
        out_shape=[near(2 * chips * share + 48, LANES), near(5 * rows, cols)],
        in_specs=[HBM] * 10,
        out_specs=[VMEM] * 2,
        scratch_shapes=[
            pltpu.VMEM(flux.shape, F32),
            pltpu.VMEM(weight.shape, F32),
            pltpu.VMEM((tiles * values, LANES), F32),
            pltpu.SMEM((slots, blocks), jnp.int32),
            pltpu.SMEM((slots, blocks), jnp.int32),
            pltpu.SMEM((blocks,), jnp.int32),
            pltpu.VMEM((rows, cols), jnp.int32),
            pltpu.SMEM((tiles * CAP,), jnp.int32),
            pltpu.SMEM((tiles,), jnp.int32),
            pltpu.SemaphoreType.DMA((9 + blocks,)),
        ],
        compiler_params=params,
        name="remap",
    )(*map(far, (flux, weight, dest_tile.T, dest_block.T, count, *state)))
    mine, other = send[: chips * share], send[chips * share :]
    other = lax.ppermute(other, "tile", [(t, t ^ 1) for t in range(tiles)])
    away, facing = other[chips * share : chips * share + 24], other[chips * share + 24 :]
    boxes = []
    for k in range(chips):
        at = position(k, chips) * share
        parts = [x[at : at + share] for x in (mine, other)]
        if beside(k):
            parts.append(away if k else facing)
        boxes.append(jnp.concatenate(parts))
    boxes[1:] = [
        lax.ppermute(boxes[k], "tile", [(t, t ^ (2 * k)) for t in range(tiles)]) for k in range(1, chips)
    ]
    message = near((5 + WET + 2) * 16, LANES)
    wet, first, second, left, right = pl.pallas_call(
        functools.partial(place_kernel, fields=fields),
        out_shape=[near(WET * rows, cols), message, message, near(rows, cols), near(rows, cols)],
        in_specs=[VMEM] * (chips + 1),
        out_specs=[VMEM] * 5,
        compiler_params=params,
        name="place",
    )(*boxes, own)
    received = [
        lax.ppermute(x, ("comp", "tile"), swaps(parity, comps, tiles))
        for parity, x in enumerate((first, second))
    ]
    forcing = pl.pallas_call(
        forcing_kernel,
        out_shape=jax.ShapeDtypeStruct((fields, rows, cols), F32),
        in_specs=[VMEM] * (chips + 1),
        out_specs=VMEM,
        compiler_params=params,
        cost_estimate=pl.CostEstimate(flops=10**8, bytes_accessed=4 * 2**20, transcendentals=0),
        name="forcing",
    )(*boxes, own)
    outs = pl.pallas_call(
        functools.partial(cycle_kernel, comps=comps),
        out_shape=[plane] * 3,
        in_specs=[VMEM] * 6,
        out_specs=[VMEM] * 3,
        compiler_params=params,
        name="cycles",
    )(own, wet, left, right, *received)
    return (forcing, *outs)


def solution(mesh):
    both = ("comp", "tile")
    grid = P("comp", "tile")
    in_specs = (P(None, both), P(both, None, None, None), P(both, None), P(both, None), P(both)) + (grid,) * 5
    out_specs = (P(None, "comp", "tile"), grid, grid, grid)
    body = functools.partial(local, mesh.shape["tile"], mesh.shape["comp"])
    return jax.shard_map(body, mesh=mesh, in_specs=in_specs, out_specs=out_specs, check_vma=False)
```

```python
import functools

import jax
import jax.numpy as jnp
from jax import lax
from jax.experimental import pallas as pl
from jax.experimental.pallas import tpu as pltpu
from jax.sharding import PartitionSpec as P

NSUB = 8
HALO = 2 * NSUB
CAP = 4
LANES = 128
ROUNDS = 3
WET = 3
F32 = jnp.float32
BF16 = jnp.bfloat16
VMEM = pl.BlockSpec(memory_space=pltpu.VMEM)
SMEM = pl.BlockSpec(memory_space=pltpu.SMEM)
HBM = pl.BlockSpec(memory_space=pltpu.HBM)


def halves(x):
    high = x.astype(BF16)
    return high, (x - high.astype(F32)).astype(BF16)


def lanes_of(rows):
    return lax.broadcasted_iota(jnp.int32, (rows, LANES), 1)


def position(k, chips):
    return lax.rem(chips - k, chips) if isinstance(k, jax.Array) else (chips - k) % chips


def remap_kernel(
    flux_far, weight, tile_far, block_far, count_far, height, vel_x, vel_y, depth, mask,
    send, own, flux, stage, held, dest_tile, dest_block, count, sea_int, table, seen, sems, *, tiles,
):
    slots, blocks = dest_tile.shape
    fields, rows = flux.shape[0], height.shape[0]
    values = CAP * fields
    share = values + 8
    chips = tiles // 2
    moves = [(tile_far, dest_tile), (block_far, dest_block), (count_far, count)]
    moves += [(flux_far, flux), (mask, sea_int)]
    moves += [(x, own.at[q * rows : (q + 1) * rows]) for q, x in enumerate((height, vel_x, vel_y, depth))]
    moves += [(weight.at[b], stage.at[b]) for b in range(blocks)]
    copies = [pltpu.make_async_copy(x, y, sems.at[i]) for i, (x, y) in enumerate(moves)]
    for copy in copies:
        copy.start()
    for t in range(tiles):
        seen[t] = 0
        for r in range(CAP):
            table[t * CAP + r] = -1
    held[...] = jnp.zeros(held.shape, F32)
    for copy in copies[:3]:
        copy.wait()
    places = []
    for b in range(blocks):
        live = count[b]
        for k in range(slots):
            t = dest_tile[k, b]
            r = jnp.minimum(seen[t], CAP - 1)
            seen[t] = r + 1
            table[t * CAP + r] = jnp.where(k < live, dest_block[k, b], -1)
            places.append(pl.multiple_of(t * values + r * fields, 8))
    for copy in copies[3:9]:
        copy.wait()
    state = [own[q * rows : (q + 1) * rows] for q in range(4)]
    sea = sea_int[...].astype(F32)
    own[4 * rows : 5 * rows] = sea
    lane16 = lanes_of(16)
    lane8 = lanes_of(8)
    row8 = lax.broadcasted_iota(jnp.int32, (8, LANES), 0)

    def edges(first):
        packed = jnp.zeros((16, LANES), F32)
        for half in range(2):
            for q in range(4):
                to = 64 * half + 16 * q
                moved = pltpu.roll(state[q][16 * half : 16 * half + 16], (to - first) % LANES, 1)
                packed = jnp.where((lane16 >= to) & (lane16 < to + 16), moved, packed)
        small = jnp.zeros((8, LANES), F32)
        for g in range(4):
            moved = pltpu.roll(sea[8 * g : 8 * g + 8], (16 * g - first) % LANES, 1)
            small = jnp.where((lane8 >= 16 * g) & (lane8 < 16 * g + 16), moved, small)
        return jnp.concatenate([packed, small], axis=0)

    me = lax.axis_index("tile")
    core, chip = me % 2, me // 2
    to_right, to_left = edges(LANES - HALO), edges(0)
    tail = 2 * chips * share
    send[tail : tail + 24, :] = jnp.where(core == 0, to_left, to_right)
    send[tail + 24 : tail + 48, :] = jnp.where(core == 0, to_right, to_left)

    for b in range(blocks):
        if b % (blocks // 2) == 0:
            for copy in copies[9 + b : 9 + b + blocks // 2]:
                copy.wait()
        high, low = halves(flux[:, b * LANES : (b + 1) * LANES])
        left = jnp.concatenate(
            [
                jnp.concatenate([high, low], axis=0),
                jnp.concatenate([high, jnp.zeros_like(low)], axis=0),
            ],
            axis=1,
        )
        for k in range(slots):
            w_high, w_low = halves(stage[b, k])
            both = jnp.dot(
                left, jnp.concatenate([w_high, w_low], axis=0), preferred_element_type=F32
            )
            held[pl.ds(places[b * slots + k], fields), :] = both[:fields] + both[fields:]

    for t in range(tiles):
        lefts, rights = max(t - 1, 0), min(t + 1, tiles - 1)
        out = jnp.zeros((8, LANES), F32)
        for f in range(WET):
            to = 64 + 16 * f
            part_l = held[pl.ds(lefts * values + f, CAP, stride=fields), :]
            part_r = held[pl.ds(rights * values + f, CAP, stride=fields), :]
            part_l = pltpu.roll(part_l, (to - (LANES - HALO)) % LANES, 1)
            part_r = pltpu.roll(part_r, to, 1)
            part = jnp.concatenate([part_l, part_r], axis=0)
            out = jnp.where((lane8 >= to) & (lane8 < to + 16), part, out)
        mine = core == t % 2
        offset = position(lax.bitwise_xor(chip, t // 2), chips) * share
        shift = jnp.where(mine, 0, CAP)
        side = jnp.full((8, LANES), -1, jnp.int32)
        main = jnp.zeros((8, LANES), jnp.int32)
        for r in range(CAP):
            if t > 0:
                side = jnp.where(row8 == r, table[lefts * CAP + r], side)
            if t < tiles - 1:
                named = table[rights * CAP + r]
                side = jnp.where(row8 == CAP + r, jnp.where(named < 0, -1, named + 32), side)
            main = jnp.where(row8 == r + shift, table[t * CAP + r], main)
        out = jnp.where(lane8 == 112, side.astype(F32), out)
        out = jnp.where(lane8 == 113, main.astype(F32), out)
        at_names = jnp.where(mine, offset, chips * share + offset + values)
        at_values = jnp.where(mine, offset + 8, chips * share + offset)
        send[pl.ds(pl.multiple_of(at_names, 8), 8), :] = out
        send[pl.ds(pl.multiple_of(at_values, 8), values), :] = held[t * values : (t + 1) * values, :]


def beside(k):
    return k & (k + 1) == 0


def spread(hot, values):
    high, low = halves(values)
    return jnp.dot(hot, high, preferred_element_type=F32) + jnp.dot(hot, low, preferred_element_type=F32)


def one_hot(ids):
    lane = lanes_of(ids.shape[0]).astype(F32)
    return jnp.where(lane == ids, 1.0, 0.0).T.astype(BF16)


def field_values(boxes, f, fields):
    return jnp.concatenate([box[pl.ds(8 + f, 2 * CAP, stride=fields), :] for box in boxes], axis=0)


def names_of(box, values):
    return box[0:8, :], box[8 + 2 * values : 16 + 2 * values, :]


def hot_slots(boxes, values, rows):
    ids = [sum(names_of(box, values)) for box in boxes]
    return one_hot(jnp.concatenate(ids, axis=0)[:, 113:114])[:rows]


def forcing_kernel(*refs):
    boxes, state, forcing = refs[:-2], refs[-2], refs[-1]
    fields, rows = forcing.shape[:2]
    hot = hot_slots(boxes, CAP * fields, rows)
    sea = state[4 * rows : 5 * rows]
    for f in range(fields):
        forcing[f] = spread(hot, field_values(boxes, f, fields)) * sea


def place_kernel(*refs, fields):
    boxes = refs[: -4 - ROUNDS]
    state, wet, left, right, *messages = refs[-4 - ROUNDS :]
    rows = left.shape[0]
    chips = len(boxes)
    values = CAP * fields
    names = jnp.concatenate([x for box in boxes for x in names_of(box, values)], axis=0)
    hot_side = one_hot(names[:, 112:113])[: 2 * rows]
    hot_main = hot_slots(boxes, values, rows)
    sea = state[4 * rows : 5 * rows]
    for f in range(WET):
        wet[f * rows : (f + 1) * rows] = spread(hot_main, field_values(boxes, f, fields)) * sea
    sides = spread(hot_side, names)
    lane = lanes_of(rows)
    me = lax.axis_index("tile")
    core, chip = me % 2, me // 2
    beyond = jnp.where(core == 0, chip - 1, chip + 1)
    at = 16 + 2 * values
    facing = boxes[0][at : at + 24, :]
    away = jnp.zeros((24, LANES), F32)
    for k in filter(beside, range(1, chips)):
        away = jnp.where(beyond == lax.bitwise_xor(chip, k), boxes[k][at : at + 24, :], away)
    for which, out in ((0, left), (1, right)):
        edge = jnp.where(core == which, away, facing)
        packed, small = edge[:16], edge[16:]
        whole = jnp.concatenate([packed, pltpu.roll(packed, 64, 1)], axis=0)
        sea_part = jnp.concatenate(
            [pltpu.roll(small, (64 - 16 * g) % LANES, 1) for g in range(4)], axis=0
        )
        driven = pltpu.roll(sides[which * rows : (which + 1) * rows], 16, 1)
        full = jnp.where(lane < 64, whole, jnp.where(lane < 80, sea_part, driven))
        exists = (me > 0) if which == 0 else (me < 2 * chips - 1)
        full = jnp.where(exists, full, 0.0)
        out[...] = full
    section = lax.axis_index("comp")
    for turn, message in enumerate(messages):
        start = pl.multiple_of(jnp.where(lax.rem(section, ROUNDS) == turn, rows - HALO, 0), 8)
        parts = [(state, q) for q in range(5)] + [(wet, f) for f in range(WET)] + [(left, 0), (right, 0)]
        for i, (ref, q) in enumerate(parts):
            message[i * HALO : (i + 1) * HALO, :] = ref[pl.ds(q * rows + start, HALO), :]


def cycle_kernel(
    state, wet, left, right, *refs, comps
):
    height_out, flow_x, flow_y = refs[ROUNDS:]
    rows = height_out.shape[0]
    section = lax.axis_index("comp")
    messages = [ref[...] for ref in refs[:ROUNDS]]
    below, above = messages[0], messages[0]
    for turn in range(1, ROUNDS):
        below = jnp.where(lax.rem(section, ROUNDS) == turn, messages[turn], below)
        above = jnp.where(lax.rem(section + ROUNDS - 1, ROUNDS) == turn, messages[turn], above)
    total = rows + 2 * HALO
    count = 5 + WET
    own = [state[q * rows : (q + 1) * rows] for q in range(5)]
    own += [wet[f * rows : (f + 1) * rows] for f in range(WET)]
    at = count * 16
    side_l = jnp.concatenate([above[at : at + 16], left[...], below[at : at + 16]], axis=0)
    side_r = jnp.concatenate([above[at + 16 : at + 32], right[...], below[at + 16 : at + 32]], axis=0)
    lane = lanes_of(total)
    wide = []
    for q in range(count):
        center = jnp.concatenate(
            [above[16 * q : 16 * q + 16], own[q], below[16 * q : 16 * q + 16]], axis=0
        )
        from_l = pltpu.roll(side_l, (LANES - HALO - 16 * q) % LANES, 1)
        from_r = pltpu.roll(side_r, (LANES - 16 * q) % LANES, 1)
        side = jnp.where(lane < HALO, from_r, jnp.where(lane >= LANES - HALO, from_l, 0.0))
        wide.append(jnp.concatenate([center, side], axis=1))
    eta, u, v, deep, sea, push_x, push_y, rain = wide
    shape = (total, 2 * LANES)
    row = lax.axis_index("comp") * rows - HALO + lax.broadcasted_iota(jnp.int32, shape, 0)
    inside = (row >= 0) & (row < rows * comps)
    deep, sea = jnp.where(inside, deep, 0.0), jnp.where(inside, sea, 0.0)
    frac = row.astype(F32) / float(rows * comps)
    turn = (0.02 + 0.06 * frac) * sea
    inverse = jnp.where(deep > 0.0, 1.0 / jnp.where(deep > 0.0, deep, 1.0), 0.0)
    wind_x = sea * (0.05 * push_x * inverse)
    wind_y = sea * (0.05 * push_y * inverse)
    fresh = sea * (0.1 * rain)
    slope = 0.2 * sea
    deep = 0.2 * deep

    def cols(x):
        return pltpu.roll(x, 2 * LANES - 1, 1) - pltpu.roll(x, 1, 1)

    def lines(x):
        return pltpu.roll(x, total - 1, 0) - pltpu.roll(x, 1, 0)

    through_x, through_y = deep * u, deep * v
    eta, u, v = sea * eta, sea * u, sea * v
    for _ in range(NSUB):
        eta = eta + fresh - sea * (cols(through_x) + lines(through_y))
        next_u = 0.98 * u - slope * cols(eta) + turn * v + wind_x
        next_v = 0.98 * v - slope * lines(eta) - turn * u + wind_y
        u, v = next_u, next_v
        through_x, through_y = deep * u, deep * v
    height_out[...] = eta[HALO : HALO + rows, :LANES]
    flow_x[...] = u[HALO : HALO + rows, :LANES]
    flow_y[...] = v[HALO : HALO + rows, :LANES]


def swaps(turn, comps, tiles):
    pairs = []
    for s in range(comps):
        other = s + 1 if s % ROUNDS == turn else s - 1 if (s - 1) % ROUNDS == turn else -1
        for t in range(tiles):
            there = other * tiles + t if 0 <= other < comps else s * tiles + (t ^ 1)
            pairs.append((s * tiles + t, there))
    return pairs


def local(tiles, comps, flux, weight, dest_tile, dest_block, count, height, vel_x, vel_y, depth, mask):
    fields = flux.shape[0]
    blocks, slots = dest_tile.shape
    rows, cols = height.shape
    state = (height, vel_x, vel_y, depth, mask)
    plane = jax.ShapeDtypeStruct((rows, cols), F32)
    params = pltpu.CompilerParams(vmem_limit_bytes=16 * 1024 * 1024)

    def near(*shape):
        return pltpu.VMEM(shape, F32)

    def far(x):
        return pltpu.with_memory_space_constraint(x, pltpu.HBM)

    values = CAP * fields
    share = values + 8
    chips = tiles // 2
    send, own = pl.pallas_call(
        functools.partial(remap_kernel, tiles=tiles),
        out_shape=[near(2 * chips * share + 48, LANES), near(5 * rows, cols)],
        in_specs=[HBM] * 10,
        out_specs=[VMEM] * 2,
        scratch_shapes=[
            pltpu.VMEM(flux.shape, F32),
            pltpu.VMEM(weight.shape, F32),
            pltpu.VMEM((tiles * values, LANES), F32),
            pltpu.SMEM((slots, blocks), jnp.int32),
            pltpu.SMEM((slots, blocks), jnp.int32),
            pltpu.SMEM((blocks,), jnp.int32),
            pltpu.VMEM((rows, cols), jnp.int32),
            pltpu.SMEM((tiles * CAP,), jnp.int32),
            pltpu.SMEM((tiles,), jnp.int32),
            pltpu.SemaphoreType.DMA((9 + blocks,)),
        ],
        compiler_params=params,
        name="remap",
    )(*map(far, (flux, weight, dest_tile.T, dest_block.T, count, *state)))
    mine, other = send[: chips * share], send[chips * share :]
    other = lax.ppermute(other, "tile", [(t, t ^ 1) for t in range(tiles)])
    away, facing = other[chips * share : chips * share + 24], other[chips * share + 24 :]
    boxes = []
    for k in range(chips):
        at = position(k, chips) * share
        parts = [x[at : at + share] for x in (mine, other)]
        if beside(k):
            parts.append(away if k else facing)
        boxes.append(jnp.concatenate(parts))
    boxes[1:] = [
        lax.ppermute(boxes[k], "tile", [(t, t ^ (2 * k)) for t in range(tiles)]) for k in range(1, chips)
    ]
    message = near((5 + WET + 2) * 16, LANES)
    wet, left, right, *messages = pl.pallas_call(
        functools.partial(place_kernel, fields=fields),
        out_shape=[near(WET * rows, cols), near(rows, cols), near(rows, cols)] + [message] * ROUNDS,
        in_specs=[VMEM] * (chips + 1),
        out_specs=[VMEM] * (3 + ROUNDS),
        compiler_params=params,
        name="place",
    )(*boxes, own)
    received = [
        lax.ppermute(x, ("comp", "tile"), swaps(turn, comps, tiles))
        for turn, x in enumerate(messages)
    ]
    forcing = pl.pallas_call(
        forcing_kernel,
        out_shape=jax.ShapeDtypeStruct((fields, rows, cols), F32),
        in_specs=[VMEM] * (chips + 1),
        out_specs=VMEM,
        compiler_params=params,
        cost_estimate=pl.CostEstimate(flops=10**8, bytes_accessed=4 * 2**20, transcendentals=0),
        name="forcing",
    )(*boxes, own)
    outs = pl.pallas_call(
        functools.partial(cycle_kernel, comps=comps),
        out_shape=[plane] * 3,
        in_specs=[VMEM] * (4 + ROUNDS),
        out_specs=[VMEM] * 3,
        compiler_params=params,
        name="cycles",
    )(own, wet, left, right, *received)
    return (forcing, *outs)


def solution(mesh):
    both = ("comp", "tile")
    grid = P("comp", "tile")
    in_specs = (P(None, both), P(both, None, None, None), P(both, None), P(both, None), P(both)) + (grid,) * 5
    out_specs = (P(None, "comp", "tile"), grid, grid, grid)
    body = functools.partial(local, mesh.shape["tile"], mesh.shape["comp"])
    return jax.shard_map(body, mesh=mesh, in_specs=in_specs, out_specs=out_specs, check_vma=False)
```

```python
import functools

import jax
import jax.numpy as jnp
from jax import lax
from jax.experimental import pallas as pl
from jax.experimental.pallas import tpu as pltpu
from jax.sharding import PartitionSpec as P

NSUB = 8
HALO = 2 * NSUB
CAP = 4
LANES = 128
ROUNDS = 3
WET = 3
F32 = jnp.float32
BF16 = jnp.bfloat16
VMEM = pl.BlockSpec(memory_space=pltpu.VMEM)
SMEM = pl.BlockSpec(memory_space=pltpu.SMEM)
HBM = pl.BlockSpec(memory_space=pltpu.HBM)


def halves(x):
    high = x.astype(BF16)
    return high, (x - high.astype(F32)).astype(BF16)


def lanes_of(rows):
    return lax.broadcasted_iota(jnp.int32, (rows, LANES), 1)


def route(k, core, chips):
    alone = (k == 0) | (k == chips - 1)
    sender = jnp.where(alone, core, lax.rem(k + 1, 2))
    place = jnp.where(alone, k, (k - 1) // 2 * 2 + 1 + jnp.where(sender == core, 0, 1))
    return sender, place


def remap_kernel(
    flux_far, weight, tile_far, block_far, count_far, height, vel_x, vel_y, depth, mask,
    send, own, flux, stage, held, dest_tile, dest_block, count, sea_int, table, seen, sems, *, tiles,
):
    slots, blocks = dest_tile.shape
    fields, rows = flux.shape[0], height.shape[0]
    values = CAP * fields
    share = values + 8
    chips = tiles // 2
    moves = [(tile_far, dest_tile), (block_far, dest_block), (count_far, count)]
    moves += [(flux_far, flux), (mask, sea_int)]
    moves += [(x, own.at[q * rows : (q + 1) * rows]) for q, x in enumerate((height, vel_x, vel_y, depth))]
    moves += [(weight.at[b], stage.at[b]) for b in range(blocks)]
    copies = [pltpu.make_async_copy(x, y, sems.at[i]) for i, (x, y) in enumerate(moves)]
    for copy in copies:
        copy.start()
    for t in range(tiles):
        seen[t] = 0
        for r in range(CAP):
            table[t * CAP + r] = -1
    held[...] = jnp.zeros(held.shape, F32)
    for copy in copies[:3]:
        copy.wait()
    places = []
    for b in range(blocks):
        live = count[b]
        for k in range(slots):
            t = dest_tile[k, b]
            r = jnp.minimum(seen[t], CAP - 1)
            seen[t] = r + 1
            table[t * CAP + r] = jnp.where(k < live, dest_block[k, b], -1)
            places.append(pl.multiple_of(t * values + r * fields, 8))
    for copy in copies[3:9]:
        copy.wait()
    state = [own[q * rows : (q + 1) * rows] for q in range(4)]
    sea = sea_int[...].astype(F32)
    own[4 * rows : 5 * rows] = sea
    lane16 = lanes_of(16)
    lane8 = lanes_of(8)
    row8 = lax.broadcasted_iota(jnp.int32, (8, LANES), 0)

    def edges(first):
        packed = jnp.zeros((16, LANES), F32)
        for half in range(2):
            for q in range(4):
                to = 64 * half + 16 * q
                moved = pltpu.roll(state[q][16 * half : 16 * half + 16], (to - first) % LANES, 1)
                packed = jnp.where((lane16 >= to) & (lane16 < to + 16), moved, packed)
        small = jnp.zeros((8, LANES), F32)
        for g in range(4):
            moved = pltpu.roll(sea[8 * g : 8 * g + 8], (16 * g - first) % LANES, 1)
            small = jnp.where((lane8 >= 16 * g) & (lane8 < 16 * g + 16), moved, small)
        return jnp.concatenate([packed, small], axis=0)

    me = lax.axis_index("tile")
    core, chip = me % 2, me // 2
    to_right, to_left = edges(LANES - HALO), edges(0)
    tail = 2 * chips * share
    send[tail : tail + 24, :] = jnp.where(core == 0, to_left, to_right)
    send[tail + 24 : tail + 48, :] = jnp.where(core == 0, to_right, to_left)

    for b in range(blocks):
        if b % (blocks // 2) == 0:
            for copy in copies[9 + b : 9 + b + blocks // 2]:
                copy.wait()
        high, low = halves(flux[:, b * LANES : (b + 1) * LANES])
        left = jnp.concatenate(
            [
                jnp.concatenate([high, low], axis=0),
                jnp.concatenate([high, jnp.zeros_like(low)], axis=0),
            ],
            axis=1,
        )
        for k in range(slots):
            w_high, w_low = halves(stage[b, k])
            both = jnp.dot(
                left, jnp.concatenate([w_high, w_low], axis=0), preferred_element_type=F32
            )
            held[pl.ds(places[b * slots + k], fields), :] = both[:fields] + both[fields:]

    for t in range(tiles):
        lefts, rights = max(t - 1, 0), min(t + 1, tiles - 1)
        out = jnp.zeros((8, LANES), F32)
        for f in range(WET):
            to = 64 + 16 * f
            part_l = held[pl.ds(lefts * values + f, CAP, stride=fields), :]
            part_r = held[pl.ds(rights * values + f, CAP, stride=fields), :]
            part_l = pltpu.roll(part_l, (to - (LANES - HALO)) % LANES, 1)
            part_r = pltpu.roll(part_r, to, 1)
            part = jnp.concatenate([part_l, part_r], axis=0)
            out = jnp.where((lane8 >= to) & (lane8 < to + 16), part, out)
        sender, place = route(lax.bitwise_xor(chip, t // 2), t % 2, chips)
        mine = core == sender
        offset = place * share
        shift = jnp.where(mine, 0, CAP)
        side = jnp.full((8, LANES), -1, jnp.int32)
        main = jnp.zeros((8, LANES), jnp.int32)
        for r in range(CAP):
            if t > 0:
                side = jnp.where(row8 == r, table[lefts * CAP + r], side)
            if t < tiles - 1:
                named = table[rights * CAP + r]
                side = jnp.where(row8 == CAP + r, jnp.where(named < 0, -1, named + 32), side)
            main = jnp.where(row8 == r + shift, table[t * CAP + r], main)
        out = jnp.where(lane8 == 112, side.astype(F32), out)
        out = jnp.where(lane8 == 113, main.astype(F32), out)
        at_names = jnp.where(mine, offset, chips * share + offset + values)
        at_values = jnp.where(mine, offset + 8, chips * share + offset)
        send[pl.ds(pl.multiple_of(at_names, 8), 8), :] = out
        send[pl.ds(pl.multiple_of(at_values, 8), values), :] = held[t * values : (t + 1) * values, :]


def beside(k):
    return k & (k + 1) == 0


def pairs_of(chips):
    return range(1, chips - 1, 2)


def spread(hot, values):
    high, low = halves(values)
    return jnp.dot(hot, high, preferred_element_type=F32) + jnp.dot(hot, low, preferred_element_type=F32)


def one_hot(ids):
    lane = lanes_of(ids.shape[0]).astype(F32)
    return jnp.where(lane == ids, 1.0, 0.0).T.astype(BF16)


def field_values(boxes, f, fields):
    return jnp.concatenate([box[pl.ds(8 + f, 2 * CAP, stride=fields), :] for box in boxes], axis=0)


def names_of(box, values):
    return box[0:8, :], box[8 + 2 * values : 16 + 2 * values, :]


def hot_slots(boxes, values, rows):
    ids = [sum(names_of(box, values)) for box in boxes]
    return one_hot(jnp.concatenate(ids, axis=0)[:, 113:114])[:rows]


def forcing_kernel(*refs):
    boxes, state, forcing = refs[:-2], refs[-2], refs[-1]
    fields, rows = forcing.shape[:2]
    hot = hot_slots(boxes, CAP * fields, rows)
    sea = state[4 * rows : 5 * rows]
    for f in range(fields):
        forcing[f] = spread(hot, field_values(boxes, f, fields)) * sea


def place_kernel(*refs, fields):
    boxes = refs[: -4 - ROUNDS]
    state, wet, left, right, *messages = refs[-4 - ROUNDS :]
    rows = left.shape[0]
    chips = len(boxes)
    values = CAP * fields
    names = jnp.concatenate([x for box in boxes for x in names_of(box, values)], axis=0)
    hot_side = one_hot(names[:, 112:113])[: 2 * rows]
    hot_main = hot_slots(boxes, values, rows)
    sea = state[4 * rows : 5 * rows]
    for f in range(WET):
        wet[f * rows : (f + 1) * rows] = spread(hot_main, field_values(boxes, f, fields)) * sea
    sides = spread(hot_side, names)
    lane = lanes_of(rows)
    me = lax.axis_index("tile")
    core, chip = me % 2, me // 2
    beyond = jnp.where(core == 0, chip - 1, chip + 1)
    at = 16 + 2 * values
    facing, away = boxes[0][at : at + 24, :], boxes[-1][at : at + 24, :]
    for k in filter(beside, pairs_of(chips)):
        direct, passed = boxes[k][2 * at : 2 * at + 24, :], boxes[k + 1][at : at + 24, :]
        away = jnp.where(beyond == lax.bitwise_xor(chip, k), jnp.where(core == 0, direct, passed), away)
    for which, out in ((0, left), (1, right)):
        edge = jnp.where(core == which, away, facing)
        packed, small = edge[:16], edge[16:]
        whole = jnp.concatenate([packed, pltpu.roll(packed, 64, 1)], axis=0)
        sea_part = jnp.concatenate(
            [pltpu.roll(small, (64 - 16 * g) % LANES, 1) for g in range(4)], axis=0
        )
        driven = pltpu.roll(sides[which * rows : (which + 1) * rows], 16, 1)
        full = jnp.where(lane < 64, whole, jnp.where(lane < 80, sea_part, driven))
        exists = (me > 0) if which == 0 else (me < 2 * chips - 1)
        full = jnp.where(exists, full, 0.0)
        out[...] = full
    section = lax.axis_index("comp")
    for turn, message in enumerate(messages):
        start = pl.multiple_of(jnp.where(lax.rem(section, ROUNDS) == turn, rows - HALO, 0), 8)
        parts = [(state, q) for q in range(5)] + [(wet, f) for f in range(WET)] + [(left, 0), (right, 0)]
        for i, (ref, q) in enumerate(parts):
            message[i * HALO : (i + 1) * HALO, :] = ref[pl.ds(q * rows + start, HALO), :]


def cycle_kernel(
    state, wet, left, right, *refs, comps
):
    height_out, flow_x, flow_y = refs[ROUNDS:]
    rows = height_out.shape[0]
    section = lax.axis_index("comp")
    messages = [ref[...] for ref in refs[:ROUNDS]]
    below, above = messages[0], messages[0]
    for turn in range(1, ROUNDS):
        below = jnp.where(lax.rem(section, ROUNDS) == turn, messages[turn], below)
        above = jnp.where(lax.rem(section + ROUNDS - 1, ROUNDS) == turn, messages[turn], above)
    total = rows + 2 * HALO
    count = 5 + WET
    own = [state[q * rows : (q + 1) * rows] for q in range(5)]
    own += [wet[f * rows : (f + 1) * rows] for f in range(WET)]
    at = count * 16
    side_l = jnp.concatenate([above[at : at + 16], left[...], below[at : at + 16]], axis=0)
    side_r = jnp.concatenate([above[at + 16 : at + 32], right[...], below[at + 16 : at + 32]], axis=0)
    lane = lanes_of(total)
    wide = []
    for q in range(count):
        center = jnp.concatenate(
            [above[16 * q : 16 * q + 16], own[q], below[16 * q : 16 * q + 16]], axis=0
        )
        from_l = pltpu.roll(side_l, (LANES - HALO - 16 * q) % LANES, 1)
        from_r = pltpu.roll(side_r, (LANES - 16 * q) % LANES, 1)
        side = jnp.where(lane < HALO, from_r, jnp.where(lane >= LANES - HALO, from_l, 0.0))
        wide.append(jnp.concatenate([center, side], axis=1))
    eta, u, v, deep, sea, push_x, push_y, rain = wide
    shape = (total, 2 * LANES)
    row = lax.axis_index("comp") * rows - HALO + lax.broadcasted_iota(jnp.int32, shape, 0)
    inside = (row >= 0) & (row < rows * comps)
    deep, sea = jnp.where(inside, deep, 0.0), jnp.where(inside, sea, 0.0)
    frac = row.astype(F32) / float(rows * comps)
    turn = (0.02 + 0.06 * frac) * sea
    inverse = jnp.where(deep > 0.0, 1.0 / jnp.where(deep > 0.0, deep, 1.0), 0.0)
    wind_x = sea * (0.05 * push_x * inverse)
    wind_y = sea * (0.05 * push_y * inverse)
    fresh = sea * (0.1 * rain)
    slope = 0.2 * sea
    deep = 0.2 * deep

    def cols(x):
        return pltpu.roll(x, 2 * LANES - 1, 1) - pltpu.roll(x, 1, 1)

    def lines(x):
        return pltpu.roll(x, total - 1, 0) - pltpu.roll(x, 1, 0)

    through_x, through_y = deep * u, deep * v
    eta, u, v = sea * eta, sea * u, sea * v
    for _ in range(NSUB):
        eta = eta + fresh - sea * (cols(through_x) + lines(through_y))
        next_u = 0.98 * u - slope * cols(eta) + turn * v + wind_x
        next_v = 0.98 * v - slope * lines(eta) - turn * u + wind_y
        u, v = next_u, next_v
        through_x, through_y = deep * u, deep * v
    height_out[...] = eta[HALO : HALO + rows, :LANES]
    flow_x[...] = u[HALO : HALO + rows, :LANES]
    flow_y[...] = v[HALO : HALO + rows, :LANES]


def swaps(turn, comps, tiles):
    pairs = []
    for s in range(comps):
        other = s + 1 if s % ROUNDS == turn else s - 1 if (s - 1) % ROUNDS == turn else -1
        for t in range(tiles):
            there = other * tiles + t if 0 <= other < comps else s * tiles + (t ^ 1)
            pairs.append((s * tiles + t, there))
    return pairs


def local(tiles, comps, flux, weight, dest_tile, dest_block, count, height, vel_x, vel_y, depth, mask):
    fields = flux.shape[0]
    blocks, slots = dest_tile.shape
    rows, cols = height.shape
    state = (height, vel_x, vel_y, depth, mask)
    plane = jax.ShapeDtypeStruct((rows, cols), F32)
    params = pltpu.CompilerParams(vmem_limit_bytes=16 * 1024 * 1024)

    def near(*shape):
        return pltpu.VMEM(shape, F32)

    def far(x):
        return pltpu.with_memory_space_constraint(x, pltpu.HBM)

    values = CAP * fields
    share = values + 8
    chips = tiles // 2
    send, own = pl.pallas_call(
        functools.partial(remap_kernel, tiles=tiles),
        out_shape=[near(2 * chips * share + 48, LANES), near(5 * rows, cols)],
        in_specs=[HBM] * 10,
        out_specs=[VMEM] * 2,
        scratch_shapes=[
            pltpu.VMEM(flux.shape, F32),
            pltpu.VMEM(weight.shape, F32),
            pltpu.VMEM((tiles * values, LANES), F32),
            pltpu.SMEM((slots, blocks), jnp.int32),
            pltpu.SMEM((slots, blocks), jnp.int32),
            pltpu.SMEM((blocks,), jnp.int32),
            pltpu.VMEM((rows, cols), jnp.int32),
            pltpu.SMEM((tiles * CAP,), jnp.int32),
            pltpu.SMEM((tiles,), jnp.int32),
            pltpu.SemaphoreType.DMA((9 + blocks,)),
        ],
        compiler_params=params,
        name="remap",
    )(*map(far, (flux, weight, dest_tile.T, dest_block.T, count, *state)))
    mine, other = send[: chips * share], send[chips * share :]
    other = lax.ppermute(other, "tile", [(t, t ^ 1) for t in range(tiles)])
    away, facing = other[chips * share : chips * share + 24], other[chips * share + 24 :]

    def joined(place):
        return [x[place * share : (place + 1) * share] for x in (mine, other)]

    tile = lax.axis_index("tile")
    outward = send[2 * chips * share : 2 * chips * share + 24]
    boxes = [jnp.concatenate(joined(0) + [facing])]
    for k in pairs_of(chips):
        parts = joined(k) + joined(k + 1)
        if beside(k):
            up = lax.bitwise_xor(tile // 2, k) > tile // 2
            parts.append(jnp.where(up, away, outward))
        swap = [(t, t ^ (2 * (k + t % 2))) for t in range(tiles)]
        box = lax.ppermute(jnp.concatenate(parts), "tile", swap)
        boxes += [box, lax.ppermute(box[2 * share :], "tile", [(t, t ^ 1) for t in range(tiles)])]
    swap = [(t, t ^ (2 * (chips - 1))) for t in range(tiles)]
    boxes.append(lax.ppermute(jnp.concatenate(joined(chips - 1) + [away]), "tile", swap))
    message = near((5 + WET + 2) * 16, LANES)
    wet, left, right, *messages = pl.pallas_call(
        functools.partial(place_kernel, fields=fields),
        out_shape=[near(WET * rows, cols), near(rows, cols), near(rows, cols)] + [message] * ROUNDS,
        in_specs=[VMEM] * (chips + 1),
        out_specs=[VMEM] * (3 + ROUNDS),
        compiler_params=params,
        name="place",
    )(*boxes, own)
    received = [
        lax.ppermute(x, ("comp", "tile"), swaps(turn, comps, tiles))
        for turn, x in enumerate(messages)
    ]
    forcing = pl.pallas_call(
        forcing_kernel,
        out_shape=jax.ShapeDtypeStruct((fields, rows, cols), F32),
        in_specs=[VMEM] * (chips + 1),
        out_specs=VMEM,
        compiler_params=params,
        cost_estimate=pl.CostEstimate(flops=10**8, bytes_accessed=4 * 2**20, transcendentals=0),
        name="forcing",
    )(*boxes, own)
    outs = pl.pallas_call(
        functools.partial(cycle_kernel, comps=comps),
        out_shape=[plane] * 3,
        in_specs=[VMEM] * (4 + ROUNDS),
        out_specs=[VMEM] * 3,
        compiler_params=params,
        name="cycles",
    )(own, wet, left, right, *received)
    return (forcing, *outs)


def solution(mesh):
    both = ("comp", "tile")
    grid = P("comp", "tile")
    in_specs = (P(None, both), P(both, None, None, None), P(both, None), P(both, None), P(both)) + (grid,) * 5
    out_specs = (P(None, "comp", "tile"), grid, grid, grid)
    body = functools.partial(local, mesh.shape["tile"], mesh.shape["comp"])
    return jax.shard_map(body, mesh=mesh, in_specs=in_specs, out_specs=out_specs, check_vma=False)
```

```python
import functools

import jax
import jax.numpy as jnp
from jax import lax
from jax.experimental import pallas as pl
from jax.experimental.pallas import tpu as pltpu
from jax.sharding import PartitionSpec as P

NSUB = 8
HALO = 2 * NSUB
CAP = 4
LANES = 128
ROUNDS = 3
WET = 3
F32 = jnp.float32
BF16 = jnp.bfloat16
VMEM = pl.BlockSpec(memory_space=pltpu.VMEM)
SMEM = pl.BlockSpec(memory_space=pltpu.SMEM)
HBM = pl.BlockSpec(memory_space=pltpu.HBM)


def halves(x):
    high = x.astype(BF16)
    return high, (x - high.astype(F32)).astype(BF16)


def lanes_of(rows):
    return lax.broadcasted_iota(jnp.int32, (rows, LANES), 1)


def route(k, core, chips):
    alone = (k == 0) | (k == chips - 1)
    sender = jnp.where(k == 0, core, jnp.where(alone, 1 - core, lax.rem(k + 1, 2)))
    place = jnp.where(alone, k, (k - 1) // 2 * 2 + 1 + jnp.where(sender == core, 1, 0))
    return sender, place


def remap_kernel(
    flux_far, weight, tile_far, block_far, count_far, height, vel_x, vel_y, depth, mask,
    send, own, flux, stage, held, dest_tile, dest_block, count, sea_int, table, seen, sems, *, tiles,
):
    slots, blocks = dest_tile.shape
    fields, rows = flux.shape[0], height.shape[0]
    values = CAP * fields
    share = values + 8
    chips = tiles // 2
    moves = [(tile_far, dest_tile), (block_far, dest_block), (count_far, count)]
    moves += [(flux_far, flux), (mask, sea_int)]
    moves += [(x, own.at[q * rows : (q + 1) * rows]) for q, x in enumerate((height, vel_x, vel_y, depth))]
    moves += [(weight.at[b], stage.at[b]) for b in range(blocks)]
    copies = [pltpu.make_async_copy(x, y, sems.at[i]) for i, (x, y) in enumerate(moves)]
    for copy in copies:
        copy.start()
    for t in range(tiles):
        seen[t] = 0
        for r in range(CAP):
            table[t * CAP + r] = -1
    held[...] = jnp.zeros(held.shape, F32)
    for copy in copies[:3]:
        copy.wait()
    places = []
    for b in range(blocks):
        live = count[b]
        for k in range(slots):
            t = dest_tile[k, b]
            r = jnp.minimum(seen[t], CAP - 1)
            seen[t] = r + 1
            table[t * CAP + r] = jnp.where(k < live, dest_block[k, b], -1)
            places.append(pl.multiple_of(t * values + r * fields, 8))
    for copy in copies[3:9]:
        copy.wait()
    state = [own[q * rows : (q + 1) * rows] for q in range(4)]
    sea = sea_int[...].astype(F32)
    own[4 * rows : 5 * rows] = sea
    lane16 = lanes_of(16)
    lane8 = lanes_of(8)
    row8 = lax.broadcasted_iota(jnp.int32, (8, LANES), 0)

    def edges(first):
        packed = jnp.zeros((16, LANES), F32)
        for half in range(2):
            for q in range(4):
                to = 64 * half + 16 * q
                moved = pltpu.roll(state[q][16 * half : 16 * half + 16], (to - first) % LANES, 1)
                packed = jnp.where((lane16 >= to) & (lane16 < to + 16), moved, packed)
        small = jnp.zeros((8, LANES), F32)
        for g in range(4):
            moved = pltpu.roll(sea[8 * g : 8 * g + 8], (16 * g - first) % LANES, 1)
            small = jnp.where((lane8 >= 16 * g) & (lane8 < 16 * g + 16), moved, small)
        return jnp.concatenate([packed, small], axis=0)

    me = lax.axis_index("tile")
    core, chip = me % 2, me // 2
    to_right, to_left = edges(LANES - HALO), edges(0)
    tail = 2 * chips * share
    send[tail : tail + 24, :] = jnp.where(core == 0, to_left, to_right)
    send[tail + 24 : tail + 48, :] = jnp.where(core == 0, to_right, to_left)

    for b in range(blocks):
        if b % (blocks // 2) == 0:
            for copy in copies[9 + b : 9 + b + blocks // 2]:
                copy.wait()
        high, low = halves(flux[:, b * LANES : (b + 1) * LANES])
        left = jnp.concatenate(
            [
                jnp.concatenate([high, low], axis=0),
                jnp.concatenate([high, jnp.zeros_like(low)], axis=0),
            ],
            axis=1,
        )
        for k in range(slots):
            w_high, w_low = halves(stage[b, k])
            both = jnp.dot(
                left, jnp.concatenate([w_high, w_low], axis=0), preferred_element_type=F32
            )
            held[pl.ds(places[b * slots + k], fields), :] = both[:fields] + both[fields:]

    for t in range(tiles):
        lefts, rights = max(t - 1, 0), min(t + 1, tiles - 1)
        out = jnp.zeros((8, LANES), F32)
        for f in range(WET):
            to = 64 + 16 * f
            part_l = held[pl.ds(lefts * values + f, CAP, stride=fields), :]
            part_r = held[pl.ds(rights * values + f, CAP, stride=fields), :]
            part_l = pltpu.roll(part_l, (to - (LANES - HALO)) % LANES, 1)
            part_r = pltpu.roll(part_r, to, 1)
            part = jnp.concatenate([part_l, part_r], axis=0)
            out = jnp.where((lane8 >= to) & (lane8 < to + 16), part, out)
        sender, place = route(lax.bitwise_xor(chip, t // 2), t % 2, chips)
        mine = core == sender
        offset = place * share
        shift = jnp.where(mine, 0, CAP)
        side = jnp.full((8, LANES), -1, jnp.int32)
        main = jnp.zeros((8, LANES), jnp.int32)
        for r in range(CAP):
            if t > 0:
                side = jnp.where(row8 == r, table[lefts * CAP + r], side)
            if t < tiles - 1:
                named = table[rights * CAP + r]
                side = jnp.where(row8 == CAP + r, jnp.where(named < 0, -1, named + 32), side)
            main = jnp.where(row8 == r + shift, table[t * CAP + r], main)
        out = jnp.where(lane8 == 112, side.astype(F32), out)
        out = jnp.where(lane8 == 113, main.astype(F32), out)
        at_names = jnp.where(mine, offset, chips * share + offset + values)
        at_values = jnp.where(mine, offset + 8, chips * share + offset)
        send[pl.ds(pl.multiple_of(at_names, 8), 8), :] = out
        send[pl.ds(pl.multiple_of(at_values, 8), values), :] = held[t * values : (t + 1) * values, :]


def beside(k):
    return k & (k + 1) == 0


def pairs_of(chips):
    return range(1, chips - 1, 2)


def spread(hot, values):
    high, low = halves(values)
    return jnp.dot(hot, high, preferred_element_type=F32) + jnp.dot(hot, low, preferred_element_type=F32)


def one_hot(ids):
    lane = lanes_of(ids.shape[0]).astype(F32)
    return jnp.where(lane == ids, 1.0, 0.0).T.astype(BF16)


def field_values(boxes, f, fields):
    return jnp.concatenate([box[pl.ds(8 + f, 2 * CAP, stride=fields), :] for box in boxes], axis=0)


def names_of(box, values):
    return box[0:8, :], box[8 + 2 * values : 16 + 2 * values, :]


def hot_slots(boxes, values, rows):
    ids = [sum(names_of(box, values)) for box in boxes]
    return one_hot(jnp.concatenate(ids, axis=0)[:, 113:114])[:rows]


def forcing_kernel(*refs):
    boxes, state, forcing = refs[:-2], refs[-2], refs[-1]
    fields, rows = forcing.shape[:2]
    hot = hot_slots(boxes, CAP * fields, rows)
    sea = state[4 * rows : 5 * rows]
    for f in range(fields):
        forcing[f] = spread(hot, field_values(boxes, f, fields)) * sea


def place_kernel(*refs, fields):
    boxes = refs[: -4 - ROUNDS]
    state, wet, left, right, *messages = refs[-4 - ROUNDS :]
    rows = left.shape[0]
    chips = len(boxes)
    values = CAP * fields
    names = jnp.concatenate([x for box in boxes for x in names_of(box, values)], axis=0)
    hot_side = one_hot(names[:, 112:113])[: 2 * rows]
    hot_main = hot_slots(boxes, values, rows)
    sea = state[4 * rows : 5 * rows]
    for f in range(WET):
        wet[f * rows : (f + 1) * rows] = spread(hot_main, field_values(boxes, f, fields)) * sea
    sides = spread(hot_side, names)
    lane = lanes_of(rows)
    me = lax.axis_index("tile")
    core, chip = me % 2, me // 2
    beyond = jnp.where(core == 0, chip - 1, chip + 1)
    at = 16 + 2 * values
    facing, away = boxes[0][at : at + 24, :], boxes[-1][at : at + 24, :]
    for k in filter(beside, pairs_of(chips)):
        direct, passed = boxes[k][2 * at : 2 * at + 24, :], boxes[k + 1][at : at + 24, :]
        away = jnp.where(beyond == lax.bitwise_xor(chip, k), jnp.where(core == 1, direct, passed), away)
    for which, out in ((0, left), (1, right)):
        edge = jnp.where(core == which, away, facing)
        packed, small = edge[:16], edge[16:]
        whole = jnp.concatenate([packed, pltpu.roll(packed, 64, 1)], axis=0)
        sea_part = jnp.concatenate(
            [pltpu.roll(small, (64 - 16 * g) % LANES, 1) for g in range(4)], axis=0
        )
        driven = pltpu.roll(sides[which * rows : (which + 1) * rows], 16, 1)
        full = jnp.where(lane < 64, whole, jnp.where(lane < 80, sea_part, driven))
        exists = (me > 0) if which == 0 else (me < 2 * chips - 1)
        full = jnp.where(exists, full, 0.0)
        out[...] = full
    section = lax.axis_index("comp")
    for turn, message in enumerate(messages):
        start = pl.multiple_of(jnp.where(lax.rem(section, ROUNDS) == turn, rows - HALO, 0), 8)
        parts = [(state, q) for q in range(5)] + [(wet, f) for f in range(WET)] + [(left, 0), (right, 0)]
        for i, (ref, q) in enumerate(parts):
            message[i * HALO : (i + 1) * HALO, :] = ref[pl.ds(q * rows + start, HALO), :]


def cycle_kernel(
    state, wet, left, right, *refs, comps
):
    height_out, flow_x, flow_y = refs[ROUNDS:]
    rows = height_out.shape[0]
    section = lax.axis_index("comp")
    messages = [ref[...] for ref in refs[:ROUNDS]]
    below, above = messages[0], messages[0]
    for turn in range(1, ROUNDS):
        below = jnp.where(lax.rem(section, ROUNDS) == turn, messages[turn], below)
        above = jnp.where(lax.rem(section + ROUNDS - 1, ROUNDS) == turn, messages[turn], above)
    total = rows + 2 * HALO
    count = 5 + WET
    own = [state[q * rows : (q + 1) * rows] for q in range(5)]
    own += [wet[f * rows : (f + 1) * rows] for f in range(WET)]
    at = count * 16
    side_l = jnp.concatenate([above[at : at + 16], left[...], below[at : at + 16]], axis=0)
    side_r = jnp.concatenate([above[at + 16 : at + 32], right[...], below[at + 16 : at + 32]], axis=0)
    lane = lanes_of(total)
    wide = []
    for q in range(count):
        center = jnp.concatenate(
            [above[16 * q : 16 * q + 16], own[q], below[16 * q : 16 * q + 16]], axis=0
        )
        from_l = pltpu.roll(side_l, (LANES - HALO - 16 * q) % LANES, 1)
        from_r = pltpu.roll(side_r, (LANES - 16 * q) % LANES, 1)
        side = jnp.where(lane < HALO, from_r, jnp.where(lane >= LANES - HALO, from_l, 0.0))
        wide.append(jnp.concatenate([center, side], axis=1))
    eta, u, v, deep, sea, push_x, push_y, rain = wide
    shape = (total, 2 * LANES)
    row = lax.axis_index("comp") * rows - HALO + lax.broadcasted_iota(jnp.int32, shape, 0)
    inside = (row >= 0) & (row < rows * comps)
    deep, sea = jnp.where(inside, deep, 0.0), jnp.where(inside, sea, 0.0)
    frac = row.astype(F32) / float(rows * comps)
    turn = (0.02 + 0.06 * frac) * sea
    inverse = jnp.where(deep > 0.0, 1.0 / jnp.where(deep > 0.0, deep, 1.0), 0.0)
    wind_x = sea * (0.05 * push_x * inverse)
    wind_y = sea * (0.05 * push_y * inverse)
    fresh = sea * (0.1 * rain)
    slope = 0.2 * sea
    deep = 0.2 * deep

    def cols(x):
        return pltpu.roll(x, 2 * LANES - 1, 1) - pltpu.roll(x, 1, 1)

    def lines(x):
        return pltpu.roll(x, total - 1, 0) - pltpu.roll(x, 1, 0)

    through_x, through_y = deep * u, deep * v
    eta, u, v = sea * eta, sea * u, sea * v
    for _ in range(NSUB):
        eta = eta + fresh - sea * (cols(through_x) + lines(through_y))
        next_u = 0.98 * u - slope * cols(eta) + turn * v + wind_x
        next_v = 0.98 * v - slope * lines(eta) - turn * u + wind_y
        u, v = next_u, next_v
        through_x, through_y = deep * u, deep * v
    height_out[...] = eta[HALO : HALO + rows, :LANES]
    flow_x[...] = u[HALO : HALO + rows, :LANES]
    flow_y[...] = v[HALO : HALO + rows, :LANES]


def swaps(turn, comps, tiles):
    pairs = []
    for s in range(comps):
        other = s + 1 if s % ROUNDS == turn else s - 1 if (s - 1) % ROUNDS == turn else -1
        for t in range(tiles):
            there = other * tiles + t if 0 <= other < comps else s * tiles + (t ^ 1)
            pairs.append((s * tiles + t, there))
    return pairs


def local(tiles, comps, flux, weight, dest_tile, dest_block, count, height, vel_x, vel_y, depth, mask):
    fields = flux.shape[0]
    blocks, slots = dest_tile.shape
    rows, cols = height.shape
    state = (height, vel_x, vel_y, depth, mask)
    plane = jax.ShapeDtypeStruct((rows, cols), F32)
    params = pltpu.CompilerParams(vmem_limit_bytes=16 * 1024 * 1024)

    def near(*shape):
        return pltpu.VMEM(shape, F32)

    def far(x):
        return pltpu.with_memory_space_constraint(x, pltpu.HBM)

    values = CAP * fields
    share = values + 8
    chips = tiles // 2
    send, own = pl.pallas_call(
        functools.partial(remap_kernel, tiles=tiles),
        out_shape=[near(2 * chips * share + 48, LANES), near(5 * rows, cols)],
        in_specs=[HBM] * 10,
        out_specs=[VMEM] * 2,
        scratch_shapes=[
            pltpu.VMEM(flux.shape, F32),
            pltpu.VMEM(weight.shape, F32),
            pltpu.VMEM((tiles * values, LANES), F32),
            pltpu.SMEM((slots, blocks), jnp.int32),
            pltpu.SMEM((slots, blocks), jnp.int32),
            pltpu.SMEM((blocks,), jnp.int32),
            pltpu.VMEM((rows, cols), jnp.int32),
            pltpu.SMEM((tiles * CAP,), jnp.int32),
            pltpu.SMEM((tiles,), jnp.int32),
            pltpu.SemaphoreType.DMA((9 + blocks,)),
        ],
        compiler_params=params,
        name="remap",
    )(*map(far, (flux, weight, dest_tile.T, dest_block.T, count, *state)))
    mine, other = send[: chips * share], send[chips * share :]
    other = lax.ppermute(other, "tile", [(t, t ^ 1) for t in range(tiles)])
    away, facing = other[chips * share : chips * share + 24], other[chips * share + 24 :]

    def joined(place):
        return [x[place * share : (place + 1) * share] for x in (mine, other)]

    tile = lax.axis_index("tile")
    outward = send[2 * chips * share : 2 * chips * share + 24]
    boxes = [jnp.concatenate(joined(0) + [facing])]
    for k in pairs_of(chips):
        parts = joined(k) + joined(k + 1)
        if beside(k):
            up = lax.bitwise_xor(tile // 2, k) > tile // 2
            parts.append(jnp.where(up, away, outward))
        swap = [(t, t ^ (2 * (k + t % 2)) ^ 1) for t in range(tiles)]
        box = lax.ppermute(jnp.concatenate(parts), "tile", swap)
        boxes += [box, lax.ppermute(box[2 * share :], "tile", [(t, t ^ 1) for t in range(tiles)])]
    swap = [(t, t ^ (2 * (chips - 1)) ^ 1) for t in range(tiles)]
    boxes.append(lax.ppermute(jnp.concatenate(joined(chips - 1) + [outward]), "tile", swap))
    message = near((5 + WET + 2) * 16, LANES)
    wet, left, right, *messages = pl.pallas_call(
        functools.partial(place_kernel, fields=fields),
        out_shape=[near(WET * rows, cols), near(rows, cols), near(rows, cols)] + [message] * ROUNDS,
        in_specs=[VMEM] * (chips + 1),
        out_specs=[VMEM] * (3 + ROUNDS),
        compiler_params=params,
        name="place",
    )(*boxes, own)
    received = [
        lax.ppermute(x, ("comp", "tile"), swaps(turn, comps, tiles))
        for turn, x in enumerate(messages)
    ]
    forcing = pl.pallas_call(
        forcing_kernel,
        out_shape=jax.ShapeDtypeStruct((fields, rows, cols), F32),
        in_specs=[VMEM] * (chips + 1),
        out_specs=VMEM,
        compiler_params=params,
        cost_estimate=pl.CostEstimate(flops=10**8, bytes_accessed=4 * 2**20, transcendentals=0),
        name="forcing",
    )(*boxes, own)
    outs = pl.pallas_call(
        functools.partial(cycle_kernel, comps=comps),
        out_shape=[plane] * 3,
        in_specs=[VMEM] * (4 + ROUNDS),
        out_specs=[VMEM] * 3,
        compiler_params=params,
        name="cycles",
    )(own, wet, left, right, *received)
    return (forcing, *outs)


def solution(mesh):
    both = ("comp", "tile")
    grid = P("comp", "tile")
    in_specs = (P(None, both), P(both, None, None, None), P(both, None), P(both, None), P(both)) + (grid,) * 5
    out_specs = (P(None, "comp", "tile"), grid, grid, grid)
    body = functools.partial(local, mesh.shape["tile"], mesh.shape["comp"])
    return jax.shard_map(body, mesh=mesh, in_specs=in_specs, out_specs=out_specs, check_vma=False)
```

```python
import functools

import jax
import jax.numpy as jnp
from jax import lax
from jax.experimental import pallas as pl
from jax.experimental.pallas import tpu as pltpu
from jax.sharding import PartitionSpec as P

NSUB = 8
HALO = 2 * NSUB
CAP = 4
LANES = 128
ROUNDS = 3
WET = 3
F32 = jnp.float32
BF16 = jnp.bfloat16
VMEM = pl.BlockSpec(memory_space=pltpu.VMEM)
SMEM = pl.BlockSpec(memory_space=pltpu.SMEM)
HBM = pl.BlockSpec(memory_space=pltpu.HBM)


def halves(x):
    high = x.astype(BF16)
    return high, (x - high.astype(F32)).astype(BF16)


def lanes_of(rows):
    return lax.broadcasted_iota(jnp.int32, (rows, LANES), 1)


def route(k, core, chips):
    alone = (k == 0) | (k == chips - 1)
    sender = jnp.where(k == 0, core, jnp.where(alone, 1 - core, lax.rem(k + 1, 2)))
    place = jnp.where(alone, k, (k - 1) // 2 * 2 + 1 + jnp.where(sender == core, 1, 0))
    return sender, place


def remap_kernel(
    flux_far, weight, tile_far, block_far, count_far, height, vel_x, vel_y, depth, mask,
    send, own, flux, stage, held, dest_tile, dest_block, count, sea_int, table, seen, sems, *, tiles,
):
    slots, blocks = dest_tile.shape
    fields, rows = flux.shape[0], height.shape[0]
    values = CAP * fields
    share = values + 8
    chips = tiles // 2
    moves = [(tile_far, dest_tile), (block_far, dest_block), (count_far, count)]
    moves += [(flux_far, flux), (mask, sea_int)]
    moves += [(x, own.at[q * rows : (q + 1) * rows]) for q, x in enumerate((height, vel_x, vel_y, depth))]
    moves += [(weight.at[b], stage.at[b]) for b in range(blocks)]
    copies = [pltpu.make_async_copy(x, y, sems.at[i]) for i, (x, y) in enumerate(moves)]
    for copy in copies:
        copy.start()
    for t in range(tiles):
        seen[t] = 0
        for r in range(CAP):
            table[t * CAP + r] = -1
    held[...] = jnp.zeros(held.shape, F32)
    for copy in copies[:3]:
        copy.wait()
    places = []
    for b in range(blocks):
        live = count[b]
        for k in range(slots):
            t = dest_tile[k, b]
            r = jnp.minimum(seen[t], CAP - 1)
            seen[t] = r + 1
            table[t * CAP + r] = jnp.where(k < live, dest_block[k, b], -1)
            places.append(pl.multiple_of(t * values + r * fields, 8))
    for copy in copies[3:9]:
        copy.wait()
    state = [own[q * rows : (q + 1) * rows] for q in range(4)]
    sea = sea_int[...].astype(F32)
    own[4 * rows : 5 * rows] = sea
    lane16 = lanes_of(16)
    lane8 = lanes_of(8)
    row8 = lax.broadcasted_iota(jnp.int32, (8, LANES), 0)

    def edges(first):
        packed = jnp.zeros((16, LANES), F32)
        for half in range(2):
            for q in range(4):
                to = 64 * half + 16 * q
                moved = pltpu.roll(state[q][16 * half : 16 * half + 16], (to - first) % LANES, 1)
                packed = jnp.where((lane16 >= to) & (lane16 < to + 16), moved, packed)
        small = jnp.zeros((8, LANES), F32)
        for g in range(4):
            moved = pltpu.roll(sea[8 * g : 8 * g + 8], (16 * g - first) % LANES, 1)
            small = jnp.where((lane8 >= 16 * g) & (lane8 < 16 * g + 16), moved, small)
        return jnp.concatenate([packed, small], axis=0)

    me = lax.axis_index("tile")
    core, chip = me % 2, me // 2
    to_right, to_left = edges(LANES - HALO), edges(0)
    tail = 2 * chips * share
    send[tail : tail + 24, :] = jnp.where(core == 0, to_left, to_right)
    send[tail + 24 : tail + 48, :] = jnp.where(core == 0, to_right, to_left)

    for b in range(blocks):
        if b % (blocks // 2) == 0:
            for copy in copies[9 + b : 9 + b + blocks // 2]:
                copy.wait()
        high, low = halves(flux[:, b * LANES : (b + 1) * LANES])
        left = jnp.concatenate(
            [
                jnp.concatenate([high, low], axis=0),
                jnp.concatenate([high, jnp.zeros_like(low)], axis=0),
            ],
            axis=1,
        )
        for k in range(slots):
            w_high, w_low = halves(stage[b, k])
            both = jnp.dot(
                left, jnp.concatenate([w_high, w_low], axis=0), preferred_element_type=F32
            )
            held[pl.ds(places[b * slots + k], fields), :] = both[:fields] + both[fields:]

    for t in range(tiles):
        lefts, rights = max(t - 1, 0), min(t + 1, tiles - 1)
        sender, place = route(lax.bitwise_xor(chip, t // 2), t % 2, chips)
        mine = core == sender
        offset = place * share
        shift = jnp.where(mine, 0, CAP)
        first_lane = jnp.where(mine, 0, 64)
        out = jnp.zeros((8, LANES), F32)
        for f in range(WET):
            to = first_lane + 16 * f
            part_l = held[pl.ds(lefts * values + f, CAP, stride=fields), :]
            part_r = held[pl.ds(rights * values + f, CAP, stride=fields), :]
            part_l = pltpu.roll(part_l, to + HALO, 1)
            part_r = pltpu.roll(part_r, to, 1)
            part = jnp.concatenate([part_l, part_r], axis=0)
            out = jnp.where((lane8 >= to) & (lane8 < to + 16), part, out)
        side = jnp.full((8, LANES), -1, jnp.int32)
        main = jnp.zeros((8, LANES), jnp.int32)
        for r in range(CAP):
            if t > 0:
                side = jnp.where(row8 == r, table[lefts * CAP + r], side)
            if t < tiles - 1:
                named = table[rights * CAP + r]
                side = jnp.where(row8 == CAP + r, jnp.where(named < 0, -1, named + 32), side)
            main = jnp.where(row8 == r + shift, table[t * CAP + r], main)
        out = jnp.where(lane8 == first_lane + 48, side.astype(F32), out)
        out = jnp.where(lane8 == 113, main.astype(F32), out)
        at_names = jnp.where(mine, offset, chips * share + offset + values)
        at_values = jnp.where(mine, offset + 8, chips * share + offset)
        send[pl.ds(pl.multiple_of(at_names, 8), 8), :] = out
        send[pl.ds(pl.multiple_of(at_values, 8), values), :] = held[t * values : (t + 1) * values, :]


def beside(k):
    return k & (k + 1) == 0


def pairs_of(chips):
    return range(1, chips - 1, 2)


def spread(hot, values):
    high, low = halves(values)
    return jnp.dot(hot, high, preferred_element_type=F32) + jnp.dot(hot, low, preferred_element_type=F32)


def one_hot(ids):
    lane = lanes_of(ids.shape[0]).astype(F32)
    return jnp.where(lane == ids, 1.0, 0.0).T.astype(BF16)


def field_values(boxes, f, fields):
    return jnp.concatenate([box[pl.ds(8 + f, 2 * CAP, stride=fields), :] for box in boxes], axis=0)


def names_of(boxes):
    return jnp.concatenate([box[0:8, :] for box in boxes], axis=0)


def hot_slots(names, rows):
    return one_hot(names[:, 113:114])[:rows]


def forcing_kernel(*refs):
    boxes, state, forcing = refs[:-2], refs[-2], refs[-1]
    fields, rows = forcing.shape[:2]
    hot = hot_slots(names_of(boxes), rows)
    sea = state[4 * rows : 5 * rows]
    for f in range(fields):
        forcing[f] = spread(hot, field_values(boxes, f, fields)) * sea


def place_kernel(*refs, fields):
    boxes = refs[: -4 - ROUNDS]
    state, wet, left, right, *messages = refs[-4 - ROUNDS :]
    rows = left.shape[0]
    chips = len(boxes)
    values = CAP * fields
    names = names_of(boxes)
    hot_mine, hot_other = (one_hot(names[:, at : at + 1])[: 2 * rows] for at in (48, 112))
    hot_main = hot_slots(names, rows)
    sea = state[4 * rows : 5 * rows]
    for f in range(WET):
        wet[f * rows : (f + 1) * rows] = spread(hot_main, field_values(boxes, f, fields)) * sea
    sides = pltpu.roll(spread(hot_mine, names), 80, 1) + pltpu.roll(spread(hot_other, names), 16, 1)
    lane = lanes_of(rows)
    me = lax.axis_index("tile")
    core, chip = me % 2, me // 2
    beyond = jnp.where(core == 0, chip - 1, chip + 1)
    at = 8 + 2 * values
    facing, away = boxes[0][at : at + 24, :], boxes[-1][at : at + 24, :]
    for k in filter(beside, pairs_of(chips)):
        direct, passed = boxes[k][2 * at : 2 * at + 24, :], boxes[k + 1][at : at + 24, :]
        away = jnp.where(beyond == lax.bitwise_xor(chip, k), jnp.where(core == 1, direct, passed), away)
    for which, out in ((0, left), (1, right)):
        edge = jnp.where(core == which, away, facing)
        packed, small = edge[:16], edge[16:]
        whole = jnp.concatenate([packed, pltpu.roll(packed, 64, 1)], axis=0)
        sea_part = jnp.concatenate(
            [pltpu.roll(small, (64 - 16 * g) % LANES, 1) for g in range(4)], axis=0
        )
        driven = sides[which * rows : (which + 1) * rows]
        full = jnp.where(lane < 64, whole, jnp.where(lane < 80, sea_part, driven))
        exists = (me > 0) if which == 0 else (me < 2 * chips - 1)
        full = jnp.where(exists, full, 0.0)
        out[...] = full
    section = lax.axis_index("comp")
    for turn, message in enumerate(messages):
        start = pl.multiple_of(jnp.where(lax.rem(section, ROUNDS) == turn, rows - HALO, 0), 8)
        parts = [(state, q) for q in range(5)] + [(wet, f) for f in range(WET)] + [(left, 0), (right, 0)]
        for i, (ref, q) in enumerate(parts):
            message[i * HALO : (i + 1) * HALO, :] = ref[pl.ds(q * rows + start, HALO), :]


def cycle_kernel(
    state, wet, left, right, *refs, comps
):
    height_out, flow_x, flow_y = refs[ROUNDS:]
    rows = height_out.shape[0]
    section = lax.axis_index("comp")
    messages = [ref[...] for ref in refs[:ROUNDS]]
    below, above = messages[0], messages[0]
    for turn in range(1, ROUNDS):
        below = jnp.where(lax.rem(section, ROUNDS) == turn, messages[turn], below)
        above = jnp.where(lax.rem(section + ROUNDS - 1, ROUNDS) == turn, messages[turn], above)
    total = rows + 2 * HALO
    count = 5 + WET
    own = [state[q * rows : (q + 1) * rows] for q in range(5)]
    own += [wet[f * rows : (f + 1) * rows] for f in range(WET)]
    at = count * 16
    side_l = jnp.concatenate([above[at : at + 16], left[...], below[at : at + 16]], axis=0)
    side_r = jnp.concatenate([above[at + 16 : at + 32], right[...], below[at + 16 : at + 32]], axis=0)
    lane = lanes_of(total)
    wide = []
    for q in range(count):
        center = jnp.concatenate(
            [above[16 * q : 16 * q + 16], own[q], below[16 * q : 16 * q + 16]], axis=0
        )
        from_l = pltpu.roll(side_l, (LANES - 16 * q) % LANES, 1)
        from_r = pltpu.roll(side_r, (LANES - HALO - 16 * q) % LANES, 1)
        west = jnp.where(lane < HALO, from_l, pltpu.roll(center, HALO, 1))
        east = jnp.where(lane < LANES - HALO, pltpu.roll(center, LANES - HALO, 1), from_r)
        wide.append(jnp.concatenate([west, east], axis=1))
    eta, u, v, deep, sea, push_x, push_y, rain = wide
    shape = (total, 2 * LANES)
    row = lax.axis_index("comp") * rows - HALO + lax.broadcasted_iota(jnp.int32, shape, 0)
    inside = (row >= 0) & (row < rows * comps)
    deep, sea = jnp.where(inside, deep, 0.0), jnp.where(inside, sea, 0.0)
    frac = row.astype(F32) / float(rows * comps)
    turn = (0.02 + 0.06 * frac) * sea
    inverse = jnp.where(deep > 0.0, 1.0 / jnp.where(deep > 0.0, deep, 1.0), 0.0)
    wind_x = sea * (0.05 * push_x * inverse)
    wind_y = sea * (0.05 * push_y * inverse)
    fresh = sea * (0.1 * rain)
    slope = 0.2 * sea
    deep = 0.2 * deep

    def cols(x):
        spans = (x[:, :LANES], x[:, LANES:])
        return jnp.concatenate([pltpu.roll(y, LANES - 1, 1) - pltpu.roll(y, 1, 1) for y in spans], axis=1)

    def lines(x):
        return pltpu.roll(x, x.shape[0] - 1, 0) - pltpu.roll(x, 1, 0)

    through_x, through_y = deep * u, deep * v
    eta, u, v = sea * eta, sea * u, sea * v
    top = HALO
    for cycle in range(NSUB):
        eta = eta + fresh - sea * (cols(through_x) + lines(through_y))
        slope_x, slope_y = cols(eta), lines(eta)
        if cycle == NSUB // 2 - 1:
            top = HALO // 2
            fields = (eta, u, v, sea, slope, turn, fresh, wind_x, wind_y, deep, slope_x, slope_y)
            fields = [x[HALO - top : total - HALO + top] for x in fields]
            eta, u, v, sea, slope, turn, fresh, wind_x, wind_y, deep, slope_x, slope_y = fields
        next_u = 0.98 * u - slope * slope_x + turn * v + wind_x
        next_v = 0.98 * v - slope * slope_y - turn * u + wind_y
        u, v = next_u, next_v
        through_x, through_y = deep * u, deep * v
    half = lanes_of(rows) < LANES // 2
    for out, field in ((height_out, eta), (flow_x, u), (flow_y, v)):
        west, east = field[top : top + rows, :LANES], field[top : top + rows, LANES:]
        out[...] = jnp.where(half, pltpu.roll(west, LANES - HALO, 1), pltpu.roll(east, HALO, 1))


def swaps(turn, comps, tiles):
    pairs = []
    for s in range(comps):
        other = s + 1 if s % ROUNDS == turn else s - 1 if (s - 1) % ROUNDS == turn else -1
        for t in range(tiles):
            there = other * tiles + t if 0 <= other < comps else s * tiles + (t ^ 1)
            pairs.append((s * tiles + t, there))
    return pairs


def local(tiles, comps, flux, weight, dest_tile, dest_block, count, height, vel_x, vel_y, depth, mask):
    fields = flux.shape[0]
    blocks, slots = dest_tile.shape
    rows, cols = height.shape
    state = (height, vel_x, vel_y, depth, mask)
    plane = jax.ShapeDtypeStruct((rows, cols), F32)
    params = pltpu.CompilerParams(vmem_limit_bytes=16 * 1024 * 1024)

    def near(*shape):
        return pltpu.VMEM(shape, F32)

    def far(x):
        return pltpu.with_memory_space_constraint(x, pltpu.HBM)

    values = CAP * fields
    share = values + 8
    chips = tiles // 2
    send, own = pl.pallas_call(
        functools.partial(remap_kernel, tiles=tiles),
        out_shape=[near(2 * chips * share + 48, LANES), near(5 * rows, cols)],
        in_specs=[HBM] * 10,
        out_specs=[VMEM] * 2,
        scratch_shapes=[
            pltpu.VMEM(flux.shape, F32),
            pltpu.VMEM(weight.shape, F32),
            pltpu.VMEM((tiles * values, LANES), F32),
            pltpu.SMEM((slots, blocks), jnp.int32),
            pltpu.SMEM((slots, blocks), jnp.int32),
            pltpu.SMEM((blocks,), jnp.int32),
            pltpu.VMEM((rows, cols), jnp.int32),
            pltpu.SMEM((tiles * CAP,), jnp.int32),
            pltpu.SMEM((tiles,), jnp.int32),
            pltpu.SemaphoreType.DMA((9 + blocks,)),
        ],
        compiler_params=params,
        name="remap",
    )(*map(far, (flux, weight, dest_tile.T, dest_block.T, count, *state)))
    mine, other = send[: chips * share], send[chips * share :]
    other = lax.ppermute(other, "tile", [(t, t ^ 1) for t in range(tiles)])
    away, facing = other[chips * share : chips * share + 24], other[chips * share + 24 :]

    def joined(place):
        left, right = (x[place * share : (place + 1) * share] for x in (mine, other))
        return [left[:8] + right[values:], left[8:], right[:values]]

    tile = lax.axis_index("tile")
    outward = send[2 * chips * share : 2 * chips * share + 24]
    boxes = [jnp.concatenate(joined(0) + [facing])]
    for k in pairs_of(chips):
        parts = joined(k) + joined(k + 1)
        if beside(k):
            up = lax.bitwise_xor(tile // 2, k) > tile // 2
            parts.append(jnp.where(up, away, outward))
        swap = [(t, t ^ (2 * (k + t % 2)) ^ 1) for t in range(tiles)]
        box = lax.ppermute(jnp.concatenate(parts), "tile", swap)
        boxes += [box, lax.ppermute(box[8 + 2 * values :], "tile", [(t, t ^ 1) for t in range(tiles)])]
    swap = [(t, t ^ (2 * (chips - 1)) ^ 1) for t in range(tiles)]
    boxes.append(lax.ppermute(jnp.concatenate(joined(chips - 1) + [outward]), "tile", swap))
    message = near((5 + WET + 2) * 16, LANES)
    wet, left, right, *messages = pl.pallas_call(
        functools.partial(place_kernel, fields=fields),
        out_shape=[near(WET * rows, cols), near(rows, cols), near(rows, cols)] + [message] * ROUNDS,
        in_specs=[VMEM] * (chips + 1),
        out_specs=[VMEM] * (3 + ROUNDS),
        compiler_params=params,
        name="place",
    )(*boxes, own)
    received = [
        lax.ppermute(x, ("comp", "tile"), swaps(turn, comps, tiles))
        for turn, x in enumerate(messages)
    ]
    forcing = pl.pallas_call(
        forcing_kernel,
        out_shape=jax.ShapeDtypeStruct((fields, rows, cols), F32),
        in_specs=[VMEM] * (chips + 1),
        out_specs=VMEM,
        compiler_params=params,
        cost_estimate=pl.CostEstimate(flops=10**8, bytes_accessed=4 * 2**20, transcendentals=0),
        name="forcing",
    )(*boxes, own)
    outs = pl.pallas_call(
        functools.partial(cycle_kernel, comps=comps),
        out_shape=[plane] * 3,
        in_specs=[VMEM] * (4 + ROUNDS),
        out_specs=[VMEM] * 3,
        compiler_params=params,
        name="cycles",
    )(own, wet, left, right, *received)
    return (forcing, *outs)


def solution(mesh):
    both = ("comp", "tile")
    grid = P("comp", "tile")
    in_specs = (P(None, both), P(both, None, None, None), P(both, None), P(both, None), P(both)) + (grid,) * 5
    out_specs = (P(None, "comp", "tile"), grid, grid, grid)
    body = functools.partial(local, mesh.shape["tile"], mesh.shape["comp"])
    return jax.shard_map(body, mesh=mesh, in_specs=in_specs, out_specs=out_specs, check_vma=False)
```

```python
import functools

import jax
import jax.numpy as jnp
from jax import lax
from jax.experimental import pallas as pl
from jax.experimental.pallas import tpu as pltpu
from jax.sharding import PartitionSpec as P

NSUB = 8
HALO = 2 * NSUB
CAP = 4
LANES = 128
EARLY = 3
ROUNDS = 2
WET = 3
F32 = jnp.float32
BF16 = jnp.bfloat16
VMEM = pl.BlockSpec(memory_space=pltpu.VMEM)
SMEM = pl.BlockSpec(memory_space=pltpu.SMEM)
HBM = pl.BlockSpec(memory_space=pltpu.HBM)


def halves(x):
    high = x.astype(BF16)
    return high, (x - high.astype(F32)).astype(BF16)


def lanes_of(rows):
    return lax.broadcasted_iota(jnp.int32, (rows, LANES), 1)


def route(k, core, chips):
    alone = (k == 0) | (k == chips - 1)
    sender = jnp.where(k == 0, core, jnp.where(alone, 1 - core, lax.rem(k + 1, 2)))
    place = jnp.where(alone, k, (k - 1) // 2 * 2 + 1 + jnp.where(sender == core, 1, 0))
    return sender, place


def remap_kernel(
    flux_far, weight, tile_far, block_far, count_far, height, vel_x, vel_y, depth, mask,
    send, own, *refs, tiles,
):
    early = refs[:EARLY]
    flux, stage, held, dest_tile, dest_block, count, sea_int, table, seen, sems = refs[EARLY:]
    slots, blocks = dest_tile.shape
    fields, rows = flux.shape[0], height.shape[0]
    values = CAP * fields
    share = values + 8
    chips = tiles // 2
    moves = [(tile_far, dest_tile), (block_far, dest_block), (count_far, count)]
    moves += [(flux_far, flux), (mask, sea_int)]
    moves += [(x, own.at[q * rows : (q + 1) * rows]) for q, x in enumerate((height, vel_x, vel_y, depth))]
    moves += [(weight.at[b], stage.at[b]) for b in range(blocks)]
    copies = [pltpu.make_async_copy(x, y, sems.at[i]) for i, (x, y) in enumerate(moves)]
    for copy in copies:
        copy.start()
    for t in range(tiles):
        seen[t] = 0
        for r in range(CAP):
            table[t * CAP + r] = -1
    held[...] = jnp.zeros(held.shape, F32)
    for copy in copies[:3]:
        copy.wait()
    places = []
    for b in range(blocks):
        live = count[b]
        for k in range(slots):
            t = dest_tile[k, b]
            r = jnp.minimum(seen[t], CAP - 1)
            seen[t] = r + 1
            table[t * CAP + r] = jnp.where(k < live, dest_block[k, b], -1)
            places.append(pl.multiple_of(t * values + r * fields, 8))
    for copy in copies[3:9]:
        copy.wait()
    state = [own[q * rows : (q + 1) * rows] for q in range(4)]
    sea = sea_int[...].astype(F32)
    own[4 * rows : 5 * rows] = sea
    for turn, message in enumerate(early):
        low = lax.rem(lax.axis_index("comp"), EARLY) == turn
        for q, x in enumerate(state + [sea]):
            message[q * HALO : (q + 1) * HALO, :] = jnp.where(low, x[rows - HALO :], x[:HALO])
    lane16 = lanes_of(16)
    lane8 = lanes_of(8)
    row8 = lax.broadcasted_iota(jnp.int32, (8, LANES), 0)

    def edges(first):
        packed = jnp.zeros((16, LANES), F32)
        for half in range(2):
            for q in range(4):
                to = 64 * half + 16 * q
                moved = pltpu.roll(state[q][16 * half : 16 * half + 16], (to - first) % LANES, 1)
                packed = jnp.where((lane16 >= to) & (lane16 < to + 16), moved, packed)
        small = jnp.zeros((8, LANES), F32)
        for g in range(4):
            moved = pltpu.roll(sea[8 * g : 8 * g + 8], (16 * g - first) % LANES, 1)
            small = jnp.where((lane8 >= 16 * g) & (lane8 < 16 * g + 16), moved, small)
        return jnp.concatenate([packed, small], axis=0)

    me = lax.axis_index("tile")
    core, chip = me % 2, me // 2
    to_right, to_left = edges(LANES - HALO), edges(0)
    tail = 2 * chips * share
    send[tail : tail + 24, :] = jnp.where(core == 0, to_left, to_right)
    send[tail + 24 : tail + 48, :] = jnp.where(core == 0, to_right, to_left)

    for b in range(blocks):
        if b % (blocks // 2) == 0:
            for copy in copies[9 + b : 9 + b + blocks // 2]:
                copy.wait()
        high, low = halves(flux[:, b * LANES : (b + 1) * LANES])
        left = jnp.concatenate(
            [
                jnp.concatenate([high, low], axis=0),
                jnp.concatenate([high, jnp.zeros_like(low)], axis=0),
            ],
            axis=1,
        )
        for k in range(slots):
            w_high, w_low = halves(stage[b, k])
            both = jnp.dot(
                left, jnp.concatenate([w_high, w_low], axis=0), preferred_element_type=F32
            )
            held[pl.ds(places[b * slots + k], fields), :] = both[:fields] + both[fields:]

    for t in range(tiles):
        lefts, rights = max(t - 1, 0), min(t + 1, tiles - 1)
        sender, place = route(lax.bitwise_xor(chip, t // 2), t % 2, chips)
        mine = core == sender
        offset = place * share
        shift = jnp.where(mine, 0, CAP)
        first_lane = jnp.where(mine, 0, 64)
        out = jnp.zeros((8, LANES), F32)
        for f in range(WET):
            to = first_lane + 16 * f
            part_l = held[pl.ds(lefts * values + f, CAP, stride=fields), :]
            part_r = held[pl.ds(rights * values + f, CAP, stride=fields), :]
            part_l = pltpu.roll(part_l, to + HALO, 1)
            part_r = pltpu.roll(part_r, to, 1)
            part = jnp.concatenate([part_l, part_r], axis=0)
            out = jnp.where((lane8 >= to) & (lane8 < to + 16), part, out)
        side = jnp.full((8, LANES), -1, jnp.int32)
        main = jnp.zeros((8, LANES), jnp.int32)
        for r in range(CAP):
            if t > 0:
                side = jnp.where(row8 == r, table[lefts * CAP + r], side)
            if t < tiles - 1:
                named = table[rights * CAP + r]
                side = jnp.where(row8 == CAP + r, jnp.where(named < 0, -1, named + 32), side)
            main = jnp.where(row8 == r + shift, table[t * CAP + r], main)
        out = jnp.where(lane8 == first_lane + 48, side.astype(F32), out)
        out = jnp.where(lane8 == 113, main.astype(F32), out)
        at_names = jnp.where(mine, offset, chips * share + offset + values)
        at_values = jnp.where(mine, offset + 8, chips * share + offset)
        send[pl.ds(pl.multiple_of(at_names, 8), 8), :] = out
        send[pl.ds(pl.multiple_of(at_values, 8), values), :] = held[t * values : (t + 1) * values, :]


def beside(k):
    return k & (k + 1) == 0


def pairs_of(chips):
    return range(1, chips - 1, 2)


def spread(hot, values):
    high, low = halves(values)
    return jnp.dot(hot, high, preferred_element_type=F32) + jnp.dot(hot, low, preferred_element_type=F32)


def one_hot(ids):
    lane = lanes_of(ids.shape[0]).astype(F32)
    return jnp.where(lane == ids, 1.0, 0.0).T.astype(BF16)


def field_values(boxes, f, fields):
    return jnp.concatenate([box[pl.ds(8 + f, 2 * CAP, stride=fields), :] for box in boxes], axis=0)


def names_of(boxes):
    return jnp.concatenate([box[0:8, :] for box in boxes], axis=0)


def hot_slots(names, rows):
    return one_hot(names[:, 113:114])[:rows]


def forcing_kernel(*refs):
    boxes, state, forcing = refs[:-2], refs[-2], refs[-1]
    fields, rows = forcing.shape[:2]
    hot = hot_slots(names_of(boxes), rows)
    sea = state[4 * rows : 5 * rows]
    for f in range(fields):
        forcing[f] = spread(hot, field_values(boxes, f, fields)) * sea


def place_kernel(*refs, fields):
    boxes = refs[: -4 - ROUNDS]
    state, wet, left, right, *messages = refs[-4 - ROUNDS :]
    rows = left.shape[0]
    chips = len(boxes)
    values = CAP * fields
    names = names_of(boxes)
    hot_mine, hot_other = (one_hot(names[:, at : at + 1])[: 2 * rows] for at in (48, 112))
    hot_main = hot_slots(names, rows)
    sea = state[4 * rows : 5 * rows]
    for f in range(WET):
        wet[f * rows : (f + 1) * rows] = spread(hot_main, field_values(boxes, f, fields)) * sea
    sides = pltpu.roll(spread(hot_mine, names), 80, 1) + pltpu.roll(spread(hot_other, names), 16, 1)
    lane = lanes_of(rows)
    me = lax.axis_index("tile")
    core, chip = me % 2, me // 2
    beyond = jnp.where(core == 0, chip - 1, chip + 1)
    at = 8 + 2 * values
    facing, away = boxes[0][at : at + 24, :], boxes[-1][at : at + 24, :]
    for k in filter(beside, pairs_of(chips)):
        direct, passed = boxes[k][2 * at : 2 * at + 24, :], boxes[k + 1][at : at + 24, :]
        away = jnp.where(beyond == lax.bitwise_xor(chip, k), jnp.where(core == 1, direct, passed), away)
    for which, out in ((0, left), (1, right)):
        edge = jnp.where(core == which, away, facing)
        packed, small = edge[:16], edge[16:]
        whole = jnp.concatenate([packed, pltpu.roll(packed, 64, 1)], axis=0)
        sea_part = jnp.concatenate(
            [pltpu.roll(small, (64 - 16 * g) % LANES, 1) for g in range(4)], axis=0
        )
        driven = sides[which * rows : (which + 1) * rows]
        full = jnp.where(lane < 64, whole, jnp.where(lane < 80, sea_part, driven))
        exists = (me > 0) if which == 0 else (me < 2 * chips - 1)
        full = jnp.where(exists, full, 0.0)
        out[...] = full
    section = lax.axis_index("comp")
    for turn, message in enumerate(messages):
        start = pl.multiple_of(jnp.where(lax.rem(section, ROUNDS) == turn, rows - HALO, 0), 8)
        parts = [(wet, f) for f in range(WET)] + [(left, 0), (right, 0)]
        for i, (ref, q) in enumerate(parts):
            message[i * HALO : (i + 1) * HALO, :] = ref[pl.ds(q * rows + start, HALO), :]


def cycle_kernel(
    state, wet, left, right, *refs, comps
):
    height_out, flow_x, flow_y = refs[EARLY + ROUNDS :]
    rows = height_out.shape[0]
    section = lax.axis_index("comp")

    def halves_of(messages):
        turns = len(messages)
        below, above = messages[0][...], messages[0][...]
        for turn in range(1, turns):
            below = jnp.where(lax.rem(section, turns) == turn, messages[turn][...], below)
            above = jnp.where(lax.rem(section + turns - 1, turns) == turn, messages[turn][...], above)
        return above, below

    parts = zip(halves_of(refs[:EARLY]), halves_of(refs[EARLY : EARLY + ROUNDS]))
    above, below = (jnp.concatenate(part, axis=0) for part in parts)
    total = rows + 2 * HALO
    count = 5 + WET
    own = [state[q * rows : (q + 1) * rows] for q in range(5)]
    own += [wet[f * rows : (f + 1) * rows] for f in range(WET)]
    at = count * 16
    side_l = jnp.concatenate([above[at : at + 16], left[...], below[at : at + 16]], axis=0)
    side_r = jnp.concatenate([above[at + 16 : at + 32], right[...], below[at + 16 : at + 32]], axis=0)
    lane = lanes_of(total)
    wide = []
    for q in range(count):
        center = jnp.concatenate(
            [above[16 * q : 16 * q + 16], own[q], below[16 * q : 16 * q + 16]], axis=0
        )
        from_l = pltpu.roll(side_l, (LANES - 16 * q) % LANES, 1)
        from_r = pltpu.roll(side_r, (LANES - HALO - 16 * q) % LANES, 1)
        west = jnp.where(lane < HALO, from_l, pltpu.roll(center, HALO, 1))
        east = jnp.where(lane < LANES - HALO, pltpu.roll(center, LANES - HALO, 1), from_r)
        wide.append(jnp.concatenate([west, east], axis=1))
    eta, u, v, deep, sea, push_x, push_y, rain = wide
    shape = (total, 2 * LANES)
    row = lax.axis_index("comp") * rows - HALO + lax.broadcasted_iota(jnp.int32, shape, 0)
    inside = (row >= 0) & (row < rows * comps)
    deep, sea = jnp.where(inside, deep, 0.0), jnp.where(inside, sea, 0.0)
    frac = row.astype(F32) / float(rows * comps)
    turn = (0.02 + 0.06 * frac) * sea
    inverse = jnp.where(deep > 0.0, 1.0 / jnp.where(deep > 0.0, deep, 1.0), 0.0)
    wind_x = sea * (0.05 * push_x * inverse)
    wind_y = sea * (0.05 * push_y * inverse)
    fresh = sea * (0.1 * rain)
    slope = 0.2 * sea
    deep = 0.2 * deep

    def cols(x):
        spans = (x[:, :LANES], x[:, LANES:])
        return jnp.concatenate([pltpu.roll(y, LANES - 1, 1) - pltpu.roll(y, 1, 1) for y in spans], axis=1)

    def lines(x):
        return pltpu.roll(x, x.shape[0] - 1, 0) - pltpu.roll(x, 1, 0)

    through_x, through_y = deep * u, deep * v
    eta, u, v = sea * eta, sea * u, sea * v
    top = HALO
    for cycle in range(NSUB):
        eta = eta + fresh - sea * (cols(through_x) + lines(through_y))
        slope_x, slope_y = cols(eta), lines(eta)
        if cycle == NSUB // 2 - 1:
            top = HALO // 2
            fields = (eta, u, v, sea, slope, turn, fresh, wind_x, wind_y, deep, slope_x, slope_y)
            fields = [x[HALO - top : total - HALO + top] for x in fields]
            eta, u, v, sea, slope, turn, fresh, wind_x, wind_y, deep, slope_x, slope_y = fields
        next_u = 0.98 * u - slope * slope_x + turn * v + wind_x
        next_v = 0.98 * v - slope * slope_y - turn * u + wind_y
        u, v = next_u, next_v
        through_x, through_y = deep * u, deep * v
    half = lanes_of(rows) < LANES // 2
    for out, field in ((height_out, eta), (flow_x, u), (flow_y, v)):
        west, east = field[top : top + rows, :LANES], field[top : top + rows, LANES:]
        out[...] = jnp.where(half, pltpu.roll(west, LANES - HALO, 1), pltpu.roll(east, HALO, 1))


def swaps(turn, rounds, comps, tiles):
    pairs = []
    for s in range(comps):
        other = s + 1 if s % rounds == turn else s - 1 if (s - 1) % rounds == turn else -1
        for t in range(tiles):
            there = other * tiles + t if 0 <= other < comps else s * tiles + (t ^ 1)
            pairs.append((s * tiles + t, there))
    return pairs


def local(tiles, comps, flux, weight, dest_tile, dest_block, count, height, vel_x, vel_y, depth, mask):
    fields = flux.shape[0]
    blocks, slots = dest_tile.shape
    rows, cols = height.shape
    state = (height, vel_x, vel_y, depth, mask)
    plane = jax.ShapeDtypeStruct((rows, cols), F32)
    params = pltpu.CompilerParams(vmem_limit_bytes=16 * 1024 * 1024)

    def near(*shape):
        return pltpu.VMEM(shape, F32)

    def far(x):
        return pltpu.with_memory_space_constraint(x, pltpu.HBM)

    values = CAP * fields
    share = values + 8
    chips = tiles // 2
    send, own, *early = pl.pallas_call(
        functools.partial(remap_kernel, tiles=tiles),
        out_shape=[near(2 * chips * share + 48, LANES), near(5 * rows, cols)] + [near(5 * HALO, LANES)] * EARLY,
        in_specs=[HBM] * 10,
        out_specs=[VMEM] * (2 + EARLY),
        scratch_shapes=[
            pltpu.VMEM(flux.shape, F32),
            pltpu.VMEM(weight.shape, F32),
            pltpu.VMEM((tiles * values, LANES), F32),
            pltpu.SMEM((slots, blocks), jnp.int32),
            pltpu.SMEM((slots, blocks), jnp.int32),
            pltpu.SMEM((blocks,), jnp.int32),
            pltpu.VMEM((rows, cols), jnp.int32),
            pltpu.SMEM((tiles * CAP,), jnp.int32),
            pltpu.SMEM((tiles,), jnp.int32),
            pltpu.SemaphoreType.DMA((9 + blocks,)),
        ],
        compiler_params=params,
        name="remap",
    )(*map(far, (flux, weight, dest_tile.T, dest_block.T, count, *state)))
    mine, other = send[: chips * share], send[chips * share :]
    other = lax.ppermute(other, "tile", [(t, t ^ 1) for t in range(tiles)])
    away, facing = other[chips * share : chips * share + 24], other[chips * share + 24 :]

    def joined(place):
        left, right = (x[place * share : (place + 1) * share] for x in (mine, other))
        return [left[:8] + right[values:], left[8:], right[:values]]

    tile = lax.axis_index("tile")
    outward = send[2 * chips * share : 2 * chips * share + 24]
    boxes = [jnp.concatenate(joined(0) + [facing])]
    for k in pairs_of(chips):
        parts = joined(k) + joined(k + 1)
        if beside(k):
            up = lax.bitwise_xor(tile // 2, k) > tile // 2
            parts.append(jnp.where(up, away, outward))
        swap = [(t, t ^ (2 * (k + t % 2)) ^ 1) for t in range(tiles)]
        box = lax.ppermute(jnp.concatenate(parts), "tile", swap)
        boxes += [box, lax.ppermute(box[8 + 2 * values :], "tile", [(t, t ^ 1) for t in range(tiles)])]
    swap = [(t, t ^ (2 * (chips - 1)) ^ 1) for t in range(tiles)]
    boxes.append(lax.ppermute(jnp.concatenate(joined(chips - 1) + [outward]), "tile", swap))
    message = near((WET + 2) * HALO, LANES)
    early, boxes[1] = lax.optimization_barrier((early, boxes[1]))
    early = [lax.ppermute(x, ("comp", "tile"), swaps(turn, EARLY, comps, tiles)) for turn, x in enumerate(early)]
    wet, left, right, *messages = pl.pallas_call(
        functools.partial(place_kernel, fields=fields),
        out_shape=[near(WET * rows, cols), near(rows, cols), near(rows, cols)] + [message] * ROUNDS,
        in_specs=[VMEM] * (chips + 1),
        out_specs=[VMEM] * (3 + ROUNDS),
        compiler_params=params,
        name="place",
    )(*boxes, own)
    received = [
        lax.ppermute(x, ("comp", "tile"), swaps(turn, ROUNDS, comps, tiles))
        for turn, x in enumerate(messages)
    ]
    forcing = pl.pallas_call(
        forcing_kernel,
        out_shape=jax.ShapeDtypeStruct((fields, rows, cols), F32),
        in_specs=[VMEM] * (chips + 1),
        out_specs=VMEM,
        compiler_params=params,
        cost_estimate=pl.CostEstimate(flops=10**8, bytes_accessed=4 * 2**20, transcendentals=0),
        name="forcing",
    )(*boxes, own)
    outs = pl.pallas_call(
        functools.partial(cycle_kernel, comps=comps),
        out_shape=[plane] * 3,
        in_specs=[VMEM] * (4 + EARLY + ROUNDS),
        out_specs=[VMEM] * 3,
        compiler_params=params,
        name="cycles",
    )(own, wet, left, right, *early, *received)
    return (forcing, *outs)


def solution(mesh):
    both = ("comp", "tile")
    grid = P("comp", "tile")
    in_specs = (P(None, both), P(both, None, None, None), P(both, None), P(both, None), P(both)) + (grid,) * 5
    out_specs = (P(None, "comp", "tile"), grid, grid, grid)
    body = functools.partial(local, mesh.shape["tile"], mesh.shape["comp"])
    return jax.shard_map(body, mesh=mesh, in_specs=in_specs, out_specs=out_specs, check_vma=False)
```

```python
import functools

import jax
import jax.numpy as jnp
from jax import lax
from jax.experimental import pallas as pl
from jax.experimental.pallas import tpu as pltpu
from jax.sharding import PartitionSpec as P

NSUB = 8
HALO = 2 * NSUB
CAP = 4
LANES = 128
EARLY = 3
ROUNDS = 2
WET = 3
F32 = jnp.float32
BF16 = jnp.bfloat16
VMEM = pl.BlockSpec(memory_space=pltpu.VMEM)
SMEM = pl.BlockSpec(memory_space=pltpu.SMEM)
HBM = pl.BlockSpec(memory_space=pltpu.HBM)


def halves(x):
    high = x.astype(BF16)
    return high, (x - high.astype(F32)).astype(BF16)


def lanes_of(rows):
    return lax.broadcasted_iota(jnp.int32, (rows, LANES), 1)


def route(k, core, chips):
    alone = (k == 0) | (k == chips - 1)
    sender = jnp.where(k == 0, core, jnp.where(alone, 1 - core, lax.rem(k + 1, 2)))
    place = jnp.where(alone, k, (k - 1) // 2 * 2 + 1 + jnp.where(sender == core, 1, 0))
    return sender, place


def remap_kernel(
    flux_far, weight, tile_far, block_far, count_far, height, vel_x, vel_y, depth, mask,
    send, own, *refs, tiles,
):
    early = refs[:EARLY]
    flux, stage, held, dest_tile, dest_block, count, sea_int, table, seen, sems = refs[EARLY:]
    slots, blocks = dest_tile.shape
    fields, rows = flux.shape[0], height.shape[0]
    values = CAP * fields
    share = values + 8
    chips = tiles // 2
    moves = [(tile_far, dest_tile), (block_far, dest_block), (count_far, count)]
    moves += [(flux_far, flux), (mask, sea_int)]
    moves += [(x, own.at[q * rows : (q + 1) * rows]) for q, x in enumerate((height, vel_x, vel_y, depth))]
    moves += [(weight.at[b], stage.at[b]) for b in range(blocks)]
    copies = [pltpu.make_async_copy(x, y, sems.at[i]) for i, (x, y) in enumerate(moves)]
    for copy in copies:
        copy.start()
    for t in range(tiles):
        seen[t] = 0
        for r in range(CAP):
            table[t * CAP + r] = -1
    held[...] = jnp.zeros(held.shape, F32)
    for copy in copies[:3]:
        copy.wait()
    places = []
    for b in range(blocks):
        live = count[b]
        for k in range(slots):
            t = dest_tile[k, b]
            r = jnp.minimum(seen[t], CAP - 1)
            seen[t] = r + 1
            table[t * CAP + r] = jnp.where(k < live, dest_block[k, b], -1)
            places.append(pl.multiple_of(t * values + r * fields, 8))
    for copy in copies[3:9]:
        copy.wait()
    state = [own[q * rows : (q + 1) * rows] for q in range(4)]
    sea = sea_int[...].astype(F32)
    own[4 * rows : 5 * rows] = sea
    for turn, message in enumerate(early):
        low = lax.rem(lax.axis_index("comp"), EARLY) == turn
        for q, x in enumerate(state + [sea]):
            message[q * HALO : (q + 1) * HALO, :] = jnp.where(low, x[rows - HALO :], x[:HALO])
    lane16 = lanes_of(16)
    lane8 = lanes_of(8)
    row8 = lax.broadcasted_iota(jnp.int32, (8, LANES), 0)

    def edges(first):
        packed = jnp.zeros((16, LANES), F32)
        for half in range(2):
            for q in range(4):
                to = 64 * half + 16 * q
                moved = pltpu.roll(state[q][16 * half : 16 * half + 16], (to - first) % LANES, 1)
                packed = jnp.where((lane16 >= to) & (lane16 < to + 16), moved, packed)
        small = jnp.zeros((8, LANES), F32)
        for g in range(4):
            moved = pltpu.roll(sea[8 * g : 8 * g + 8], (16 * g - first) % LANES, 1)
            small = jnp.where((lane8 >= 16 * g) & (lane8 < 16 * g + 16), moved, small)
        return jnp.concatenate([packed, small], axis=0)

    me = lax.axis_index("tile")
    core, chip = me % 2, me // 2
    to_right, to_left = edges(LANES - HALO), edges(0)
    tail = 2 * chips * share
    send[tail : tail + 24, :] = jnp.where(core == 0, to_left, to_right)
    send[tail + 24 : tail + 48, :] = jnp.where(core == 0, to_right, to_left)

    for b in range(blocks):
        if b % (blocks // 2) == 0:
            for copy in copies[9 + b : 9 + b + blocks // 2]:
                copy.wait()
        high, low = halves(flux[:, b * LANES : (b + 1) * LANES])
        left = jnp.concatenate(
            [
                jnp.concatenate([high, low], axis=0),
                jnp.concatenate([high, jnp.zeros_like(low)], axis=0),
            ],
            axis=1,
        )
        for first in range(0, slots, 4):
            group = range(first, min(first + 4, slots))
            w_high, w_low = halves(jnp.concatenate([stage[b, k] for k in group], axis=1))
            both = jnp.dot(
                left, jnp.concatenate([w_high, w_low], axis=0), preferred_element_type=F32
            )
            both = both[:fields] + both[fields:]
            for i, k in enumerate(group):
                held[pl.ds(places[b * slots + k], fields), :] = both[:, i * LANES : (i + 1) * LANES]

    for t in range(tiles):
        lefts, rights = max(t - 1, 0), min(t + 1, tiles - 1)
        sender, place = route(lax.bitwise_xor(chip, t // 2), t % 2, chips)
        mine = core == sender
        offset = place * share
        shift = jnp.where(mine, 0, CAP)
        first_lane = jnp.where(mine, 0, 64)
        out = jnp.zeros((8, LANES), F32)
        for f in range(WET):
            to = first_lane + 16 * f
            part_l = held[pl.ds(lefts * values + f, CAP, stride=fields), :]
            part_r = held[pl.ds(rights * values + f, CAP, stride=fields), :]
            part_l = pltpu.roll(part_l, to + HALO, 1)
            part_r = pltpu.roll(part_r, to, 1)
            part = jnp.concatenate([part_l, part_r], axis=0)
            out = jnp.where((lane8 >= to) & (lane8 < to + 16), part, out)
        side = jnp.full((8, LANES), -1, jnp.int32)
        main = jnp.zeros((8, LANES), jnp.int32)
        for r in range(CAP):
            if t > 0:
                side = jnp.where(row8 == r, table[lefts * CAP + r], side)
            if t < tiles - 1:
                named = table[rights * CAP + r]
                side = jnp.where(row8 == CAP + r, jnp.where(named < 0, -1, named + 32), side)
            main = jnp.where(row8 == r + shift, table[t * CAP + r], main)
        out = jnp.where(lane8 == first_lane + 48, side.astype(F32), out)
        out = jnp.where(lane8 == 113, main.astype(F32), out)
        at_names = jnp.where(mine, offset, chips * share + offset + values)
        at_values = jnp.where(mine, offset + 8, chips * share + offset)
        send[pl.ds(pl.multiple_of(at_names, 8), 8), :] = out
        send[pl.ds(pl.multiple_of(at_values, 8), values), :] = held[t * values : (t + 1) * values, :]


def beside(k):
    return k & (k + 1) == 0


def pairs_of(chips):
    return range(1, chips - 1, 2)


def spread(hot, values):
    high, low = halves(values)
    return jnp.dot(hot, high, preferred_element_type=F32) + jnp.dot(hot, low, preferred_element_type=F32)


def one_hot(ids):
    lane = lanes_of(ids.shape[0]).astype(F32)
    return jnp.where(lane == ids, 1.0, 0.0).T.astype(BF16)


def field_values(boxes, f, fields):
    return jnp.concatenate([box[pl.ds(8 + f, 2 * CAP, stride=fields), :] for box in boxes], axis=0)


def names_of(boxes):
    return jnp.concatenate([box[0:8, :] for box in boxes], axis=0)


def hot_slots(names, rows):
    return one_hot(names[:, 113:114])[:rows]


def forcing_kernel(*refs):
    boxes, state, forcing = refs[:-2], refs[-2], refs[-1]
    fields, rows = forcing.shape[:2]
    hot = hot_slots(names_of(boxes), rows)
    sea = state[4 * rows : 5 * rows]
    for f in range(fields):
        forcing[f] = spread(hot, field_values(boxes, f, fields)) * sea


def place_kernel(*refs, fields):
    boxes = refs[: -4 - ROUNDS]
    state, wet, left, right, *messages = refs[-4 - ROUNDS :]
    rows = left.shape[0]
    chips = len(boxes)
    values = CAP * fields
    names = names_of(boxes)
    hot_mine, hot_other = (one_hot(names[:, at : at + 1])[: 2 * rows] for at in (48, 112))
    hot_main = hot_slots(names, rows)
    sea = state[4 * rows : 5 * rows]
    for f in range(WET):
        wet[f * rows : (f + 1) * rows] = spread(hot_main, field_values(boxes, f, fields)) * sea
    sides = pltpu.roll(spread(hot_mine, names), 80, 1) + pltpu.roll(spread(hot_other, names), 16, 1)
    lane = lanes_of(rows)
    me = lax.axis_index("tile")
    core, chip = me % 2, me // 2
    beyond = jnp.where(core == 0, chip - 1, chip + 1)
    at = 8 + 2 * values
    facing, away = boxes[0][at : at + 24, :], boxes[-1][at : at + 24, :]
    for k in filter(beside, pairs_of(chips)):
        direct, passed = boxes[k][2 * at : 2 * at + 24, :], boxes[k + 1][at : at + 24, :]
        away = jnp.where(beyond == lax.bitwise_xor(chip, k), jnp.where(core == 1, direct, passed), away)
    for which, out in ((0, left), (1, right)):
        edge = jnp.where(core == which, away, facing)
        packed, small = edge[:16], edge[16:]
        whole = jnp.concatenate([packed, pltpu.roll(packed, 64, 1)], axis=0)
        sea_part = jnp.concatenate(
            [pltpu.roll(small, (64 - 16 * g) % LANES, 1) for g in range(4)], axis=0
        )
        driven = sides[which * rows : (which + 1) * rows]
        full = jnp.where(lane < 64, whole, jnp.where(lane < 80, sea_part, driven))
        exists = (me > 0) if which == 0 else (me < 2 * chips - 1)
        full = jnp.where(exists, full, 0.0)
        out[...] = full
    section = lax.axis_index("comp")
    for turn, message in enumerate(messages):
        start = pl.multiple_of(jnp.where(lax.rem(section, ROUNDS) == turn, rows - HALO, 0), 8)
        parts = [(wet, f) for f in range(WET)] + [(left, 0), (right, 0)]
        for i, (ref, q) in enumerate(parts):
            message[i * HALO : (i + 1) * HALO, :] = ref[pl.ds(q * rows + start, HALO), :]


def cycle_kernel(
    state, wet, left, right, *refs, comps
):
    height_out, flow_x, flow_y = refs[EARLY + ROUNDS :]
    rows = height_out.shape[0]
    section = lax.axis_index("comp")

    def halves_of(messages):
        turns = len(messages)
        below, above = messages[0][...], messages[0][...]
        for turn in range(1, turns):
            below = jnp.where(lax.rem(section, turns) == turn, messages[turn][...], below)
            above = jnp.where(lax.rem(section + turns - 1, turns) == turn, messages[turn][...], above)
        return above, below

    parts = zip(halves_of(refs[:EARLY]), halves_of(refs[EARLY : EARLY + ROUNDS]))
    above, below = (jnp.concatenate(part, axis=0) for part in parts)
    total = rows + 2 * HALO
    count = 5 + WET
    own = [state[q * rows : (q + 1) * rows] for q in range(5)]
    own += [wet[f * rows : (f + 1) * rows] for f in range(WET)]
    at = count * 16
    side_l = jnp.concatenate([above[at : at + 16], left[...], below[at : at + 16]], axis=0)
    side_r = jnp.concatenate([above[at + 16 : at + 32], right[...], below[at + 16 : at + 32]], axis=0)
    lane = lanes_of(total)
    wide = []
    for q in range(count):
        center = jnp.concatenate(
            [above[16 * q : 16 * q + 16], own[q], below[16 * q : 16 * q + 16]], axis=0
        )
        from_l = pltpu.roll(side_l, (LANES - 16 * q) % LANES, 1)
        from_r = pltpu.roll(side_r, (LANES - HALO - 16 * q) % LANES, 1)
        west = jnp.where(lane < HALO, from_l, pltpu.roll(center, HALO, 1))
        east = jnp.where(lane < LANES - HALO, pltpu.roll(center, LANES - HALO, 1), from_r)
        wide.append(jnp.concatenate([west, east], axis=1))
    eta, u, v, deep, sea, push_x, push_y, rain = wide
    shape = (total, 2 * LANES)
    row = lax.axis_index("comp") * rows - HALO + lax.broadcasted_iota(jnp.int32, shape, 0)
    inside = (row >= 0) & (row < rows * comps)
    deep, sea = jnp.where(inside, deep, 0.0), jnp.where(inside, sea, 0.0)
    frac = row.astype(F32) / float(rows * comps)
    turn = (0.02 + 0.06 * frac) * sea
    inverse = jnp.where(deep > 0.0, 1.0 / jnp.where(deep > 0.0, deep, 1.0), 0.0)
    wind_x = sea * (0.05 * push_x * inverse)
    wind_y = sea * (0.05 * push_y * inverse)
    fresh = sea * (0.1 * rain)
    slope = 0.2 * sea
    deep = 0.2 * deep

    def cols(x):
        spans = (x[:, :LANES], x[:, LANES:])
        return jnp.concatenate([pltpu.roll(y, LANES - 1, 1) - pltpu.roll(y, 1, 1) for y in spans], axis=1)

    def lines(x):
        return pltpu.roll(x, x.shape[0] - 1, 0) - pltpu.roll(x, 1, 0)

    through_x, through_y = deep * u, deep * v
    eta, u, v = sea * eta, sea * u, sea * v
    top = HALO
    for cycle in range(NSUB):
        eta = eta + fresh - sea * (cols(through_x) + lines(through_y))
        slope_x, slope_y = cols(eta), lines(eta)
        if cycle == NSUB // 2 - 1:
            top = HALO // 2
            fields = (eta, u, v, sea, slope, turn, fresh, wind_x, wind_y, deep, slope_x, slope_y)
            fields = [x[HALO - top : total - HALO + top] for x in fields]
            eta, u, v, sea, slope, turn, fresh, wind_x, wind_y, deep, slope_x, slope_y = fields
        next_u = 0.98 * u - slope * slope_x + turn * v + wind_x
        next_v = 0.98 * v - slope * slope_y - turn * u + wind_y
        u, v = next_u, next_v
        through_x, through_y = deep * u, deep * v
    half = lanes_of(rows) < LANES // 2
    for out, field in ((height_out, eta), (flow_x, u), (flow_y, v)):
        west, east = field[top : top + rows, :LANES], field[top : top + rows, LANES:]
        out[...] = jnp.where(half, pltpu.roll(west, LANES - HALO, 1), pltpu.roll(east, HALO, 1))


def swaps(turn, rounds, comps, tiles):
    pairs = []
    for s in range(comps):
        other = s + 1 if s % rounds == turn else s - 1 if (s - 1) % rounds == turn else -1
        for t in range(tiles):
            there = other * tiles + t if 0 <= other < comps else s * tiles + (t ^ 1)
            pairs.append((s * tiles + t, there))
    return pairs


def local(tiles, comps, flux, weight, dest_tile, dest_block, count, height, vel_x, vel_y, depth, mask):
    fields = flux.shape[0]
    blocks, slots = dest_tile.shape
    rows, cols = height.shape
    state = (height, vel_x, vel_y, depth, mask)
    plane = jax.ShapeDtypeStruct((rows, cols), F32)
    params = pltpu.CompilerParams(vmem_limit_bytes=16 * 1024 * 1024)

    def near(*shape):
        return pltpu.VMEM(shape, F32)

    def far(x):
        return pltpu.with_memory_space_constraint(x, pltpu.HBM)

    values = CAP * fields
    share = values + 8
    chips = tiles // 2
    send, own, *early = pl.pallas_call(
        functools.partial(remap_kernel, tiles=tiles),
        out_shape=[near(2 * chips * share + 48, LANES), near(5 * rows, cols)] + [near(5 * HALO, LANES)] * EARLY,
        in_specs=[HBM] * 10,
        out_specs=[VMEM] * (2 + EARLY),
        scratch_shapes=[
            pltpu.VMEM(flux.shape, F32),
            pltpu.VMEM(weight.shape, F32),
            pltpu.VMEM((tiles * values, LANES), F32),
            pltpu.SMEM((slots, blocks), jnp.int32),
            pltpu.SMEM((slots, blocks), jnp.int32),
            pltpu.SMEM((blocks,), jnp.int32),
            pltpu.VMEM((rows, cols), jnp.int32),
            pltpu.SMEM((tiles * CAP,), jnp.int32),
            pltpu.SMEM((tiles,), jnp.int32),
            pltpu.SemaphoreType.DMA((9 + blocks,)),
        ],
        compiler_params=params,
        name="remap",
    )(*map(far, (flux, weight, dest_tile.T, dest_block.T, count, *state)))
    mine, other = send[: chips * share], send[chips * share :]
    other = lax.ppermute(other, "tile", [(t, t ^ 1) for t in range(tiles)])
    away, facing = other[chips * share : chips * share + 24], other[chips * share + 24 :]

    def joined(place):
        left, right = (x[place * share : (place + 1) * share] for x in (mine, other))
        return [left[:8] + right[values:], left[8:], right[:values]]

    tile = lax.axis_index("tile")
    outward = send[2 * chips * share : 2 * chips * share + 24]
    boxes = [jnp.concatenate(joined(0) + [facing])]
    for k in pairs_of(chips):
        parts = joined(k) + joined(k + 1)
        if beside(k):
            up = lax.bitwise_xor(tile // 2, k) > tile // 2
            parts.append(jnp.where(up, away, outward))
        swap = [(t, t ^ (2 * (k + t % 2)) ^ 1) for t in range(tiles)]
        box = lax.ppermute(jnp.concatenate(parts), "tile", swap)
        boxes += [box, lax.ppermute(box[8 + 2 * values :], "tile", [(t, t ^ 1) for t in range(tiles)])]
    swap = [(t, t ^ (2 * (chips - 1)) ^ 1) for t in range(tiles)]
    boxes.append(lax.ppermute(jnp.concatenate(joined(chips - 1) + [outward]), "tile", swap))
    message = near((WET + 2) * HALO, LANES)
    early, boxes[1] = lax.optimization_barrier((early, boxes[1]))
    early = [lax.ppermute(x, ("comp", "tile"), swaps(turn, EARLY, comps, tiles)) for turn, x in enumerate(early)]
    wet, left, right, *messages = pl.pallas_call(
        functools.partial(place_kernel, fields=fields),
        out_shape=[near(WET * rows, cols), near(rows, cols), near(rows, cols)] + [message] * ROUNDS,
        in_specs=[VMEM] * (chips + 1),
        out_specs=[VMEM] * (3 + ROUNDS),
        compiler_params=params,
        name="place",
    )(*boxes, own)
    received = [
        lax.ppermute(x, ("comp", "tile"), swaps(turn, ROUNDS, comps, tiles))
        for turn, x in enumerate(messages)
    ]
    forcing = pl.pallas_call(
        forcing_kernel,
        out_shape=jax.ShapeDtypeStruct((fields, rows, cols), F32),
        in_specs=[VMEM] * (chips + 1),
        out_specs=VMEM,
        compiler_params=params,
        cost_estimate=pl.CostEstimate(flops=10**8, bytes_accessed=4 * 2**20, transcendentals=0),
        name="forcing",
    )(*boxes, own)
    outs = pl.pallas_call(
        functools.partial(cycle_kernel, comps=comps),
        out_shape=[plane] * 3,
        in_specs=[VMEM] * (4 + EARLY + ROUNDS),
        out_specs=[VMEM] * 3,
        compiler_params=params,
        name="cycles",
    )(own, wet, left, right, *early, *received)
    return (forcing, *outs)


def solution(mesh):
    both = ("comp", "tile")
    grid = P("comp", "tile")
    in_specs = (P(None, both), P(both, None, None, None), P(both, None), P(both, None), P(both)) + (grid,) * 5
    out_specs = (P(None, "comp", "tile"), grid, grid, grid)
    body = functools.partial(local, mesh.shape["tile"], mesh.shape["comp"])
    return jax.shard_map(body, mesh=mesh, in_specs=in_specs, out_specs=out_specs, check_vma=False)
```

```python
import functools

import jax
import jax.numpy as jnp
from jax import lax
from jax.experimental import pallas as pl
from jax.experimental.pallas import tpu as pltpu
from jax.sharding import PartitionSpec as P

NSUB = 8
HALO = 2 * NSUB
CAP = 4
LANES = 128
EARLY = 3
ROUNDS = 2
WET = 3
F32 = jnp.float32
BF16 = jnp.bfloat16
VMEM = pl.BlockSpec(memory_space=pltpu.VMEM)
SMEM = pl.BlockSpec(memory_space=pltpu.SMEM)
HBM = pl.BlockSpec(memory_space=pltpu.HBM)


def halves(x):
    high = x.astype(BF16)
    return high, (x - high.astype(F32)).astype(BF16)


def lanes_of(rows):
    return lax.broadcasted_iota(jnp.int32, (rows, LANES), 1)


def route(k, core, chips):
    alone = (k == 0) | (k == chips - 1)
    sender = jnp.where(k == 0, core, jnp.where(alone, 1 - core, lax.rem(k, 2)))
    place = jnp.where(alone, k, (k - 1) // 2 * 2 + 1 + jnp.where(sender == core, 1, 0))
    return sender, place


def remap_kernel(
    flux_far, weight, tile_far, block_far, count_far, height, vel_x, vel_y, depth, mask,
    send, own, *refs, tiles,
):
    early = refs[:EARLY]
    flux, stage, held, dest_tile, dest_block, count, sea_int, table, seen, sems = refs[EARLY:]
    slots, blocks = dest_tile.shape
    fields, rows = flux.shape[0], height.shape[0]
    values = CAP * fields
    share = values + 8
    chips = tiles // 2
    moves = [(tile_far, dest_tile), (block_far, dest_block), (count_far, count)]
    moves += [(flux_far, flux), (mask, sea_int)]
    moves += [(x, own.at[q * rows : (q + 1) * rows]) for q, x in enumerate((height, vel_x, vel_y, depth))]
    moves += [(weight.at[b], stage.at[b]) for b in range(blocks)]
    copies = [pltpu.make_async_copy(x, y, sems.at[i]) for i, (x, y) in enumerate(moves)]
    for copy in copies:
        copy.start()
    for t in range(tiles):
        seen[t] = 0
        for r in range(CAP):
            table[t * CAP + r] = -1
    held[...] = jnp.zeros(held.shape, F32)
    for copy in copies[:3]:
        copy.wait()
    places = []
    for b in range(blocks):
        live = count[b]
        for k in range(slots):
            t = dest_tile[k, b]
            r = jnp.minimum(seen[t], CAP - 1)
            seen[t] = r + 1
            table[t * CAP + r] = jnp.where(k < live, dest_block[k, b], -1)
            places.append(pl.multiple_of(t * values + r * fields, 8))
    for copy in copies[3:9]:
        copy.wait()
    state = [own[q * rows : (q + 1) * rows] for q in range(4)]
    sea = sea_int[...].astype(F32)
    own[4 * rows : 5 * rows] = sea
    for turn, message in enumerate(early):
        low = lax.rem(lax.axis_index("comp"), EARLY) == turn
        for q, x in enumerate(state + [sea]):
            message[q * HALO : (q + 1) * HALO, :] = jnp.where(low, x[rows - HALO :], x[:HALO])
    lane16 = lanes_of(16)
    lane8 = lanes_of(8)
    row8 = lax.broadcasted_iota(jnp.int32, (8, LANES), 0)

    def edges(first):
        packed = jnp.zeros((16, LANES), F32)
        for half in range(2):
            for q in range(4):
                to = 64 * half + 16 * q
                moved = pltpu.roll(state[q][16 * half : 16 * half + 16], (to - first) % LANES, 1)
                packed = jnp.where((lane16 >= to) & (lane16 < to + 16), moved, packed)
        small = jnp.zeros((8, LANES), F32)
        for g in range(4):
            moved = pltpu.roll(sea[8 * g : 8 * g + 8], (16 * g - first) % LANES, 1)
            small = jnp.where((lane8 >= 16 * g) & (lane8 < 16 * g + 16), moved, small)
        return jnp.concatenate([packed, small], axis=0)

    me = lax.axis_index("tile")
    core, chip = me % 2, me // 2
    to_right, to_left = edges(LANES - HALO), edges(0)
    tail = 2 * chips * share
    send[tail : tail + 24, :] = jnp.where(core == 0, to_left, to_right)
    send[tail + 24 : tail + 48, :] = jnp.where(core == 0, to_right, to_left)

    for b in range(blocks):
        if b % (blocks // 2) == 0:
            for copy in copies[9 + b : 9 + b + blocks // 2]:
                copy.wait()
        high, low = halves(flux[:, b * LANES : (b + 1) * LANES])
        left = jnp.concatenate(
            [
                jnp.concatenate([high, low], axis=0),
                jnp.concatenate([high, jnp.zeros_like(low)], axis=0),
            ],
            axis=1,
        )
        for k in range(slots):
            w_high, w_low = halves(stage[b, k])
            both = jnp.dot(
                left, jnp.concatenate([w_high, w_low], axis=0), preferred_element_type=F32
            )
            held[pl.ds(places[b * slots + k], fields), :] = both[:fields] + both[fields:]

    for t in range(tiles):
        lefts, rights = max(t - 1, 0), min(t + 1, tiles - 1)
        sender, place = route(lax.bitwise_xor(chip, t // 2), t % 2, chips)
        mine = core == sender
        offset = place * share
        shift = jnp.where(mine, 0, CAP)
        first_lane = jnp.where(mine, 0, 64)
        out = jnp.zeros((8, LANES), F32)
        for f in range(WET):
            to = first_lane + 16 * f
            part_l = held[pl.ds(lefts * values + f, CAP, stride=fields), :]
            part_r = held[pl.ds(rights * values + f, CAP, stride=fields), :]
            part_l = pltpu.roll(part_l, to + HALO, 1)
            part_r = pltpu.roll(part_r, to, 1)
            part = jnp.concatenate([part_l, part_r], axis=0)
            out = jnp.where((lane8 >= to) & (lane8 < to + 16), part, out)
        side = jnp.full((8, LANES), -1, jnp.int32)
        main = jnp.zeros((8, LANES), jnp.int32)
        for r in range(CAP):
            if t > 0:
                side = jnp.where(row8 == r, table[lefts * CAP + r], side)
            if t < tiles - 1:
                named = table[rights * CAP + r]
                side = jnp.where(row8 == CAP + r, jnp.where(named < 0, -1, named + 32), side)
            main = jnp.where(row8 == r + shift, table[t * CAP + r], main)
        out = jnp.where(lane8 == first_lane + 48, side.astype(F32), out)
        out = jnp.where(lane8 == 113, main.astype(F32), out)
        at_names = jnp.where(mine, offset, chips * share + offset + values)
        at_values = jnp.where(mine, offset + 8, chips * share + offset)
        send[pl.ds(pl.multiple_of(at_names, 8), 8), :] = out
        send[pl.ds(pl.multiple_of(at_values, 8), values), :] = held[t * values : (t + 1) * values, :]


def beside(k):
    return k & (k + 1) == 0


def pairs_of(chips):
    return range(1, chips - 1, 2)


def spread(hot, values):
    high, low = halves(values)
    return jnp.dot(hot, high, preferred_element_type=F32) + jnp.dot(hot, low, preferred_element_type=F32)


def one_hot(ids):
    lane = lanes_of(ids.shape[0]).astype(F32)
    return jnp.where(lane == ids, 1.0, 0.0).T.astype(BF16)


def field_values(boxes, f, fields):
    return jnp.concatenate([box[pl.ds(8 + f, 2 * CAP, stride=fields), :] for box in boxes], axis=0)


def names_of(boxes):
    return jnp.concatenate([box[0:8, :] for box in boxes], axis=0)


def hot_slots(names, rows):
    return one_hot(names[:, 113:114])[:rows]


def forcing_kernel(*refs):
    boxes, state, forcing = refs[:-2], refs[-2], refs[-1]
    fields, rows = forcing.shape[:2]
    hot = hot_slots(names_of(boxes), rows)
    sea = state[4 * rows : 5 * rows]
    for f in range(fields):
        forcing[f] = spread(hot, field_values(boxes, f, fields)) * sea


def place_kernel(*refs, fields):
    boxes = refs[: -4 - ROUNDS]
    state, wet, left, right, *messages = refs[-4 - ROUNDS :]
    rows = left.shape[0]
    chips = len(boxes)
    values = CAP * fields
    names = names_of(boxes)
    hot_mine, hot_other = (one_hot(names[:, at : at + 1])[: 2 * rows] for at in (48, 112))
    hot_main = hot_slots(names, rows)
    sea = state[4 * rows : 5 * rows]
    for f in range(WET):
        wet[f * rows : (f + 1) * rows] = spread(hot_main, field_values(boxes, f, fields)) * sea
    sides = pltpu.roll(spread(hot_mine, names), 80, 1) + pltpu.roll(spread(hot_other, names), 16, 1)
    lane = lanes_of(rows)
    me = lax.axis_index("tile")
    core, chip = me % 2, me // 2
    beyond = jnp.where(core == 0, chip - 1, chip + 1)
    at = 8 + 2 * values
    facing, away = boxes[0][at : at + 24, :], boxes[-1][at : at + 24, :]
    for k in filter(beside, pairs_of(chips)):
        direct, passed = boxes[k][2 * at : 2 * at + 24, :], boxes[k + 1][at : at + 24, :]
        away = jnp.where(beyond == lax.bitwise_xor(chip, k), jnp.where(core == 0, direct, passed), away)
    for which, out in ((0, left), (1, right)):
        edge = jnp.where(core == which, away, facing)
        packed, small = edge[:16], edge[16:]
        whole = jnp.concatenate([packed, pltpu.roll(packed, 64, 1)], axis=0)
        sea_part = jnp.concatenate(
            [pltpu.roll(small, (64 - 16 * g) % LANES, 1) for g in range(4)], axis=0
        )
        driven = sides[which * rows : (which + 1) * rows]
        full = jnp.where(lane < 64, whole, jnp.where(lane < 80, sea_part, driven))
        exists = (me > 0) if which == 0 else (me < 2 * chips - 1)
        full = jnp.where(exists, full, 0.0)
        out[...] = full
    section = lax.axis_index("comp")
    for turn, message in enumerate(messages):
        start = pl.multiple_of(jnp.where(lax.rem(section, ROUNDS) == turn, rows - HALO, 0), 8)
        parts = [(wet, f) for f in range(WET)] + [(left, 0), (right, 0)]
        for i, (ref, q) in enumerate(parts):
            message[i * HALO : (i + 1) * HALO, :] = ref[pl.ds(q * rows + start, HALO), :]


def cycle_kernel(
    state, wet, left, right, *refs, comps
):
    height_out, flow_x, flow_y = refs[EARLY + ROUNDS :]
    rows = height_out.shape[0]
    section = lax.axis_index("comp")

    def halves_of(messages):
        turns = len(messages)
        below, above = messages[0][...], messages[0][...]
        for turn in range(1, turns):
            below = jnp.where(lax.rem(section, turns) == turn, messages[turn][...], below)
            above = jnp.where(lax.rem(section + turns - 1, turns) == turn, messages[turn][...], above)
        return above, below

    parts = zip(halves_of(refs[:EARLY]), halves_of(refs[EARLY : EARLY + ROUNDS]))
    above, below = (jnp.concatenate(part, axis=0) for part in parts)
    total = rows + 2 * HALO
    count = 5 + WET
    own = [state[q * rows : (q + 1) * rows] for q in range(5)]
    own += [wet[f * rows : (f + 1) * rows] for f in range(WET)]
    at = count * 16
    side_l = jnp.concatenate([above[at : at + 16], left[...], below[at : at + 16]], axis=0)
    side_r = jnp.concatenate([above[at + 16 : at + 32], right[...], below[at + 16 : at + 32]], axis=0)
    lane = lanes_of(total)
    wide = []
    for q in range(count):
        center = jnp.concatenate(
            [above[16 * q : 16 * q + 16], own[q], below[16 * q : 16 * q + 16]], axis=0
        )
        from_l = pltpu.roll(side_l, (LANES - 16 * q) % LANES, 1)
        from_r = pltpu.roll(side_r, (LANES - HALO - 16 * q) % LANES, 1)
        west = jnp.where(lane < HALO, from_l, pltpu.roll(center, HALO, 1))
        east = jnp.where(lane < LANES - HALO, pltpu.roll(center, LANES - HALO, 1), from_r)
        wide.append(jnp.concatenate([west, east], axis=1))
    eta, u, v, deep, sea, push_x, push_y, rain = wide
    shape = (total, 2 * LANES)
    row = lax.axis_index("comp") * rows - HALO + lax.broadcasted_iota(jnp.int32, shape, 0)
    inside = (row >= 0) & (row < rows * comps)
    deep, sea = jnp.where(inside, deep, 0.0), jnp.where(inside, sea, 0.0)
    frac = row.astype(F32) / float(rows * comps)
    turn = (0.02 + 0.06 * frac) * sea
    inverse = jnp.where(deep > 0.0, 1.0 / jnp.where(deep > 0.0, deep, 1.0), 0.0)
    wind_x = sea * (0.05 * push_x * inverse)
    wind_y = sea * (0.05 * push_y * inverse)
    fresh = sea * (0.1 * rain)
    slope = 0.2 * sea
    deep = 0.2 * deep

    def cols(x):
        spans = (x[:, :LANES], x[:, LANES:])
        return jnp.concatenate([pltpu.roll(y, LANES - 1, 1) - pltpu.roll(y, 1, 1) for y in spans], axis=1)

    def lines(x):
        return pltpu.roll(x, x.shape[0] - 1, 0) - pltpu.roll(x, 1, 0)

    through_x, through_y = deep * u, deep * v
    eta, u, v = sea * eta, sea * u, sea * v
    top = HALO
    for cycle in range(NSUB):
        eta = eta + fresh - sea * (cols(through_x) + lines(through_y))
        slope_x, slope_y = cols(eta), lines(eta)
        if cycle == NSUB // 2 - 1:
            top = HALO // 2
            fields = (eta, u, v, sea, slope, turn, fresh, wind_x, wind_y, deep, slope_x, slope_y)
            fields = [x[HALO - top : total - HALO + top] for x in fields]
            eta, u, v, sea, slope, turn, fresh, wind_x, wind_y, deep, slope_x, slope_y = fields
        next_u = 0.98 * u - slope * slope_x + turn * v + wind_x
        next_v = 0.98 * v - slope * slope_y - turn * u + wind_y
        u, v = next_u, next_v
        through_x, through_y = deep * u, deep * v
    half = lanes_of(rows) < LANES // 2
    for out, field in ((height_out, eta), (flow_x, u), (flow_y, v)):
        west, east = field[top : top + rows, :LANES], field[top : top + rows, LANES:]
        out[...] = jnp.where(half, pltpu.roll(west, LANES - HALO, 1), pltpu.roll(east, HALO, 1))


def swaps(turn, rounds, comps, tiles):
    pairs = []
    for s in range(comps):
        other = s + 1 if s % rounds == turn else s - 1 if (s - 1) % rounds == turn else -1
        for t in range(tiles):
            there = other * tiles + t if 0 <= other < comps else s * tiles + (t ^ 1)
            pairs.append((s * tiles + t, there))
    return pairs


def local(tiles, comps, flux, weight, dest_tile, dest_block, count, height, vel_x, vel_y, depth, mask):
    fields = flux.shape[0]
    blocks, slots = dest_tile.shape
    rows, cols = height.shape
    state = (height, vel_x, vel_y, depth, mask)
    plane = jax.ShapeDtypeStruct((rows, cols), F32)
    params = pltpu.CompilerParams(vmem_limit_bytes=16 * 1024 * 1024)

    def near(*shape):
        return pltpu.VMEM(shape, F32)

    def far(x):
        return pltpu.with_memory_space_constraint(x, pltpu.HBM)

    values = CAP * fields
    share = values + 8
    chips = tiles // 2
    send, own, *early = pl.pallas_call(
        functools.partial(remap_kernel, tiles=tiles),
        out_shape=[near(2 * chips * share + 48, LANES), near(5 * rows, cols)] + [near(5 * HALO, LANES)] * EARLY,
        in_specs=[HBM] * 10,
        out_specs=[VMEM] * (2 + EARLY),
        scratch_shapes=[
            pltpu.VMEM(flux.shape, F32),
            pltpu.VMEM(weight.shape, F32),
            pltpu.VMEM((tiles * values, LANES), F32),
            pltpu.SMEM((slots, blocks), jnp.int32),
            pltpu.SMEM((slots, blocks), jnp.int32),
            pltpu.SMEM((blocks,), jnp.int32),
            pltpu.VMEM((rows, cols), jnp.int32),
            pltpu.SMEM((tiles * CAP,), jnp.int32),
            pltpu.SMEM((tiles,), jnp.int32),
            pltpu.SemaphoreType.DMA((9 + blocks,)),
        ],
        compiler_params=params,
        name="remap",
    )(*map(far, (flux, weight, dest_tile.T, dest_block.T, count, *state)))
    mine, other = send[: chips * share], send[chips * share :]
    other = lax.ppermute(other, "tile", [(t, t ^ 1) for t in range(tiles)])
    away, facing = other[chips * share : chips * share + 24], other[chips * share + 24 :]

    def joined(place):
        left, right = (x[place * share : (place + 1) * share] for x in (mine, other))
        return [left[:8] + right[values:], left[8:], right[:values]]

    tile = lax.axis_index("tile")
    outward = send[2 * chips * share : 2 * chips * share + 24]
    boxes = [jnp.concatenate(joined(0) + [facing])]
    for k in pairs_of(chips):
        parts = joined(k) + joined(k + 1)
        if beside(k):
            up = lax.bitwise_xor(tile // 2, k) > tile // 2
            parts.append(jnp.where(up, outward, away))
        swap = [(t, t ^ (2 * (k + 1 - t % 2)) ^ 1) for t in range(tiles)]
        box = lax.ppermute(jnp.concatenate(parts), "tile", swap)
        boxes += [box, lax.ppermute(box[8 + 2 * values :], "tile", [(t, t ^ 1) for t in range(tiles)])]
    swap = [(t, t ^ (2 * (chips - 1)) ^ 1) for t in range(tiles)]
    boxes.append(lax.ppermute(jnp.concatenate(joined(chips - 1) + [outward]), "tile", swap))
    message = near((WET + 2) * HALO, LANES)
    early, boxes[1] = lax.optimization_barrier((early, boxes[1]))
    early = [lax.ppermute(x, ("comp", "tile"), swaps(turn, EARLY, comps, tiles)) for turn, x in enumerate(early)]
    wet, left, right, *messages = pl.pallas_call(
        functools.partial(place_kernel, fields=fields),
        out_shape=[near(WET * rows, cols), near(rows, cols), near(rows, cols)] + [message] * ROUNDS,
        in_specs=[VMEM] * (chips + 1),
        out_specs=[VMEM] * (3 + ROUNDS),
        compiler_params=params,
        name="place",
    )(*boxes, own)
    received = [
        lax.ppermute(x, ("comp", "tile"), swaps(turn, ROUNDS, comps, tiles))
        for turn, x in enumerate(messages)
    ]
    forcing = pl.pallas_call(
        forcing_kernel,
        out_shape=jax.ShapeDtypeStruct((fields, rows, cols), F32),
        in_specs=[VMEM] * (chips + 1),
        out_specs=VMEM,
        compiler_params=params,
        cost_estimate=pl.CostEstimate(flops=10**8, bytes_accessed=4 * 2**20, transcendentals=0),
        name="forcing",
    )(*boxes, own)
    outs = pl.pallas_call(
        functools.partial(cycle_kernel, comps=comps),
        out_shape=[plane] * 3,
        in_specs=[VMEM] * (4 + EARLY + ROUNDS),
        out_specs=[VMEM] * 3,
        compiler_params=params,
        name="cycles",
    )(own, wet, left, right, *early, *received)
    return (forcing, *outs)


def solution(mesh):
    both = ("comp", "tile")
    grid = P("comp", "tile")
    in_specs = (P(None, both), P(both, None, None, None), P(both, None), P(both, None), P(both)) + (grid,) * 5
    out_specs = (P(None, "comp", "tile"), grid, grid, grid)
    body = functools.partial(local, mesh.shape["tile"], mesh.shape["comp"])
    return jax.shard_map(body, mesh=mesh, in_specs=in_specs, out_specs=out_specs, check_vma=False)
```

```python
import functools

import jax
import jax.numpy as jnp
from jax import lax
from jax.experimental import pallas as pl
from jax.experimental.pallas import tpu as pltpu
from jax.sharding import PartitionSpec as P

NSUB = 8
HALO = 2 * NSUB
CAP = 4
LANES = 128
EARLY = 3
ROUNDS = 2
WET = 3
F32 = jnp.float32
BF16 = jnp.bfloat16
VMEM = pl.BlockSpec(memory_space=pltpu.VMEM)
SMEM = pl.BlockSpec(memory_space=pltpu.SMEM)
HBM = pl.BlockSpec(memory_space=pltpu.HBM)


def halves(x):
    high = x.astype(BF16)
    return high, (x - high.astype(F32)).astype(BF16)


def lanes_of(rows):
    return lax.broadcasted_iota(jnp.int32, (rows, LANES), 1)


def route(k, core, chips):
    alone = (k == 0) | (k == chips - 1)
    sender = jnp.where(k == 0, core, jnp.where(alone, 1 - core, lax.rem(k + 1, 2)))
    place = jnp.where(alone, k, (k - 1) // 2 * 2 + 1 + jnp.where(sender == core, 1, 0))
    return sender, place


def remap_kernel(
    flux_far, weight, tile_far, block_far, count_far, height, vel_x, vel_y, depth, mask,
    send, own, *refs, tiles,
):
    early = refs[:EARLY]
    flux, stage, held, dest_tile, dest_block, count, sea_int, table, seen, sems = refs[EARLY:]
    slots, blocks = dest_tile.shape
    fields, rows = flux.shape[0], height.shape[0]
    values = CAP * fields
    share = values + 8
    chips = tiles // 2
    moves = [(tile_far, dest_tile), (block_far, dest_block), (count_far, count)]
    moves += [(flux_far, flux), (mask, sea_int)]
    moves += [(x, own.at[q * rows : (q + 1) * rows]) for q, x in enumerate((height, vel_x, vel_y, depth))]
    moves += [(weight.at[b], stage.at[b]) for b in range(blocks)]
    copies = [pltpu.make_async_copy(x, y, sems.at[i]) for i, (x, y) in enumerate(moves)]
    for copy in copies:
        copy.start()
    for t in range(tiles):
        seen[t] = 0
        for r in range(CAP):
            table[t * CAP + r] = -1
    held[...] = jnp.zeros(held.shape, F32)
    for copy in copies[:3]:
        copy.wait()
    places = []
    for b in range(blocks):
        live = count[b]
        for k in range(slots):
            t = dest_tile[k, b]
            r = jnp.minimum(seen[t], CAP - 1)
            seen[t] = r + 1
            table[t * CAP + r] = jnp.where(k < live, dest_block[k, b], -1)
            places.append(pl.multiple_of(t * values + r * fields, 8))
    for copy in copies[3:9]:
        copy.wait()
    state = [own[q * rows : (q + 1) * rows] for q in range(4)]
    sea = sea_int[...].astype(F32)
    own[4 * rows : 5 * rows] = sea
    for turn, message in enumerate(early):
        low = lax.rem(lax.axis_index("comp"), EARLY) == turn
        for q, x in enumerate(state + [sea]):
            message[q * HALO : (q + 1) * HALO, :] = jnp.where(low, x[rows - HALO :], x[:HALO])
    lane16 = lanes_of(16)
    lane8 = lanes_of(8)
    row8 = lax.broadcasted_iota(jnp.int32, (8, LANES), 0)

    def edges(first):
        packed = jnp.zeros((16, LANES), F32)
        for half in range(2):
            for q in range(4):
                to = 64 * half + 16 * q
                moved = pltpu.roll(state[q][16 * half : 16 * half + 16], (to - first) % LANES, 1)
                packed = jnp.where((lane16 >= to) & (lane16 < to + 16), moved, packed)
        small = jnp.zeros((8, LANES), F32)
        for g in range(4):
            moved = pltpu.roll(sea[8 * g : 8 * g + 8], (16 * g - first) % LANES, 1)
            small = jnp.where((lane8 >= 16 * g) & (lane8 < 16 * g + 16), moved, small)
        return jnp.concatenate([packed, small], axis=0)

    me = lax.axis_index("tile")
    core, chip = me % 2, me // 2
    to_right, to_left = edges(LANES - HALO), edges(0)
    tail = 2 * chips * share
    send[tail : tail + 24, :] = jnp.where(core == 0, to_left, to_right)
    send[tail + 24 : tail + 48, :] = jnp.where(core == 0, to_right, to_left)

    for b in range(blocks):
        if b % (blocks // 2) == 0:
            for copy in copies[9 + b : 9 + b + blocks // 2]:
                copy.wait()
        high, low = halves(flux[:, b * LANES : (b + 1) * LANES])
        left = jnp.concatenate(
            [
                jnp.concatenate([high, low], axis=0),
                jnp.concatenate([high, jnp.zeros_like(low)], axis=0),
            ],
            axis=1,
        )
        for k in range(slots):
            w_high, w_low = halves(stage[b, k])
            both = jnp.dot(
                left, jnp.concatenate([w_high, w_low], axis=0), preferred_element_type=F32
            )
            held[pl.ds(places[b * slots + k], fields), :] = both[:fields] + both[fields:]

    for t in range(tiles):
        lefts, rights = max(t - 1, 0), min(t + 1, tiles - 1)
        sender, place = route(lax.bitwise_xor(chip, t // 2), t % 2, chips)
        mine = core == sender
        offset = place * share
        shift = jnp.where(mine, 0, CAP)
        first_lane = jnp.where(mine, 0, 64)
        out = jnp.zeros((8, LANES), F32)
        for f in range(WET):
            to = first_lane + 16 * f
            part_l = held[pl.ds(lefts * values + f, CAP, stride=fields), :]
            part_r = held[pl.ds(rights * values + f, CAP, stride=fields), :]
            part_l = pltpu.roll(part_l, to + HALO, 1)
            part_r = pltpu.roll(part_r, to, 1)
            part = jnp.concatenate([part_l, part_r], axis=0)
            out = jnp.where((lane8 >= to) & (lane8 < to + 16), part, out)
        side = jnp.full((8, LANES), -1, jnp.int32)
        main = jnp.zeros((8, LANES), jnp.int32)
        for r in range(CAP):
            if t > 0:
                side = jnp.where(row8 == r, table[lefts * CAP + r], side)
            if t < tiles - 1:
                named = table[rights * CAP + r]
                side = jnp.where(row8 == CAP + r, jnp.where(named < 0, -1, named + 32), side)
            main = jnp.where(row8 == r + shift, table[t * CAP + r], main)
        out = jnp.where(lane8 == first_lane + 48, side.astype(F32), out)
        out = jnp.where(lane8 == 113, main.astype(F32), out)
        at_names = jnp.where(mine, offset, chips * share + offset + values)
        at_values = jnp.where(mine, offset + 8, chips * share + offset)
        send[pl.ds(pl.multiple_of(at_names, 8), 8), :] = out
        send[pl.ds(pl.multiple_of(at_values, 8), values), :] = held[t * values : (t + 1) * values, :]


def beside(k):
    return k & (k + 1) == 0


def pairs_of(chips):
    return range(1, chips - 1, 2)


def spread(hot, values):
    high, low = halves(values)
    return jnp.dot(hot, high, preferred_element_type=F32) + jnp.dot(hot, low, preferred_element_type=F32)


def one_hot(ids):
    lane = lanes_of(ids.shape[0]).astype(F32)
    return jnp.where(lane == ids, 1.0, 0.0).T.astype(BF16)


def field_values(boxes, f, fields):
    return jnp.concatenate([box[pl.ds(8 + f, 2 * CAP, stride=fields), :] for box in boxes], axis=0)


def names_of(boxes):
    return jnp.concatenate([box[0:8, :] for box in boxes], axis=0)


def hot_slots(names, rows):
    return one_hot(names[:, 113:114])[:rows]


def forcing_kernel(*refs):
    boxes, state, forcing = refs[:-2], refs[-2], refs[-1]
    fields, rows = forcing.shape[:2]
    hot = hot_slots(names_of(boxes), rows)
    sea = state[4 * rows : 5 * rows]
    for f in range(fields):
        forcing[f] = spread(hot, field_values(boxes, f, fields)) * sea


def place_kernel(*refs, fields):
    boxes = refs[: -4 - ROUNDS]
    state, wet, left, right, *messages = refs[-4 - ROUNDS :]
    rows = left.shape[0]
    chips = len(boxes)
    values = CAP * fields
    names = names_of(boxes)
    hot_mine, hot_other = (one_hot(names[:, at : at + 1])[: 2 * rows] for at in (48, 112))
    hot_main = hot_slots(names, rows)
    sea = state[4 * rows : 5 * rows]
    driven_by = jnp.concatenate([field_values(boxes, f, fields) for f in range(WET)], axis=1)
    grids = spread(hot_main, driven_by)
    for f in range(WET):
        wet[f * rows : (f + 1) * rows] = grids[:, f * LANES : (f + 1) * LANES] * sea
    sides = pltpu.roll(spread(hot_mine, names), 80, 1) + pltpu.roll(spread(hot_other, names), 16, 1)
    lane = lanes_of(rows)
    me = lax.axis_index("tile")
    core, chip = me % 2, me // 2
    beyond = jnp.where(core == 0, chip - 1, chip + 1)
    at = 8 + 2 * values
    facing, away = boxes[0][at : at + 24, :], boxes[-1][at : at + 24, :]
    for k in filter(beside, pairs_of(chips)):
        direct, passed = boxes[k][2 * at : 2 * at + 24, :], boxes[k + 1][at : at + 24, :]
        away = jnp.where(beyond == lax.bitwise_xor(chip, k), jnp.where(core == 1, direct, passed), away)
    for which, out in ((0, left), (1, right)):
        edge = jnp.where(core == which, away, facing)
        packed, small = edge[:16], edge[16:]
        whole = jnp.concatenate([packed, pltpu.roll(packed, 64, 1)], axis=0)
        sea_part = jnp.concatenate(
            [pltpu.roll(small, (64 - 16 * g) % LANES, 1) for g in range(4)], axis=0
        )
        driven = sides[which * rows : (which + 1) * rows]
        full = jnp.where(lane < 64, whole, jnp.where(lane < 80, sea_part, driven))
        exists = (me > 0) if which == 0 else (me < 2 * chips - 1)
        full = jnp.where(exists, full, 0.0)
        out[...] = full
    section = lax.axis_index("comp")
    for turn, message in enumerate(messages):
        start = pl.multiple_of(jnp.where(lax.rem(section, ROUNDS) == turn, rows - HALO, 0), 8)
        parts = [(wet, f) for f in range(WET)] + [(left, 0), (right, 0)]
        for i, (ref, q) in enumerate(parts):
            message[i * HALO : (i + 1) * HALO, :] = ref[pl.ds(q * rows + start, HALO), :]


def cycle_kernel(
    state, wet, left, right, *refs, comps
):
    height_out, flow_x, flow_y = refs[EARLY + ROUNDS :]
    rows = height_out.shape[0]
    section = lax.axis_index("comp")

    def halves_of(messages):
        turns = len(messages)
        below, above = messages[0][...], messages[0][...]
        for turn in range(1, turns):
            below = jnp.where(lax.rem(section, turns) == turn, messages[turn][...], below)
            above = jnp.where(lax.rem(section + turns - 1, turns) == turn, messages[turn][...], above)
        return above, below

    parts = zip(halves_of(refs[:EARLY]), halves_of(refs[EARLY : EARLY + ROUNDS]))
    above, below = (jnp.concatenate(part, axis=0) for part in parts)
    total = rows + 2 * HALO
    count = 5 + WET
    own = [state[q * rows : (q + 1) * rows] for q in range(5)]
    own += [wet[f * rows : (f + 1) * rows] for f in range(WET)]
    at = count * 16
    side_l = jnp.concatenate([above[at : at + 16], left[...], below[at : at + 16]], axis=0)
    side_r = jnp.concatenate([above[at + 16 : at + 32], right[...], below[at + 16 : at + 32]], axis=0)
    lane = lanes_of(total)
    wide = []
    for q in range(count):
        center = jnp.concatenate(
            [above[16 * q : 16 * q + 16], own[q], below[16 * q : 16 * q + 16]], axis=0
        )
        from_l = pltpu.roll(side_l, (LANES - 16 * q) % LANES, 1)
        from_r = pltpu.roll(side_r, (LANES - HALO - 16 * q) % LANES, 1)
        west = jnp.where(lane < HALO, from_l, pltpu.roll(center, HALO, 1))
        east = jnp.where(lane < LANES - HALO, pltpu.roll(center, LANES - HALO, 1), from_r)
        wide.append(jnp.concatenate([west, east], axis=1))
    eta, u, v, deep, sea, push_x, push_y, rain = wide
    shape = (total, 2 * LANES)
    row = lax.axis_index("comp") * rows - HALO + lax.broadcasted_iota(jnp.int32, shape, 0)
    inside = (row >= 0) & (row < rows * comps)
    deep, sea = jnp.where(inside, deep, 0.0), jnp.where(inside, sea, 0.0)
    frac = row.astype(F32) / float(rows * comps)
    turn = (0.02 + 0.06 * frac) * sea
    inverse = jnp.where(deep > 0.0, 1.0 / jnp.where(deep > 0.0, deep, 1.0), 0.0)
    wind_x = sea * (0.05 * push_x * inverse)
    wind_y = sea * (0.05 * push_y * inverse)
    fresh = sea * (0.1 * rain)
    slope = 0.2 * sea
    deep = 0.2 * deep

    def cols(x):
        spans = (x[:, :LANES], x[:, LANES:])
        return jnp.concatenate([pltpu.roll(y, LANES - 1, 1) - pltpu.roll(y, 1, 1) for y in spans], axis=1)

    def lines(x):
        return pltpu.roll(x, x.shape[0] - 1, 0) - pltpu.roll(x, 1, 0)

    through_x, through_y = deep * u, deep * v
    eta, u, v = sea * eta, sea * u, sea * v
    top = HALO
    for cycle in range(NSUB):
        eta = eta + fresh - sea * (cols(through_x) + lines(through_y))
        slope_x, slope_y = cols(eta), lines(eta)
        if cycle == NSUB // 2 - 1:
            top = HALO // 2
            fields = (eta, u, v, sea, slope, turn, fresh, wind_x, wind_y, deep, slope_x, slope_y)
            fields = [x[HALO - top : total - HALO + top] for x in fields]
            eta, u, v, sea, slope, turn, fresh, wind_x, wind_y, deep, slope_x, slope_y = fields
        next_u = 0.98 * u - slope * slope_x + turn * v + wind_x
        next_v = 0.98 * v - slope * slope_y - turn * u + wind_y
        u, v = next_u, next_v
        through_x, through_y = deep * u, deep * v
    half = lanes_of(rows) < LANES // 2
    for out, field in ((height_out, eta), (flow_x, u), (flow_y, v)):
        west, east = field[top : top + rows, :LANES], field[top : top + rows, LANES:]
        out[...] = jnp.where(half, pltpu.roll(west, LANES - HALO, 1), pltpu.roll(east, HALO, 1))


def swaps(turn, rounds, comps, tiles):
    pairs = []
    for s in range(comps):
        other = s + 1 if s % rounds == turn else s - 1 if (s - 1) % rounds == turn else -1
        for t in range(tiles):
            there = other * tiles + t if 0 <= other < comps else s * tiles + (t ^ 1)
            pairs.append((s * tiles + t, there))
    return pairs


def local(tiles, comps, flux, weight, dest_tile, dest_block, count, height, vel_x, vel_y, depth, mask):
    fields = flux.shape[0]
    blocks, slots = dest_tile.shape
    rows, cols = height.shape
    state = (height, vel_x, vel_y, depth, mask)
    plane = jax.ShapeDtypeStruct((rows, cols), F32)
    params = pltpu.CompilerParams(vmem_limit_bytes=16 * 1024 * 1024)

    def near(*shape):
        return pltpu.VMEM(shape, F32)

    def far(x):
        return pltpu.with_memory_space_constraint(x, pltpu.HBM)

    values = CAP * fields
    share = values + 8
    chips = tiles // 2
    send, own, *early = pl.pallas_call(
        functools.partial(remap_kernel, tiles=tiles),
        out_shape=[near(2 * chips * share + 48, LANES), near(5 * rows, cols)] + [near(5 * HALO, LANES)] * EARLY,
        in_specs=[HBM] * 10,
        out_specs=[VMEM] * (2 + EARLY),
        scratch_shapes=[
            pltpu.VMEM(flux.shape, F32),
            pltpu.VMEM(weight.shape, F32),
            pltpu.VMEM((tiles * values, LANES), F32),
            pltpu.SMEM((slots, blocks), jnp.int32),
            pltpu.SMEM((slots, blocks), jnp.int32),
            pltpu.SMEM((blocks,), jnp.int32),
            pltpu.VMEM((rows, cols), jnp.int32),
            pltpu.SMEM((tiles * CAP,), jnp.int32),
            pltpu.SMEM((tiles,), jnp.int32),
            pltpu.SemaphoreType.DMA((9 + blocks,)),
        ],
        compiler_params=params,
        name="remap",
    )(*map(far, (flux, weight, dest_tile.T, dest_block.T, count, *state)))
    mine, other = send[: chips * share], send[chips * share :]
    other = lax.ppermute(other, "tile", [(t, t ^ 1) for t in range(tiles)])
    away, facing = other[chips * share : chips * share + 24], other[chips * share + 24 :]

    def joined(place):
        left, right = (x[place * share : (place + 1) * share] for x in (mine, other))
        return [left[:8] + right[values:], left[8:], right[:values]]

    tile = lax.axis_index("tile")
    outward = send[2 * chips * share : 2 * chips * share + 24]
    boxes = [jnp.concatenate(joined(0) + [facing])]
    for k in pairs_of(chips):
        parts = joined(k) + joined(k + 1)
        if beside(k):
            up = lax.bitwise_xor(tile // 2, k) > tile // 2
            parts.append(jnp.where(up, away, outward))
        swap = [(t, t ^ (2 * (k + t % 2)) ^ 1) for t in range(tiles)]
        box = lax.ppermute(jnp.concatenate(parts), "tile", swap)
        boxes += [box, lax.ppermute(box[8 + 2 * values :], "tile", [(t, t ^ 1) for t in range(tiles)])]
    swap = [(t, t ^ (2 * (chips - 1)) ^ 1) for t in range(tiles)]
    boxes.append(lax.ppermute(jnp.concatenate(joined(chips - 1) + [outward]), "tile", swap))
    message = near((WET + 2) * HALO, LANES)
    early, boxes[1] = lax.optimization_barrier((early, boxes[1]))
    early = [lax.ppermute(x, ("comp", "tile"), swaps(turn, EARLY, comps, tiles)) for turn, x in enumerate(early)]
    wet, left, right, *messages = pl.pallas_call(
        functools.partial(place_kernel, fields=fields),
        out_shape=[near(WET * rows, cols), near(rows, cols), near(rows, cols)] + [message] * ROUNDS,
        in_specs=[VMEM] * (chips + 1),
        out_specs=[VMEM] * (3 + ROUNDS),
        compiler_params=params,
        name="place",
    )(*boxes, own)
    received = [
        lax.ppermute(x, ("comp", "tile"), swaps(turn, ROUNDS, comps, tiles))
        for turn, x in enumerate(messages)
    ]
    forcing = pl.pallas_call(
        forcing_kernel,
        out_shape=jax.ShapeDtypeStruct((fields, rows, cols), F32),
        in_specs=[VMEM] * (chips + 1),
        out_specs=VMEM,
        compiler_params=params,
        cost_estimate=pl.CostEstimate(flops=10**8, bytes_accessed=4 * 2**20, transcendentals=0),
        name="forcing",
    )(*boxes, own)
    outs = pl.pallas_call(
        functools.partial(cycle_kernel, comps=comps),
        out_shape=[plane] * 3,
        in_specs=[VMEM] * (4 + EARLY + ROUNDS),
        out_specs=[VMEM] * 3,
        compiler_params=params,
        name="cycles",
    )(own, wet, left, right, *early, *received)
    return (forcing, *outs)


def solution(mesh):
    both = ("comp", "tile")
    grid = P("comp", "tile")
    in_specs = (P(None, both), P(both, None, None, None), P(both, None), P(both, None), P(both)) + (grid,) * 5
    out_specs = (P(None, "comp", "tile"), grid, grid, grid)
    body = functools.partial(local, mesh.shape["tile"], mesh.shape["comp"])
    return jax.shard_map(body, mesh=mesh, in_specs=in_specs, out_specs=out_specs, check_vma=False)
```
